32 devices in a mesh: dp: 4 (over y, x), seq: 8 (over z, core).
Axes of the slice: x: 2, y: 2, z: 4, core: 2. Of those that a mesh axis runs over, the one named last changes fastest.
Arguments:
- x_prompt: bfloat16 [8, 2048, 1024], P('dp', 'seq'), may hold values from -6 to 6
- x_cont: bfloat16 [8, 1024, 1024], P('dp', 'seq'), may hold values from -6 to 6
- dy_prompt: bfloat16 [8, 2048, 1024], P('dp', 'seq'), may hold values from -6 to 6
- dy_cont: bfloat16 [8, 1024, 1024], P('dp', 'seq'), may hold values from -6 to 6
- prompt_pos: int32 [8, 2048], P('dp'), may hold values from 0 to 2047, each once within a row
- weights: bfloat16 [15730944], replicated
- master: float32 [15730944], P(('dp', 'seq')), may hold values from -0.015625 to 0.015625
- moment1: float32 [15730944], P(('dp', 'seq')), may hold values from -6 to 6
- moment2: float32 [15730944], P(('dp', 'seq')), may hold values from 0.1 to 10
Outputs:
- y_prompt: float32 [8, 2048, 1024], P('dp', 'seq')
- y_cont: float32 [8, 1024, 1024], P('dp', 'seq')
- dx_prompt: float32 [8, 2048, 1024], P('dp', 'seq')
- dx_cont: float32 [8, 1024, 1024], P('dp', 'seq')
- grad: float32 [15730944], P(('dp', 'seq'))
- master_new: float32 [15730944], P(('dp', 'seq'))
- moment1_new: float32 [15730944], P(('dp', 'seq'))
- weights_new: bfloat16 [15730944], P('dp')
The draws below stay inside these ranges and needn't reach their ends.
Inputs may be any that keep to these rules, and one draw needn't show every extreme that they name: `prompt_pos`: each row holds every position 0 to 2047 once.
All inputs are finite; a program needn't handle non-finite values.
Results may differ from the reference program's by a relative error of at most 0.017.
Values may be sent and summed in bfloat16 or wider, within the bound.
No kernel may reach another device: no remote copies, remote signals or barrier semaphores. Data moves between devices by JAX's collectives and lax.ppermute only.
A program may use at most 448 MiB of HBM per device.

```python
import math
import jax
import jax.numpy as jnp
from jax import lax

D = 1024
FF = 3072
HEADS = 16
KV_HEADS = 8
HEAD_DIM = 128
CL = 256
PROMPT = 2048
CONT = 1024
GROUPS = 8
NPARAM = 15730944


def parameter_draw(key):
    q_width = HEADS * HEAD_DIM
    kv_width = KV_HEADS * HEAD_DIM
    out_std = 0.6
    specs = [(D, 0.0), (D * q_width, D ** (-0.5)), (D * kv_width, D ** (-0.5)), (D * kv_width, D ** (-0.5)), (HEAD_DIM, 0.0), (HEAD_DIM, 0.0), (q_width * D, out_std), (D, 0.0), (D * FF, D ** (-0.5)), (D * FF, D ** (-0.5)), (FF * D, FF ** (-0.5))]
    pieces = []
    for number, spec in enumerate(specs):
        sub_key = jax.random.fold_in(key, number)
        if spec[1] == 0.0:
            pieces.append(1.0 + 0.25 * jax.random.uniform(sub_key, (spec[0],), jnp.float32, -1.0, 1.0))
        else:
            pieces.append(spec[1] * jax.random.normal(sub_key, (spec[0],), jnp.float32))
    return jnp.concatenate(pieces)


def draw_weights(key, part):
    return parameter_draw(jax.random.fold_in(key, 11)).astype(jnp.bfloat16)


def block_scale(rng, shape, shards, low, largest):
    loudness, own = 1.0, jax.random.fold_in(rng, 6)
    for position, parts in shards:
        steps = jnp.exp(jax.random.uniform(jax.random.fold_in(own, position), (parts,), jnp.float32, low / len(shards), largest / len(shards)))
        loudness = loudness * jnp.repeat(steps, shape[position] // parts).reshape([-1 if axis == position else 1 for axis in range(len(shape))])
    return loudness


def bell_draw(key, extent, scale, most, cuts=(), kind=jnp.bfloat16):
    entries = jax.random.normal(key, extent, jnp.float32) * scale
    if len(cuts) > 0:
        entries = block_scale(key, extent, cuts, -0.22, 0.18) * entries
    return jnp.clip(entries, min=-most, max=most).astype(kind)


def setup_inputs(seed: int = 0) -> dict:
    arg_keys = jax.random.split(jax.random.key(seed), 10)
    return {
        "x_prompt": bell_draw(arg_keys[0], (GROUPS, PROMPT, D), 1.0, 6.0, ((0, 4), (1, 8))),
        "x_cont": bell_draw(arg_keys[1], (GROUPS, CONT, D), 1.0, 6.0, ((0, 4), (1, 8))),
        "dy_prompt": bell_draw(arg_keys[2], (GROUPS, PROMPT, D), 1.0, 6.0, ((0, 4), (1, 8))),
        "dy_cont": bell_draw(arg_keys[3], (GROUPS, CONT, D), 1.0, 6.0, ((0, 4), (1, 8))),
        "prompt_pos": jax.vmap(lambda own: jax.random.permutation(own, PROMPT))(jax.random.split(arg_keys[4], GROUPS)).reshape((GROUPS, PROMPT)).astype(jnp.int32),
        "weights": draw_weights(jax.random.fold_in(arg_keys[9], 71), 0),
        "master": bell_draw(arg_keys[6], (NPARAM,), 0.001, 0.015625, ((0, 32),), jnp.float32),
        "moment1": bell_draw(arg_keys[7], (NPARAM,), 1.0, 6.0, ((0, 32),), jnp.float32),
        "moment2": jnp.clip(jnp.exp(math.log(10.0) - 4.6051702 * jax.random.uniform(arg_keys[8], (NPARAM,), jnp.float32) ** block_scale(arg_keys[8], (NPARAM,), ((0, 32),), -0.2, 0.2)), 0.1, 10.0),
    }


EPS_NORM = 1e-06
ROPE_BASE = 1000000.0
BETA_ONE = 0.9
BETA_TWO = 0.95
ADAM_EPS = 1e-08
LEARN_RATE = 0.0003
DECAY_RATE = 0.1
CORRECT_ONE = 1.0 - 2.656139888758747e-05
CORRECT_TWO = 1.0 - 0.005920529220333996

@jax.custom_vjp
def low(v):
    return lax.optimization_barrier(v.astype(jnp.bfloat16)).astype(jnp.float32)

@jax.custom_vjp
def low_back(v):
    return v

def low_keep(v):
    return (low(v), None)

def low_pass(kept, grad):
    return (grad,)

def back_keep(v):
    return (v, None)

def back_low(kept, grad):
    return (low(grad),)
low.defvjp(low_keep, low_pass)
low_back.defvjp(back_keep, back_low)

def layout():
    q_width = HEADS * HEAD_DIM
    kv_width = KV_HEADS * HEAD_DIM
    return [(D,), (D, q_width), (D, kv_width), (D, kv_width), (HEAD_DIM,), (HEAD_DIM,), (q_width, D), (D,), (D, FF), (D, FF), (FF, D)]

def unpack(flat_vec):
    pieces = []
    offset = 0
    for shape in layout():
        count = shape[0] if len(shape) == 1 else shape[0] * shape[1]
        pieces.append(lax.slice(flat_vec, (offset,), (offset + count,)).reshape(shape))
        offset += count
    return pieces

def exact_dot(left, right):
    return jnp.dot(left, right, precision=lax.Precision.HIGHEST, preferred_element_type=jnp.float32)

def rms_norm(field, gain_vec):
    return field * lax.rsqrt(lax.optimization_barrier(jnp.mean(field * field, axis=-1, keepdims=True)) + EPS_NORM) * gain_vec

def rotate(field, positions):
    half_dim = field.shape[-1] // 2
    frequency = ROPE_BASE ** (-jnp.arange(half_dim, dtype=jnp.float32) * 2.0 / field.shape[-1])
    angles = positions.astype(jnp.float32)[:, None] * frequency[None, :]
    cosine = jnp.cos(angles)[:, None, :]
    sine_part = jnp.sin(angles)[:, None, :]
    front_half = field[..., :half_dim]
    second = field[..., half_dim:]
    return jnp.concatenate([front_half * cosine - second * sine_part, second * cosine + front_half * sine_part], axis=-1)

def group_layer(pieces, x_rows, positions, segments):
    ln_one, w_query, w_key, w_value, gain_q, gain_k, w_out, ln_two, w_gate, w_up, w_down = pieces
    row_count = x_rows.shape[0]
    group_size = HEADS // KV_HEADS
    normed = low(rms_norm(x_rows, ln_one))
    q_raw = low_back(exact_dot(normed, w_query))
    k_raw = low_back(exact_dot(normed, w_key))
    values = low(low_back(exact_dot(normed, w_value))).reshape(row_count, KV_HEADS, HEAD_DIM)
    queries = low(rotate(rms_norm(q_raw.reshape(row_count, HEADS, HEAD_DIM), gain_q), positions))
    keys_rot = low(rotate(rms_norm(k_raw.reshape(row_count, KV_HEADS, HEAD_DIM), gain_k), positions))
    grouped = queries.reshape(row_count, KV_HEADS, group_size, HEAD_DIM)
    block_rows = 512 if row_count % 512 == 0 else row_count
    blocks = row_count // block_rows
    score_scale = HEAD_DIM ** (-0.5)

    def attend(block_args):
        q_block, q_pos, q_seg = block_args
        scores = low_back(jnp.einsum('rhgd,khd->hgrk', q_block, keys_rot, precision=lax.Precision.HIGHEST) * score_scale)
        allowed = (positions[None, :] <= q_pos[:, None]) & ((segments[None, :] < 0) | (segments[None, :] == q_seg[:, None]))
        scores = jnp.where(allowed[None, None], scores, -1e+30)
        highest = lax.optimization_barrier(jnp.max(scores, axis=-1, keepdims=True))
        exponent = jnp.exp(scores - highest)
        probability = exponent / lax.optimization_barrier(jnp.sum(exponent, axis=-1, keepdims=True))
        return jnp.einsum('hgrk,khd->rhgd', low(probability), values, precision=lax.Precision.HIGHEST)
    attended = lax.map(jax.checkpoint(attend), (grouped.reshape(blocks, block_rows, KV_HEADS, group_size, HEAD_DIM), positions.reshape(blocks, block_rows), segments.reshape(blocks, block_rows)))
    mixed = low(low_back(attended.reshape(row_count, HEADS * HEAD_DIM)))
    attn_out = low_back(exact_dot(mixed, w_out))
    resid = x_rows + attn_out
    normed_two = low(rms_norm(resid, ln_two))
    gate_proj = low_back(exact_dot(normed_two, w_gate))
    up_proj = low_back(exact_dot(normed_two, w_up))
    hidden = low(jax.nn.silu(gate_proj) * up_proj)
    return resid + exact_dot(hidden, w_down)

def reference(x_prompt, x_cont, dy_prompt, dy_cont, prompt_pos, weights, master, moment1, moment2):
    quarter = CL // 4
    row_in = jnp.arange(CONT, dtype=jnp.int32) % CL
    block_id = row_in // quarter
    mapped = jnp.where(block_id == 1, 3, jnp.where(block_id == 2, 1, jnp.where(block_id == 3, 2, 0))).astype(jnp.int32)
    cont_pos = (PROMPT + mapped * quarter + row_in % quarter).astype(jnp.int32)
    segments = jnp.concatenate([jnp.full((PROMPT,), -1, jnp.int32), (jnp.arange(CONT, dtype=jnp.int32) // CL).astype(jnp.int32)])

    def forward(flat_w, prompt_x, cont_x):
        pieces = unpack(flat_w)

        def one_group(carry, item):
            prompt_rows, cont_rows, prompt_positions = item
            x_rows = jnp.concatenate([prompt_rows, cont_rows], axis=0)
            positions = jnp.concatenate([prompt_positions, cont_pos]).astype(jnp.int32)
            output = group_layer(pieces, x_rows, positions, segments)
            return (carry, (output[:PROMPT], output[PROMPT:]))
        carry_out, outputs = lax.scan(jax.checkpoint(one_group), None, (prompt_x, cont_x, prompt_pos))
        return outputs
    flat_w = weights.astype(jnp.float32)
    outputs, pullback = jax.vjp(forward, flat_w, x_prompt.astype(jnp.float32), x_cont.astype(jnp.float32))
    grad, dx_prompt, dx_cont = pullback((dy_prompt.astype(jnp.float32), dy_cont.astype(jnp.float32)))
    moment1_new = BETA_ONE * moment1 + (1.0 - BETA_ONE) * grad
    moment2_new = BETA_TWO * moment2 + (1.0 - BETA_TWO) * grad * grad
    update = moment1_new / CORRECT_ONE / (jnp.sqrt(moment2_new / CORRECT_TWO) + ADAM_EPS)
    master_new = master - LEARN_RATE * (update + DECAY_RATE * master)
    return (outputs[0], outputs[1], dx_prompt, dx_cont, grad, master_new, moment1_new, master_new.astype(jnp.bfloat16))
```

```python
import functools

import jax
import jax.numpy as jnp
from jax import lax
from jax.experimental import pallas as pl
from jax.experimental.pallas import tpu as pltpu
from jax.sharding import PartitionSpec as P

D = 1024
FF = 3072
HEADS = 16
KV_HEADS = 8
HEAD_DIM = 128

EPS_NORM = 1e-06
ROPE_BASE = 1000000.0
BETA_ONE = 0.9
BETA_TWO = 0.95
ADAM_EPS = 1e-08
LEARN_RATE = 0.0003
DECAY_RATE = 0.1
CORRECT_ONE = 1.0 - 2.656139888758747e-05
CORRECT_TWO = 1.0 - 0.005920529220333996

CORES = 2
Q_HEADS_C = HEADS // CORES
KV_HEADS_C = KV_HEADS // CORES
QW = Q_HEADS_C * HEAD_DIM
KW = KV_HEADS_C * HEAD_DIM
FW = FF // CORES
GROUP = HEADS // KV_HEADS
LOG2E = 1.4426950408889634
SCORE_FOLD = HEAD_DIM ** (-0.5) * LOG2E
VMEM_LIMIT = 52 * 1024 * 1024
BF = jnp.bfloat16
F32 = jnp.float32


def dot(left, right):
    return jnp.dot(left, right, preferred_element_type=F32)


def dot_t(left, right):
    return lax.dot_general(left, right, (((1,), (1,)), ((), ())), preferred_element_type=F32)


def t_dot(left, right):
    return lax.dot_general(left, right, (((0,), (0,)), ((), ())), preferred_element_type=F32)


def xor_seq(block, mask):
    count = lax.axis_size("seq")
    return lax.ppermute(block, "seq", [(i, i ^ mask) for i in range(count)])


def params(*semantics):
    return pltpu.CompilerParams(vmem_limit_bytes=VMEM_LIMIT)


def whole(shape):
    return pl.BlockSpec(shape, lambda *ids: (0,) * len(shape))


def head_norm_rot(raw, gain, cos, sin):
    r = lax.rsqrt(jnp.mean(raw * raw, axis=-1, keepdims=True) + EPS_NORM)
    n = raw * r * gain
    return n * cos + pltpu.roll(n, HEAD_DIM // 2, 1) * sin


def head_norm_rot_back(raw, gain, cos, sin, grad):
    dn = grad * cos - pltpu.roll(grad, HEAD_DIM // 2, 1) * sin
    r = lax.rsqrt(jnp.mean(raw * raw, axis=-1, keepdims=True) + EPS_NORM)
    xh = raw * r
    gain_rows = dn * xh
    dg = dn * gain
    return r * (dg - xh * jnp.mean(dg * xh, axis=-1, keepdims=True)), gain_rows


def project_kernel(with_q, *refs):
    if with_q:
        (x, g1, cos, sin, wq, wkv, gq, gk, a_out, q_out, qraw_out, k_out, kraw_out, v_out) = refs
    else:
        (x, g1, cos, sin, wkv, gk, a_out, k_out, kraw_out, v_out) = refs
    xv = x[...].astype(F32)
    a = xv * lax.rsqrt(jnp.mean(xv * xv, axis=-1, keepdims=True) + EPS_NORM) * g1[...]
    a = a.astype(BF)
    a_out[...] = a
    cosv, sinv = cos[...], sin[...]
    kv = dot(a, wkv[...])
    for head in range(KV_HEADS_C):
        cols = slice(head * HEAD_DIM, (head + 1) * HEAD_DIM)
        raw = kv[:, cols]
        kraw_out[:, cols] = raw.astype(BF)
        k_out[:, cols] = head_norm_rot(raw, gk[...], cosv, sinv).astype(BF)
    v_out[...] = kv[:, KW:].astype(BF)
    if with_q:
        qv = dot(a, wq[...])
        for head in range(Q_HEADS_C):
            cols = slice(head * HEAD_DIM, (head + 1) * HEAD_DIM)
            raw = qv[:, cols]
            qraw_out[:, cols] = raw.astype(BF)
            rot = head_norm_rot(raw, gq[...], cosv, sinv)
            q_out[:, cols] = (rot * SCORE_FOLD).astype(BF)


def project(x, g1, cos, sin, wq, wkv, gq, gk, with_q):
    rows = x.shape[0]
    bm = 256
    row = lambda width: pl.BlockSpec((bm, width), lambda i: (i, 0))
    ins = [x, g1, cos, sin] + ([wq] if with_q else []) + [wkv] + ([gq] if with_q else []) + [gk]
    specs = [row(D), whole((1, D)), row(HEAD_DIM), row(HEAD_DIM)]
    specs += [whole((D, QW))] if with_q else []
    specs += [whole((D, 2 * KW))]
    specs += [whole((1, HEAD_DIM))] * (2 if with_q else 1)
    widths = [D] + ([QW, QW] if with_q else []) + [KW, KW, KW]
    return pl.pallas_call(
        functools.partial(project_kernel, with_q),
        out_shape=[jax.ShapeDtypeStruct((rows, w), BF) for w in widths],
        grid=(rows // bm,),
        in_specs=specs,
        out_specs=[row(w) for w in widths],
        compiler_params=params(),
        cost_estimate=pl.CostEstimate(
            flops=2 * rows * D * (2 * KW + (QW if with_q else 0)),
            bytes_accessed=2 * rows * sum(widths) + 2 * D * (2 * KW + QW),
            transcendentals=0,
        ),
    )(*ins)


def attend_kernel(own_p, oth, q, k_own, v_own, k_oth, v_oth, qpos, kpos, cqc, ckc, o_out, l_out):
    i = pl.program_id(1)
    bq = q.shape[0]
    is_prompt = i * bq < own_p

    def run(kind):
        for head in range(GROUP):
            cols = slice(head * HEAD_DIM, (head + 1) * HEAD_DIM)
            qh = q[:, cols]
            parts = [(dot_t(qh, k_own[:own_p, :]), v_own[:own_p, :])]
            if oth:
                parts.append((dot_t(qh, k_oth[...]), v_oth[...]))
            if kind == 0:
                at = 0
                masked = []
                for s, v in parts:
                    n = s.shape[1]
                    ok = kpos[:, at : at + n] <= qpos[...]
                    masked.append((jnp.where(ok, s, -1e30), v))
                    at += n
                parts = masked
            else:
                s = dot_t(qh, k_own[own_p:, :])
                code, lowest = cqc[:, 0:1], cqc[:, 1:2]
                ok = (ckc[...] <= code) & (ckc[...] >= lowest)
                parts.append((jnp.where(ok, s, -1e30), v_own[own_p:, :]))
            top = functools.reduce(
                jnp.maximum, [jnp.max(s, axis=-1, keepdims=True) for s, _ in parts]
            )
            total = jnp.zeros((bq, 1), F32)
            acc = jnp.zeros((bq, HEAD_DIM), F32)
            for s, v in parts:
                e = jnp.exp2(s - top)
                total += jnp.sum(e, axis=-1, keepdims=True)
                acc += dot(e.astype(BF), v)
            o_out[:, cols] = (acc / total).astype(BF)
            level = jnp.broadcast_to(top + jnp.log2(total), (bq, HEAD_DIM))
            l_out[0, head : head + 1, :] = level.T[0:1, :]

    @pl.when(is_prompt)
    def _():
        run(0)

    @pl.when(jnp.logical_not(is_prompt))
    def _():
        run(1)


def attend(q, k_own, v_own, k_oth, v_oth, pos, own_p, bq=256):
    rows = q.shape[0]
    oth = k_oth.shape[0]
    keys = own_p + oth
    head_col = lambda n: pl.BlockSpec((n, HEAD_DIM), lambda h, i: (0, h))
    cont_block = lambda h, i: (jnp.maximum(i - own_p // bq, 0), 0)
    return pl.pallas_call(
        functools.partial(attend_kernel, own_p, oth),
        out_shape=[
            jax.ShapeDtypeStruct((rows, QW), BF),
            jax.ShapeDtypeStruct((KV_HEADS_C, GROUP, rows), F32),
        ],
        grid=(KV_HEADS_C, rows // bq),
        in_specs=[
            pl.BlockSpec((bq, GROUP * HEAD_DIM), lambda h, i: (i, h)),
            head_col(rows),
            head_col(rows),
            head_col(oth),
            head_col(oth),
            pl.BlockSpec((bq, 1), lambda h, i: (i, 0)),
            whole((1, keys)),
            pl.BlockSpec((bq, 2), cont_block),
            whole((1, rows - own_p)),
        ],
        out_specs=[
            pl.BlockSpec((bq, GROUP * HEAD_DIM), lambda h, i: (i, h)),
            pl.BlockSpec((1, GROUP, bq), lambda h, i: (h, 0, i)),
        ],
        compiler_params=params(),
        cost_estimate=pl.CostEstimate(
            flops=4 * rows * keys * QW * 2,
            bytes_accessed=4 * rows * QW,
            transcendentals=rows * keys * Q_HEADS_C,
        ),
    )(q, k_own, v_own, k_oth, v_oth, pos["q_col"], pos["k_row"], pos["cq_col"], pos["ck_row"])


def attend_back_kernel(
    own_p, oth, chunk,
    q, qraw, do, o, level, cos_q, sin_q, gq, gk,
    k_own, v_own, kraw_own, cos_o, sin_o, k_oth, v_oth, kraw_oth, cos_t, sin_t,
    qpos, kpos, cqc, ckc,
    dq_out, dk_own_out, dv_own_out, dk_oth_out, dv_oth_out, dgq_out, dgk_out,
    dk_own, dv_own, dk_oth, dv_oth, dq_acc,
):
    h, i = pl.program_id(0), pl.program_id(1)
    bq = q.shape[0]
    is_prompt = i * bq < own_p

    @pl.when(i == 0)
    def _():
        dk_own[...] = jnp.zeros_like(dk_own)
        dv_own[...] = jnp.zeros_like(dv_own)
        dk_oth[...] = jnp.zeros_like(dk_oth)
        dv_oth[...] = jnp.zeros_like(dv_oth)

    @pl.when((i == 0) & (h == 0))
    def _():
        dgq_out[...] = jnp.zeros_like(dgq_out)
        dgk_out[...] = jnp.zeros_like(dgk_out)

    heads = [slice(g * HEAD_DIM, (g + 1) * HEAD_DIM) for g in range(GROUP)]
    q2 = jnp.concatenate([q[:, c] for c in heads], axis=0)
    do2 = jnp.concatenate([do[:, c] for c in heads], axis=0)
    lev = jnp.concatenate([level[0, g : g + 1, :] for g in range(GROUP)], axis=1)
    drows = []
    for c in heads:
        both = jnp.sum(do[:, c].astype(F32) * o[:, c].astype(F32), axis=-1, keepdims=True)
        drows.append(jnp.broadcast_to(both, (bq, HEAD_DIM)).T[0:1, :])
    drow = jnp.concatenate(drows, axis=1)

    def step(k, v, ok, dk, dv, rows):
        s = dot_t(k, q2)
        p = jnp.exp2(s - lev)
        if ok is not None:
            p = jnp.where(ok, p, 0.0)
        dp = dot_t(v, do2)
        ds = (p * (dp - drow)).astype(BF)
        dv[rows, :] += dot(p.astype(BF), do2)
        dk[rows, :] += dot(ds, q2)
        return t_dot(k, ds)

    def twice(row):
        return jnp.concatenate([row] * GROUP, axis=1)

    qrow = twice(qpos[...])
    dq = None
    for at in range(0, own_p, chunk):
        rows = slice(at, at + chunk)
        ok = kpos[rows, :] <= qrow
        part = step(k_own[rows, :], v_own[rows, :], ok, dk_own, dv_own, rows)
        dq = part if dq is None else dq + part
    dq_acc[...] = dq
    if oth // chunk <= 4:
        for at in range(0, oth, chunk):
            rows = slice(at, at + chunk)
            ok = kpos[own_p + at : own_p + at + chunk, :] <= qrow
            dq_acc[...] += step(k_oth[rows, :], v_oth[rows, :], ok, dk_oth, dv_oth, rows)
    else:

        @pl.loop(0, oth // chunk)
        def _(j):
            rows = pl.ds(pl.multiple_of(j * chunk, chunk), chunk)
            ok = kpos[pl.ds(pl.multiple_of(own_p + j * chunk, chunk), chunk), :] <= qrow
            dq_acc[...] += step(k_oth[rows, :], v_oth[rows, :], ok, dk_oth, dv_oth, rows)

    @pl.when(jnp.logical_not(is_prompt))
    def _():
        code, lowest = twice(cqc[0:1, :]), twice(cqc[1:2, :])
        rows = slice(own_p, k_own.shape[0])
        ok = (ckc[...] <= code) & (ckc[...] >= lowest)
        dq_acc[...] += step(k_own[rows, :], v_own[rows, :], ok, dk_own, dv_own, rows)

    scale = HEAD_DIM ** (-0.5)
    gain_sum = jnp.zeros((8, HEAD_DIM), F32)
    for g, c in enumerate(heads):
        grad = dq_acc[:, g * bq : (g + 1) * bq].T * scale
        raw, rows = head_norm_rot_back(
            qraw[:, c].astype(F32), gq[...], cos_q[...], sin_q[...], grad
        )
        dq_out[:, c] = raw.astype(BF)
        gain_sum += jnp.sum(rows.reshape(bq // 8, 8, HEAD_DIM), axis=0)
    dgq_out[...] += gain_sum

    @pl.when(i == pl.num_programs(1) - 1)
    def _():
        for total, raw_in, cos, sin, out in (
            (dk_own, kraw_own, cos_o, sin_o, dk_own_out),
            (dk_oth, kraw_oth, cos_t, sin_t, dk_oth_out),
        ):
            n = total.shape[0]
            part = 256

            def finish(rows, total=total, raw_in=raw_in, cos=cos, sin=sin, out=out):
                raw, gain_rows = head_norm_rot_back(
                    raw_in[rows, :].astype(F32),
                    gk[...],
                    cos[rows, :],
                    sin[rows, :],
                    total[rows, :] * (1.0 / LOG2E),
                )
                out[rows, :] = raw.astype(BF)
                dgk_out[...] += jnp.sum(gain_rows.reshape(part // 8, 8, HEAD_DIM), axis=0)

            @pl.loop(0, n // part)
            def _(j):
                finish(pl.ds(pl.multiple_of(j * part, part), part))

        dv_own_out[...] = dv_own[...].astype(BF)
        dv_oth_out[...] = dv_oth[...].astype(BF)


def attend_back(q, qraw, do, o, level, own, oth, tabs, gq, gk, pos, own_p, bq=256):
    rows = q.shape[0]
    n_oth = oth[0].shape[0]
    keys = own_p + n_oth
    chunk = min(512, own_p)
    wide = pl.BlockSpec((bq, GROUP * HEAD_DIM), lambda h, i: (i, h))
    tab = pl.BlockSpec((bq, HEAD_DIM), lambda h, i: (i, 0))
    head_col = lambda n: pl.BlockSpec((n, HEAD_DIM), lambda h, i: (0, h))
    cont_block = lambda h, i: (0, jnp.maximum(i - own_p // bq, 0))
    one = whole((1, HEAD_DIM))
    full = lambda n: whole((n, HEAD_DIM))
    cos_own, sin_own, cos_oth, sin_oth = tabs
    return pl.pallas_call(
        functools.partial(attend_back_kernel, own_p, n_oth, chunk),
        out_shape=[
            jax.ShapeDtypeStruct((rows, QW), BF),
            jax.ShapeDtypeStruct((rows, KW), BF),
            jax.ShapeDtypeStruct((rows, KW), BF),
            jax.ShapeDtypeStruct((n_oth, KW), BF),
            jax.ShapeDtypeStruct((n_oth, KW), BF),
            jax.ShapeDtypeStruct((8, HEAD_DIM), F32),
            jax.ShapeDtypeStruct((8, HEAD_DIM), F32),
        ],
        grid=(KV_HEADS_C, rows // bq),
        in_specs=[
            wide, wide, wide, wide,
            pl.BlockSpec((1, GROUP, bq), lambda h, i: (h, 0, i)),
            tab, tab, one, one,
            head_col(rows), head_col(rows), head_col(rows), full(rows), full(rows),
            head_col(n_oth), head_col(n_oth), head_col(n_oth), full(n_oth), full(n_oth),
            pl.BlockSpec((1, bq), lambda h, i: (0, i)),
            whole((keys, 1)),
            pl.BlockSpec((2, bq), cont_block),
            whole((rows - own_p, 1)),
        ],
        out_specs=[
            wide, head_col(rows), head_col(rows), head_col(n_oth), head_col(n_oth),
            whole((8, HEAD_DIM)), whole((8, HEAD_DIM)),
        ],
        scratch_shapes=[
            pltpu.VMEM((rows, HEAD_DIM), F32),
            pltpu.VMEM((rows, HEAD_DIM), F32),
            pltpu.VMEM((n_oth, HEAD_DIM), F32),
            pltpu.VMEM((n_oth, HEAD_DIM), F32),
            pltpu.VMEM((HEAD_DIM, GROUP * bq), F32),
        ],
        compiler_params=params(),
        cost_estimate=pl.CostEstimate(
            flops=10 * rows * keys * QW * 2,
            bytes_accessed=12 * rows * QW,
            transcendentals=rows * keys * Q_HEADS_C,
        ),
    )(
        q, qraw, do, o, level, cos_own, sin_own, gq, gk,
        own[0], own[1], own[2], cos_own, sin_own,
        oth[0], oth[1], oth[2], cos_oth, sin_oth,
        pos["q_row"], pos["k_col"], pos["cq_row"], pos["ck_col"],
    )


def feed_kernel(h1, dy, g2, wg, wu, wd, b_out, hid_out, dg_out, du_out, y_out, db_out):
    hv = h1[...]
    b = hv * lax.rsqrt(jnp.mean(hv * hv, axis=-1, keepdims=True) + EPS_NORM) * g2[...]
    b = b.astype(BF)
    b_out[...] = b
    dyv = dy[...]
    step = 512
    y = db = None
    for at in range(0, FW, step):
        cols = slice(at, at + step)
        gate = dot(b, wg[:, cols])
        up = dot(b, wu[:, cols])
        dhid = dot_t(dyv, wd[cols, :])
        sig = 1.0 / (1.0 + jnp.exp(-gate))
        act = gate * sig
        hid = (act * up).astype(BF)
        dgate = (dhid * up * (sig * (1.0 + gate * (1.0 - sig)))).astype(BF)
        dup = (dhid * act).astype(BF)
        hid_out[:, cols] = hid
        dg_out[:, cols] = dgate
        du_out[:, cols] = dup
        y_part = dot(hid, wd[cols, :])
        db_part = dot_t(dgate, wg[:, cols]) + dot_t(dup, wu[:, cols])
        y = y_part if y is None else y + y_part
        db = db_part if db is None else db + db_part
    y_out[...] = y
    db_out[...] = db


def feed(h1, dy, g2, wg, wu, wd):
    rows = h1.shape[0]
    bm = 256
    row = lambda width: pl.BlockSpec((bm, width), lambda i: (i, 0))
    return pl.pallas_call(
        feed_kernel,
        out_shape=[
            jax.ShapeDtypeStruct((rows, D), BF),
            jax.ShapeDtypeStruct((rows, FW), BF),
            jax.ShapeDtypeStruct((rows, FW), BF),
            jax.ShapeDtypeStruct((rows, FW), BF),
            jax.ShapeDtypeStruct((rows, D), F32),
            jax.ShapeDtypeStruct((rows, D), F32),
        ],
        grid=(rows // bm,),
        in_specs=[
            row(D), row(D), whole((1, D)), whole((D, FW)), whole((D, FW)), whole((FW, D)),
        ],
        out_specs=[row(D), row(FW), row(FW), row(FW), row(D), row(D)],
        compiler_params=params(),
        cost_estimate=pl.CostEstimate(
            flops=12 * rows * D * FW,
            bytes_accessed=rows * (16 * D + 6 * FW) + 6 * D * FW,
            transcendentals=rows * FW,
        ),
    )(h1, dy, g2, wg, wu, wd)


def layout():
    q_width = HEADS * HEAD_DIM
    kv_width = KV_HEADS * HEAD_DIM
    return [
        (D,),
        (D, q_width),
        (D, kv_width),
        (D, kv_width),
        (HEAD_DIM,),
        (HEAD_DIM,),
        (q_width, D),
        (D,),
        (D, FF),
        (D, FF),
        (FF, D),
    ]


def unpack(flat_vec, core):
    lanes = flat_vec.reshape(-1, 128)
    split = {1: 1, 2: 1, 3: 1, 6: 0, 8: 1, 9: 1, 10: 0}
    pieces = []
    offset = 0
    for number, shape in enumerate(layout()):
        count = shape[0] if len(shape) == 1 else shape[0] * shape[1]
        if number not in split:
            pieces.append(lax.slice(flat_vec, (offset,), (offset + count,)))
        else:
            rows, cols = shape
            block = lanes[offset // 128 : (offset + count) // 128]
            block = block.reshape(rows, cols // 128, 128)
            axis = split[number]
            width = block.shape[axis] // CORES
            block = lax.dynamic_slice_in_dim(block, core * width, width, axis)
            pieces.append(block.reshape(block.shape[0], -1))
        offset += count
    return pieces


def plain_grads(
    pick, a, a_far, b, o, hid, dgate, dup, dy, da_out, dq, dk, dv, dg1, dgq, dgk, dg2
):
    a_all = jnp.concatenate([a, a_far])
    grads = [
        dg1,
        t_dot(a, dq),
        t_dot(a_all, jnp.concatenate(dk)),
        t_dot(a_all, jnp.concatenate(dv)),
        jnp.sum(dgq, axis=0),
        jnp.sum(dgk, axis=0),
        t_dot(o, da_out),
        0.5 * dg2,
        t_dot(b, dgate),
        t_dot(b, dup),
        t_dot(hid, dy),
    ]
    flat = []
    for number, (grad, shape) in enumerate(zip(grads, layout())):
        if len(shape) == 2:
            axis = 0 if number in (6, 10) else 1
            blank = jnp.zeros_like(grad)
            grad = jnp.concatenate([pick(grad, blank), pick(blank, grad)], axis=axis)
        flat.append(grad.reshape(-1).astype(F32))
    return lax.psum_scatter(
        jnp.concatenate(flat), ("dp", "seq"), scatter_dimension=0, tiled=True
    )


LANES = 128
SHARD = 491592
FLAT_AT = {"g1": 0, "wq": 8, "wk": 16392, "wv": 24584, "gqk": 32776, "wo": 32778,
           "g2": 49162, "wg": 49170, "wu": 73746, "wd": 98322}
PER_ROW = {"wq": 16, "wk": 8, "wv": 8, "wo": 8, "wg": 24, "wu": 24, "wd": 8}
X_FIRST = ("wq", "wo", "wd")
FEED_PARTS = {
    (1, 0): [("wo", 0, 704)],
    (1, 1): [("wo", 704, 1664)],
    (1, 2): [("wo", 1664, 2048), ("wg", 0, 192)],
    (1, 3): [("wg", 192, 512)],
    (2, 0): [("wg", 512, 832)],
    (2, 1): [("wg", 832, 1024), ("wu", 0, 128)],
    (2, 2): [("wu", 128, 448)],
    (2, 3): [("wu", 448, 768)],
    (3, 0): [("wu", 768, 1024), ("wd", 0, 192)],
    (3, 1): [("wd", 192, 1152)],
    (3, 2): [("wd", 1152, 2112)],
    (3, 3): [("wd", 2112, 3072)],
}
HEAD_PARTS = {0: ("wq", 0, 512), 1: ("wq", 512, 1024), 2: ("wk", 0, 1024), 3: ("wv", 0, 1024)}
TAIL = 288


def plane_pairs(distance, wanted=lambda dp, seq: True):
    pairs = []
    for dp in range(4):
        for seq in range(8):
            to = dp ^ distance
            if wanted(to, seq):
                pairs.append((dp * 8 + seq, to * 8 + seq))
    return pairs


def swap_dp(block, distance):
    return lax.ppermute(block, "dp", [(i, i ^ distance) for i in range(4)])


def cut(block, index, axis=1):
    width = block.shape[axis] // 2
    return lax.dynamic_slice_in_dim(block, index * width, width, axis)


def plane_sum(grad, x_first):
    dp = lax.axis_index("dp")
    order = ((dp % 2, 1), (dp // 2, 2)) if x_first else ((dp // 2, 2), (dp % 2, 1))
    for mine, distance in order:
        got = swap_dp(cut(grad, 1 - mine), distance)
        grad = (cut(grad, mine).astype(F32) + got.astype(F32)).astype(BF)
    return grad


def line_sum(parts):
    line = lax.axis_index("seq") // 2
    low, high = line % 2, line // 2
    parts = parts.reshape((2, 2) + parts.shape[1:])
    for mine, mask, axis in ((low, 2, 1), (high, 4, 0)):
        keep = lax.dynamic_index_in_dim(parts, mine, axis, keepdims=False)
        send = lax.dynamic_index_in_dim(parts, 1 - mine, axis, keepdims=False)
        parts = (keep.astype(F32) + xor_seq(send, mask).astype(F32)).astype(BF)
    return parts


def stack_rows(grad, low, high):
    return [grad[low:high, at : at + LANES] for at in range(0, grad.shape[1], LANES)]


def flat_rows(cores, name, low, high, dp):
    rows = high - low
    per = PER_ROW[name] // 8
    blocks = []
    for core in range(2):
        for place in range(4):
            chip = (place % 2) * 2 + place // 2 if name in X_FIRST else place
            part = cores[core][chip ^ dp]
            blocks += [part[at * rows : (at + 1) * rows] for at in range(per)]
    return jnp.stack(blocks, axis=1).reshape(rows * 8 * per, LANES)


def fast_grads(
    core, pick, a, a_far, b, o, hid, dgate, dup, dy, da_out, dq, dk, dv, dg1, dgq, dgk, dg2
):
    dp = lax.axis_index("dp")
    line = lax.axis_index("seq") // 2

    def both(mine):
        got = xor_seq(mine, 1)
        return jnp.concatenate([pick(mine, got), pick(got, mine)], axis=1)

    def my_columns(rows):
        return cut(rows, core)

    def grad_of(left, right, name):
        return plane_sum(t_dot(left, right).astype(BF), name in X_FIRST)

    sums = {}
    sums["wg"] = grad_of(b, dgate, "wg")
    sums["wu"] = grad_of(b, dup, "wu")
    sums["wd"] = grad_of(both(hid), my_columns(dy), "wd")
    sums["wo"] = grad_of(both(o), my_columns(da_out), "wo")
    spare = jnp.zeros((256, LANES), BF)
    per_line = []
    for z in range(4):
        blocks = [spare] if z == 0 else []
        for d in (1, 2, 3):
            for name, low, high in FEED_PARTS[d, z]:
                blocks += stack_rows(sums[name], low, high)
        per_line.append(jnp.concatenate(blocks))
    feed_part = line_sum(jnp.stack(per_line)).reshape(3, 960, LANES)

    def for_chip(d):
        return lax.dynamic_index_in_dim(feed_part, jnp.maximum(d - 1, 0), 0, keepdims=False)

    got = [for_chip(dp)]
    for distance in (1, 2, 3):
        pairs = plane_pairs(distance, lambda d, s: d > 0)
        got.append(lax.ppermute(for_chip(dp ^ distance), ("dp", "seq"), pairs))
    got = jnp.stack(got)
    far = xor_seq(got, 1)
    feed_cores = (pick(got, far), pick(far, got))

    def feed_branch(d, z):
        def build(cores):
            if d == 0:
                return jnp.zeros((7680, LANES), BF)
            at = 256 if z == 0 and d == 1 else 0
            rows = [jnp.zeros((2048, LANES), BF)] if at else []
            for name, low, high in FEED_PARTS[d, z]:
                size = (high - low) * PER_ROW[name] // 8
                part = [[cores[c][k][at : at + size] for k in range(4)] for c in range(2)]
                rows.append(flat_rows(part, name, low, high, d))
                at += size
            return jnp.concatenate(rows)

        return build

    place = dp * 4 + line
    feed_flat = lax.switch(
        place, [feed_branch(d, z) for d in range(4) for z in range(4)], feed_cores
    )
    chain = [(8 * d + s, 8 * d + s + 2) for d in range(4) for s in range(8) if 8 * d + s < 30]
    before = lax.ppermute(feed_flat[-16:], ("dp", "seq"), chain)

    a_all = jnp.concatenate([a, a_far])
    head_q = grad_of(a, dq, "wq")
    pair = [t_dot(a_all, jnp.concatenate(part)).astype(BF) for part in (dk, dv)]
    head_kv = plane_sum(jnp.concatenate(pair), False)
    head_part = line_sum(
        jnp.stack(
            [
                jnp.concatenate(stack_rows(head_q, 0, 512)),
                jnp.concatenate(stack_rows(head_q, 512, 1024)),
                head_kv[:1024],
                head_kv[1024:],
            ]
        )
    )
    tail = jnp.where(
        line < 2,
        jnp.concatenate([head_part[512 - TAIL // 2 : 512], head_part[1024 - TAIL // 2 :]]),
        head_part[1024 - TAIL :],
    )
    ring = [(8 * d + s, 8 * d + (s + 2) % 8) for d in range(4) for s in range(8)]
    head_all = jnp.concatenate([head_part, lax.ppermute(tail, ("dp", "seq"), ring)])
    got = [head_all]
    for distance in (1, 2, 3):
        pairs = plane_pairs(distance, lambda d, s: d == 0 or (d == 1 and s < 2))
        got.append(lax.ppermute(head_all, ("dp", "seq"), pairs))
    got = jnp.stack(got)
    far = xor_seq(got, 1)
    head_cores = (pick(got, far), pick(far, got))

    gains = jnp.concatenate([dg1, jnp.sum(dgq, 0), jnp.sum(dgk, 0), 0.5 * dg2])
    gains = lax.psum(gains, ("dp", "seq")).reshape(-1, LANES)

    def shard_branch(d, z, c):
        first = (8 * d + 2 * z + c) * SHARD // LANES
        last = min(first + 3842, 122898)

        def build(cores, flat, before, gains):
            parts = []
            part_at = lambda low, high: [[cores[k][j][low:high] for j in range(4)] for k in (0, 1)]
            if d == 0 or (d == 1 and z == 0):
                if d == 0 and z == 0:
                    parts.append((FLAT_AT["g1"], gains[:8]))
                else:
                    name, low, high = HEAD_PARTS[(z - 1) % 4]
                    low = high - TAIL * 8 // PER_ROW[name]
                    rows = flat_rows(part_at(1024, 1024 + TAIL), name, low, high, d)
                    parts.append((FLAT_AT[name] + low * PER_ROW[name], rows.astype(F32)))
            if d == 0:
                name, low, high = HEAD_PARTS[z]
                rows = flat_rows(part_at(0, 1024), name, low, high, d)
                parts.append((FLAT_AT[name] + low * PER_ROW[name], rows.astype(F32)))
            elif d == 1 and z == 0:
                parts.append((FLAT_AT["gqk"], gains[8:10]))
                parts.append((FLAT_AT["wo"], flat[2048:].astype(F32)))
            else:
                name, low, high = FEED_PARTS[d, z][0]
                at = FLAT_AT[name] + low * PER_ROW[name]
                parts.append((at - 16, before.astype(F32)))
                used = 0
                for name, low, high in FEED_PARTS[d, z]:
                    size = (high - low) * PER_ROW[name]
                    if used and name == "wg":
                        parts.append((FLAT_AT["g2"], gains[10:18]))
                    at = FLAT_AT[name] + low * PER_ROW[name]
                    parts.append((at, flat[used : used + size].astype(F32)))
                    used += size
            kept = []
            reached = first
            for at, rows in parts:
                low = max(first, at)
                high = min(last, at + rows.shape[0])
                if high > low:
                    assert low == reached
                    kept.append(rows[low - at : high - at])
                    reached = high
            assert reached == last
            kept.append(jnp.zeros((3856 - (last - first), LANES), F32))
            return jnp.concatenate(kept)

        return build

    branches = [shard_branch(d, z, c) for d in range(4) for z in range(4) for c in range(2)]
    rows = lax.switch(place * 2 + core, branches, head_cores, feed_flat, before, gains)
    skip = ((place * 2 + core) * (SHARD % LANES)) % LANES
    return shift_rows(rows, LANES - skip, 3848).reshape(-1)[:SHARD]


def shift_kernel(lanes, rows_in, out):
    count = out.shape[0]
    col = lax.broadcasted_iota(jnp.int32, (count, LANES), 1)
    shift = lanes[0]
    turn = lax.rem(shift, LANES)
    now = pltpu.roll(rows_in[0:count, :], turn, 1)
    after = pltpu.roll(rows_in[pl.ds(1, count), :], turn, 1)
    out[...] = jnp.where(col < shift, now, after)


def shift_rows(rows, shift, count):
    shift = jnp.asarray(shift, jnp.int32).reshape(1)
    return pl.pallas_call(
        shift_kernel,
        out_shape=jax.ShapeDtypeStruct((count, LANES), F32),
        in_specs=[pl.BlockSpec(memory_space=pltpu.SMEM), pl.BlockSpec(memory_space=pltpu.VMEM)],
        out_specs=pl.BlockSpec(memory_space=pltpu.VMEM),
        compiler_params=params(),
    )(shift, rows)


def gather_weights(master_new):
    rank = lax.axis_index("seq")
    flat = jnp.concatenate([master_new, jnp.zeros((3848 * LANES - SHARD,), F32)])
    rows = flat.reshape(3848, LANES)
    moved = rank * 72
    ahead = moved // LANES
    blank = jnp.zeros((8, LANES), F32)
    rows = jnp.concatenate([blank, rows, blank])
    rows = lax.dynamic_slice_in_dim(rows, 7 - ahead, 3856 + 1, 0)
    rows = jnp.concatenate([rows, jnp.zeros((7, LANES), F32)])
    block = shift_rows(rows, moved % LANES, 3848 + 8)[:3848].astype(BF)
    blocks = lax.all_gather(block, "seq", axis=0)
    body, ends = blocks[:, :3840], blocks[:, 3840:]
    heads = body[1:, :8] + ends[:-1]
    heads = jnp.concatenate([body[:1, :8], heads])
    rows = jnp.concatenate([heads, body[:, 8:]], axis=1).reshape(-1, LANES)
    rows = jnp.concatenate([rows, ends[-1]])
    return rows.reshape(-1)[: 8 * SHARD]


def norm_back(x, gain, grad):
    r = lax.rsqrt(jnp.mean(x * x, axis=-1, keepdims=True) + EPS_NORM)
    xh = x * r
    dg = grad * gain
    return r * (dg - xh * jnp.mean(dg * xh, axis=-1, keepdims=True)), jnp.sum(grad * xh, axis=0)


def tables(positions):
    half_dim = HEAD_DIM // 2
    frequency = ROPE_BASE ** (-jnp.arange(half_dim, dtype=F32) * 2.0 / HEAD_DIM)
    angles = positions.astype(F32)[:, None] * frequency[None, :]
    cosine, sine = jnp.cos(angles), jnp.sin(angles)
    return jnp.concatenate([cosine, cosine], 1), jnp.concatenate([-sine, sine], 1)


def shards(x_prompt, x_cont, dy_prompt, dy_cont, prompt_pos, weights, master, moment1, moment2):
    count = lax.axis_size("seq")
    rank = lax.axis_index("seq")
    half = count // 2
    side = rank // half
    core = rank % CORES
    chips = half // CORES
    p = x_prompt.shape[1]
    c = x_cont.shape[1]
    prompt_len = p * count
    own_p = 4 * p
    first = core == 0

    def pick(lo, hi):
        return jnp.where(first, lo, hi)

    def share(mine, got):
        return pick(mine, got), pick(got, mine)

    def chip_rows(prompt, cont):
        both = jnp.concatenate([prompt, cont], axis=1)
        own = lax.dynamic_index_in_dim(both, side, 0, keepdims=False)
        other = lax.dynamic_index_in_dim(both, 1 - side, 0, keepdims=False)
        mine = jnp.stack([own, xor_seq(other, half)])
        return mine, xor_seq(mine, 1)

    def join(mine, got):
        lo, hi = share(mine, got)
        rows_p = jnp.concatenate([lo[:, :p], hi[:, :p]], axis=0).reshape(4 * p, D)
        rows_c = jnp.concatenate([lo[:, p:], hi[:, p:]], axis=0).reshape(4 * c, D)
        return jnp.concatenate([rows_p, rows_c], axis=0)

    x_mine, x_got = chip_rows(x_prompt, x_cont)
    x = join(x_mine, x_got)
    far = x_mine[:, :p].reshape(1, 2 * p, D)
    mask = 2
    while mask < half:
        far = jnp.concatenate([far, xor_seq(far, mask)], axis=0)
        mask *= 2
    far = far[1:]
    lo, hi = share(far, xor_seq(far, 1))
    x_far = jnp.stack([lo, hi], axis=1).reshape(-1, D)
    dy = join(*chip_rows(dy_prompt, dy_cont))

    (g1, w_q, w_k, w_v, gq, gk, w_o, g2, w_g, w_u, w_d) = unpack(weights, core)
    g1, g2, gq, gk = [gain.astype(F32).reshape(1, -1) for gain in (g1, g2, gq, gk)]
    w_kv = jnp.concatenate([w_k, w_v], axis=1)

    chip_ids = (rank - core) ^ (CORES * jnp.arange(chips)[:, None, None])
    ids = (chip_ids + jnp.arange(CORES)[None, :, None]) ^ (half * jnp.arange(2)[None, None, :])
    own_group = lax.dynamic_index_in_dim(prompt_pos, side, 0, keepdims=False)
    key_pos = jnp.take(own_group.reshape(count, p), ids.reshape(-1), axis=0).reshape(-1)
    quarter = c // 2
    steps = jnp.arange(quarter, dtype=jnp.int32)
    own_half = [
        prompt_len + jnp.concatenate([k * quarter + steps, (3 - k) * quarter + steps])
        for k in range(CORES)
    ]
    cont_pos = jnp.concatenate([own_half[0], own_half[0], own_half[1], own_half[1]])
    seg = jnp.tile(jnp.repeat(jnp.arange(2, dtype=jnp.int32), c), CORES)
    big = 2 * prompt_len + 4 * c
    cont_code = seg * big + cont_pos
    query_pos = jnp.concatenate([key_pos[:own_p], cont_pos])
    cont_q = jnp.stack([cont_code, seg * big])
    pos = {
        "q_col": query_pos[:, None], "q_row": query_pos[None, :],
        "k_col": key_pos[:, None], "k_row": key_pos[None, :],
        "cq_col": cont_q.T, "cq_row": cont_q,
        "ck_col": cont_code[:, None], "ck_row": cont_code[None, :],
    }
    cos_own, sin_own = tables(query_pos)
    cos_far, sin_far = tables(key_pos[own_p:])

    a, q, qraw, k_own, kraw_own, v_own = project(x, g1, cos_own, sin_own, w_q, w_kv, gq, gk, True)
    a_far, k_far, kraw_far, v_far = project(x_far, g1, cos_far, sin_far, w_q, w_kv, gq, gk, False)
    o, level = attend(q, k_own, v_own, k_far, v_far, pos, own_p)

    h1_part = dot(o, w_o)
    h1 = x.astype(F32) + h1_part + xor_seq(h1_part.astype(BF), 1).astype(F32)
    b, hid, dgate, dup, y_part, db_part = feed(h1, dy, g2, w_g, w_u, w_d)

    def core_rows(rows, which):
        return jnp.concatenate(
            [
                lax.dynamic_slice_in_dim(rows, which * 2 * p, 2 * p),
                lax.dynamic_slice_in_dim(rows, own_p + which * 2 * c, 2 * c),
            ]
        )

    def core_sum(rows):
        sent = core_rows(rows, 1 - core).astype(BF)
        return core_rows(rows, core).astype(F32) + xor_seq(sent, 1).astype(F32)

    def send_home(rows):
        rows_p, rows_c = rows[: 2 * p], rows[2 * p :]
        own = jnp.concatenate([rows_p[:p], rows_c[:c]])
        away = jnp.concatenate([rows_p[p:], rows_c[c:]]).astype(BF)
        back = xor_seq(away, half).astype(F32)
        zero = side == 0
        out = jnp.stack([jnp.where(zero, own, back), jnp.where(zero, back, own)])
        return out[:, :p], out[:, p:]

    y_prompt, y_cont = send_home(core_rows(h1, core) + core_sum(y_part))

    db = db_part + xor_seq(db_part.astype(BF), 1).astype(F32)
    dh1_back, dg2 = norm_back(h1, g2, db)
    dh1 = dy.astype(F32) + dh1_back
    da_out = dh1.astype(BF)
    d_o = dot_t(da_out, w_o).astype(BF)

    (dq, dk_own, dv_own, dk_far, dv_far, dgq, dgk) = attend_back(
        q, qraw, d_o, o, level,
        (k_own, v_own, kraw_own), (k_far, v_far, kraw_far),
        (cos_own, sin_own, cos_far, sin_far), gq, gk, pos, own_p,
    )

    dkv_own = jnp.concatenate([dk_own, dv_own], axis=1)
    dkv_far = jnp.concatenate([dk_far, dv_far], axis=1)
    da_far = dot_t(dkv_far, w_kv).astype(BF).reshape(chips - 1, CORES, 2 * p, D)
    da_own = dot_t(dq, w_q) + dot_t(dkv_own, w_kv)
    far_keep = lax.dynamic_index_in_dim(da_far, core, 1, keepdims=False)
    far_send = lax.dynamic_index_in_dim(da_far, 1 - core, 1, keepdims=False)
    far_sum = far_keep.astype(F32) + xor_seq(far_send, 1).astype(F32)
    mine = core_sum(da_own)
    blocks = jnp.concatenate([mine[None, : 2 * p], far_sum])
    mask = half // 2
    while mask > 1:
        near, away = blocks[: mask // 2], blocks[mask // 2 :]
        blocks = near + xor_seq(away.astype(BF), mask).astype(F32)
        mask //= 2
    da = jnp.concatenate([blocks[0], mine[2 * p :]])
    x_core = core_rows(x, core).astype(F32)
    dx_back, dg1 = norm_back(x_core, g1, da)
    dx_prompt, dx_cont = send_home(core_rows(dh1, core) + dx_back)

    fast = count == 8 and lax.axis_size("dp") == 4
    if fast:
        grad_shard = fast_grads(
            core, pick, a, a_far, b, o, hid, dgate, dup, dy, da_out, dq,
            (dk_own, dk_far), (dv_own, dv_far), dg1, dgq, dgk, dg2,
        )
    else:
        grad_shard = plain_grads(
            pick, a, a_far, b, o, hid, dgate, dup, dy, da_out, dq,
            (dk_own, dk_far), (dv_own, dv_far), dg1, dgq, dgk, dg2,
        )
    moment1_new = BETA_ONE * moment1 + (1.0 - BETA_ONE) * grad_shard
    moment2_new = BETA_TWO * moment2 + (1.0 - BETA_TWO) * grad_shard * grad_shard
    update = moment1_new / CORRECT_ONE / (jnp.sqrt(moment2_new / CORRECT_TWO) + ADAM_EPS)
    master_new = master - LEARN_RATE * (update + DECAY_RATE * master)
    if fast:
        weights_new = gather_weights(master_new)
    else:
        weights_new = lax.all_gather(master_new.astype(BF), "seq", axis=0, tiled=True)
    return (y_prompt, y_cont, dx_prompt, dx_cont, grad_shard, master_new, moment1_new, weights_new)


def solution(mesh):
    placed = (
        P("dp", "seq", None),
        P("dp", "seq", None),
        P("dp", "seq", None),
        P("dp", "seq", None),
        P("dp", None),
        P(),
        P(("dp", "seq")),
        P(("dp", "seq")),
        P(("dp", "seq")),
    )
    return jax.shard_map(
        shards,
        mesh=mesh,
        in_specs=placed,
        out_specs=(
            P("dp", "seq", None),
            P("dp", "seq", None),
            P("dp", "seq", None),
            P("dp", "seq", None),
            P(("dp", "seq")),
            P(("dp", "seq")),
            P(("dp", "seq")),
            P("dp"),
        ),
        check_vma=False,
    )
```

```python
import functools

import jax
import jax.numpy as jnp
from jax import lax
from jax.experimental import pallas as pl
from jax.experimental.pallas import tpu as pltpu
from jax.sharding import PartitionSpec as P

D = 1024
FF = 3072
HEADS = 16
KV_HEADS = 8
HEAD_DIM = 128

EPS_NORM = 1e-06
ROPE_BASE = 1000000.0
BETA_ONE = 0.9
BETA_TWO = 0.95
ADAM_EPS = 1e-08
LEARN_RATE = 0.0003
DECAY_RATE = 0.1
CORRECT_ONE = 1.0 - 2.656139888758747e-05
CORRECT_TWO = 1.0 - 0.005920529220333996

CORES = 2
Q_HEADS_C = HEADS // CORES
KV_HEADS_C = KV_HEADS // CORES
QW = Q_HEADS_C * HEAD_DIM
KW = KV_HEADS_C * HEAD_DIM
FW = FF // CORES
GROUP = HEADS // KV_HEADS
LOG2E = 1.4426950408889634
SCORE_FOLD = HEAD_DIM ** (-0.5) * LOG2E
VMEM_LIMIT = 52 * 1024 * 1024
SMALL = pl.CostEstimate(flops=1000, bytes_accessed=1000, transcendentals=0)
BF = jnp.bfloat16
F32 = jnp.float32


def dot(left, right):
    return jnp.dot(left, right, preferred_element_type=F32)


def dot_t(left, right):
    return lax.dot_general(left, right, (((1,), (1,)), ((), ())), preferred_element_type=F32)


def t_dot(left, right):
    return lax.dot_general(left, right, (((0,), (0,)), ((), ())), preferred_element_type=F32)


def xor_seq(block, mask):
    count = lax.axis_size("seq")
    return lax.ppermute(block, "seq", [(i, i ^ mask) for i in range(count)])


def after(values, *earlier):
    return lax.optimization_barrier((values, earlier))[0]


def home_start(rows, half, p, c):
    rows_p, rows_c = rows[: 2 * p], rows[2 * p :]
    own = jnp.concatenate([rows_p[:p], rows_c[:c]])
    away = jnp.concatenate([rows_p[p:], rows_c[c:]]).astype(BF)
    return own, xor_seq(away, half)


def home_end(both, side, p):
    own, back = both[0], both[1].astype(F32)
    zero = side == 0
    out = jnp.stack([jnp.where(zero, own, back), jnp.where(zero, back, own)])
    return out[:, :p], out[:, p:]


def params(*semantics):
    return pltpu.CompilerParams(vmem_limit_bytes=VMEM_LIMIT)


def whole(shape):
    return pl.BlockSpec(shape, lambda *ids: (0,) * len(shape))


def head_norm_rot(raw, gain, cos, sin):
    r = lax.rsqrt(jnp.mean(raw * raw, axis=-1, keepdims=True) + EPS_NORM)
    n = raw * r * gain
    return n * cos + pltpu.roll(n, HEAD_DIM // 2, 1) * sin


def head_norm_rot_back(raw, gain, cos, sin, grad):
    dn = grad * cos - pltpu.roll(grad, HEAD_DIM // 2, 1) * sin
    r = lax.rsqrt(jnp.mean(raw * raw, axis=-1, keepdims=True) + EPS_NORM)
    xh = raw * r
    gain_rows = dn * xh
    dg = dn * gain
    return r * (dg - xh * jnp.mean(dg * xh, axis=-1, keepdims=True)), gain_rows


def project_kernel(with_q, *refs):
    if with_q:
        (x, g1, cos, sin, wq, wk, wv, gq, gk, a_out, q_out, qraw_out, k_out, kraw_out, v_out) = refs
    else:
        (x, g1, cos, sin, wk, wv, gk, a_out, k_out, kraw_out, v_out) = refs
    xv = x[...].astype(F32)
    a = xv * lax.rsqrt(jnp.mean(xv * xv, axis=-1, keepdims=True) + EPS_NORM) * g1[...]
    a = a.astype(BF)
    a_out[...] = a
    cosv, sinv = cos[...], sin[...]
    kv = dot(a, wk[...])
    for head in range(KV_HEADS_C):
        cols = slice(head * HEAD_DIM, (head + 1) * HEAD_DIM)
        raw = kv[:, cols]
        kraw_out[:, cols] = raw.astype(BF)
        k_out[:, cols] = head_norm_rot(raw, gk[...], cosv, sinv).astype(BF)
    v_out[...] = dot(a, wv[...]).astype(BF)
    if with_q:
        qv = dot(a, wq[...])
        for head in range(Q_HEADS_C):
            cols = slice(head * HEAD_DIM, (head + 1) * HEAD_DIM)
            raw = qv[:, cols]
            qraw_out[:, cols] = raw.astype(BF)
            rot = head_norm_rot(raw, gq[...], cosv, sinv)
            q_out[:, cols] = (rot * SCORE_FOLD).astype(BF)


def project(x, g1, cos, sin, wq, wk, wv, gq, gk, with_q):
    rows = x.shape[0]
    bm = 256
    row = lambda width: pl.BlockSpec((bm, width), lambda i: (i, 0))
    ins = [x, g1, cos, sin] + ([wq] if with_q else []) + [wk, wv] + ([gq] if with_q else []) + [gk]
    specs = [row(D), whole((1, D)), row(HEAD_DIM), row(HEAD_DIM)]
    specs += [whole((D, QW))] if with_q else []
    specs += [whole((D, KW))] * 2
    specs += [whole((1, HEAD_DIM))] * (2 if with_q else 1)
    widths = [D] + ([QW, QW] if with_q else []) + [KW, KW, KW]
    return pl.pallas_call(
        functools.partial(project_kernel, with_q),
        out_shape=[jax.ShapeDtypeStruct((rows, w), BF) for w in widths],
        grid=(rows // bm,),
        in_specs=specs,
        out_specs=[row(w) for w in widths],
        compiler_params=params(),
        cost_estimate=SMALL,
    )(*ins)


def attend_kernel(own_p, oth, cont, q, k_own, v_own, k_oth, v_oth, qpos, kpos, cqc, ckc, o_out, l_out):
    bq = q.shape[0]

    def run(kind):
        for head in range(GROUP):
            cols = slice(head * HEAD_DIM, (head + 1) * HEAD_DIM)
            qh = q[:, cols]
            parts = [(dot_t(qh, k_own[:own_p, :]), v_own[:own_p, :])]
            if oth:
                parts.append((dot_t(qh, k_oth[...]), v_oth[...]))
            if kind == 0:
                at = 0
                masked = []
                for s, v in parts:
                    n = s.shape[1]
                    ok = kpos[:, at : at + n] <= qpos[...]
                    masked.append((jnp.where(ok, s, -1e30), v))
                    at += n
                parts = masked
            else:
                s = dot_t(qh, k_own[own_p:, :])
                code, lowest = cqc[:, 0:1], cqc[:, 1:2]
                ok = (ckc[...] <= code) & (ckc[...] >= lowest)
                parts.append((jnp.where(ok, s, -1e30), v_own[own_p:, :]))
            top = functools.reduce(
                jnp.maximum, [jnp.max(s, axis=-1, keepdims=True) for s, _ in parts]
            )
            total = jnp.zeros((bq, 1), F32)
            acc = jnp.zeros((bq, HEAD_DIM), F32)
            for s, v in parts:
                e = jnp.exp2(s - top)
                total += jnp.sum(e, axis=-1, keepdims=True)
                acc += dot(e.astype(BF), v)
            o_out[:, cols] = (acc / total).astype(BF)
            level = jnp.broadcast_to(top + jnp.log2(total), (bq, HEAD_DIM))
            l_out[0, head : head + 1, :] = level.T[0:1, :]

    run(1 if cont else 0)


def attend(q, k_own, v_own, k_oth, v_oth, pos, own_p, cont, bq=256):
    rows = q.shape[0]
    oth = k_oth.shape[0]
    keys = own_p + oth
    base = own_p // bq if cont else 0
    here = rows - own_p if cont else own_p
    head_col = lambda n: pl.BlockSpec((n, HEAD_DIM), lambda h, i: (0, h))
    cont_block = lambda h, i: (i if cont else 0, 0)
    return pl.pallas_call(
        functools.partial(attend_kernel, own_p, oth, cont),
        out_shape=[
            jax.ShapeDtypeStruct((here, QW), BF),
            jax.ShapeDtypeStruct((KV_HEADS_C, GROUP, here), F32),
        ],
        grid=(KV_HEADS_C, here // bq),
        in_specs=[
            pl.BlockSpec((bq, GROUP * HEAD_DIM), lambda h, i: (base + i, h)),
            head_col(rows),
            head_col(rows),
            head_col(oth),
            head_col(oth),
            pl.BlockSpec((bq, 1), lambda h, i: (base + i, 0)),
            whole((1, keys)),
            pl.BlockSpec((bq, 2), cont_block),
            whole((1, rows - own_p)),
        ],
        out_specs=[
            pl.BlockSpec((bq, GROUP * HEAD_DIM), lambda h, i: (i, h)),
            pl.BlockSpec((1, GROUP, bq), lambda h, i: (h, 0, i)),
        ],
        compiler_params=params(),
        cost_estimate=SMALL,
    )(q, k_own, v_own, k_oth, v_oth, pos["q_col"], pos["k_row"], pos["cq_col"], pos["ck_row"])


def attend_back_kernel(
    own_p, oth, chunk,
    q, qraw, do, o, level, cos_q, sin_q, gq, gk,
    k_own, v_own, kraw_own, cos_o, sin_o, k_oth, v_oth, kraw_oth, cos_t, sin_t,
    qpos, kpos, cqc, ckc, *rest,
):
    (dq_out, dk_own_out, dv_own_out, dk_oth_out, dv_oth_out, dgq_out, dgk_out,
     dk_own, dv_own, dk_oth, dv_oth, dq_acc) = rest[-12:]
    i = pl.program_id(0)
    bq = q.shape[0]
    is_prompt = i * bq < own_p

    @pl.when(i == 0)
    def _():
        dk_own[...] = jnp.zeros_like(dk_own)
        dv_own[...] = jnp.zeros_like(dv_own)
        dk_oth[...] = jnp.zeros_like(dk_oth)
        dv_oth[...] = jnp.zeros_like(dv_oth)

    @pl.when(i == 0)
    def _():
        dgq_out[...] = jnp.zeros_like(dgq_out)
        dgk_out[...] = jnp.zeros_like(dgk_out)

    heads = [slice(g * HEAD_DIM, (g + 1) * HEAD_DIM) for g in range(GROUP)]
    q2 = jnp.concatenate([q[:, c] for c in heads], axis=0)
    do2 = jnp.concatenate([do[:, c] for c in heads], axis=0)
    lev = jnp.concatenate([level[0, g : g + 1, :] for g in range(GROUP)], axis=1)
    drows = []
    for c in heads:
        both = jnp.sum(do[:, c].astype(F32) * o[:, c].astype(F32), axis=-1, keepdims=True)
        drows.append(jnp.broadcast_to(both, (bq, HEAD_DIM)).T[0:1, :])
    drow = jnp.concatenate(drows, axis=1)

    def step(k, v, ok, dk, dv, rows):
        s = dot_t(k, q2)
        p = jnp.exp2(s - lev)
        if ok is not None:
            p = jnp.where(ok, p, 0.0)
        dp = dot_t(v, do2)
        ds = (p * (dp - drow)).astype(BF)
        dv[rows, :] += dot(p.astype(BF), do2)
        dk[rows, :] += dot(ds, q2)
        return t_dot(k, ds)

    def twice(row):
        return jnp.concatenate([row] * GROUP, axis=1)

    qrow = twice(qpos[...])
    dq = None
    for at in range(0, own_p, chunk):
        rows = slice(at, at + chunk)
        ok = kpos[rows, :] <= qrow
        part = step(k_own[rows, :], v_own[rows, :], ok, dk_own, dv_own, rows)
        dq = part if dq is None else dq + part
    dq_acc[...] = dq
    if oth // chunk <= 4:
        for at in range(0, oth, chunk):
            rows = slice(at, at + chunk)
            ok = kpos[own_p + at : own_p + at + chunk, :] <= qrow
            dq_acc[...] += step(k_oth[rows, :], v_oth[rows, :], ok, dk_oth, dv_oth, rows)
    else:

        @pl.loop(0, oth // chunk)
        def _(j):
            rows = pl.ds(pl.multiple_of(j * chunk, chunk), chunk)
            ok = kpos[pl.ds(pl.multiple_of(own_p + j * chunk, chunk), chunk), :] <= qrow
            dq_acc[...] += step(k_oth[rows, :], v_oth[rows, :], ok, dk_oth, dv_oth, rows)

    @pl.when(jnp.logical_not(is_prompt))
    def _():
        code, lowest = twice(cqc[0:1, :]), twice(cqc[1:2, :])
        rows = slice(own_p, k_own.shape[0])
        ok = (ckc[...] <= code) & (ckc[...] >= lowest)
        dq_acc[...] += step(k_own[rows, :], v_own[rows, :], ok, dk_own, dv_own, rows)

    scale = HEAD_DIM ** (-0.5)
    gain_sum = jnp.zeros((8, HEAD_DIM), F32)
    for g, c in enumerate(heads):
        grad = dq_acc[:, g * bq : (g + 1) * bq].T * scale
        raw, rows = head_norm_rot_back(
            qraw[:, c].astype(F32), gq[...], cos_q[...], sin_q[...], grad
        )
        dq_out[:, c] = raw.astype(BF)
        gain_sum += jnp.sum(rows.reshape(bq // 8, 8, HEAD_DIM), axis=0)
    dgq_out[...] += gain_sum

    @pl.when(i == pl.num_programs(0) - 1)
    def _():
        for total, raw_in, cos, sin, out in (
            (dk_own, kraw_own, cos_o, sin_o, dk_own_out),
            (dk_oth, kraw_oth, cos_t, sin_t, dk_oth_out),
        ):
            n = total.shape[0]
            part = 256

            def finish(rows, total=total, raw_in=raw_in, cos=cos, sin=sin, out=out):
                raw, gain_rows = head_norm_rot_back(
                    raw_in[rows, :].astype(F32),
                    gk[...],
                    cos[rows, :],
                    sin[rows, :],
                    total[rows, :] * (1.0 / LOG2E),
                )
                out[rows, :] = raw.astype(BF)
                dgk_out[...] += jnp.sum(gain_rows.reshape(part // 8, 8, HEAD_DIM), axis=0)

            @pl.loop(0, n // part)
            def _(j):
                finish(pl.ds(pl.multiple_of(j * part, part), part))

        dv_own_out[...] = dv_own[...].astype(BF)
        dv_oth_out[...] = dv_oth[...].astype(BF)


def attend_back(
    head, filled, waits, q, qraw, do, o, level, own, oth, tabs, gq, gk, pos, own_p, bq=256
):
    rows = q.shape[0]
    n_oth = oth[0].shape[0]
    keys = own_p + n_oth
    chunk = min(512, own_p)
    wide = pl.BlockSpec((bq, GROUP * HEAD_DIM), lambda i: (i, head))
    tab = pl.BlockSpec((bq, HEAD_DIM), lambda i: (i, 0))
    head_col = lambda n: pl.BlockSpec((n, HEAD_DIM), lambda i: (0, head))
    cont_block = lambda i: (0, jnp.maximum(i - own_p // bq, 0))
    one = whole((1, HEAD_DIM))
    full = lambda n: whole((n, HEAD_DIM))
    cos_own, sin_own, cos_oth, sin_oth = tabs
    ins = [
        q, qraw, do, o, level, cos_own, sin_own, gq, gk,
        own[0], own[1], own[2], cos_own, sin_own,
        oth[0], oth[1], oth[2], cos_oth, sin_oth,
        pos["q_row"], pos["k_col"], pos["cq_row"], pos["ck_col"],
    ]
    specs = [
        wide, wide, wide, wide,
        pl.BlockSpec((1, GROUP, bq), lambda i: (head, 0, i)),
        tab, tab, one, one,
        head_col(rows), head_col(rows), head_col(rows), full(rows), full(rows),
        head_col(n_oth), head_col(n_oth), head_col(n_oth), full(n_oth), full(n_oth),
        pl.BlockSpec((1, bq), lambda i: (0, i)),
        whole((keys, 1)),
        pl.BlockSpec((2, bq), cont_block),
        whole((rows - own_p, 1)),
    ]
    anywhere = pl.BlockSpec(memory_space=pl.ANY)
    aliases = {len(ins) + n: n for n in range(len(filled))}
    extra = list(filled) + list(waits)
    return pl.pallas_call(
        functools.partial(attend_back_kernel, own_p, n_oth, chunk),
        out_shape=[
            jax.ShapeDtypeStruct((rows, QW), BF),
            jax.ShapeDtypeStruct((rows, KW), BF),
            jax.ShapeDtypeStruct((rows, KW), BF),
            jax.ShapeDtypeStruct((n_oth, KW), BF),
            jax.ShapeDtypeStruct((n_oth, KW), BF),
            jax.ShapeDtypeStruct((8, HEAD_DIM), F32),
            jax.ShapeDtypeStruct((8, HEAD_DIM), F32),
        ],
        grid=(rows // bq,),
        in_specs=specs + [anywhere] * len(extra),
        out_specs=[
            wide, head_col(rows), head_col(rows), head_col(n_oth), head_col(n_oth),
            whole((8, HEAD_DIM)), whole((8, HEAD_DIM)),
        ],
        scratch_shapes=[
            pltpu.VMEM((rows, HEAD_DIM), F32),
            pltpu.VMEM((rows, HEAD_DIM), F32),
            pltpu.VMEM((n_oth, HEAD_DIM), F32),
            pltpu.VMEM((n_oth, HEAD_DIM), F32),
            pltpu.VMEM((HEAD_DIM, GROUP * bq), F32),
        ],
        input_output_aliases=aliases,
        compiler_params=params(),
        cost_estimate=SMALL,
    )(*ins, *extra)


def feed_kernel(x, part, got, dy, g2, wg, wu, wd, *rest):
    h1_out, b_out, hid_out, dg_out, du_out, y_out, db_out = rest[-7:]
    hv = x[...].astype(F32) + (part[...].astype(F32) + got[...].astype(F32))
    h1_out[...] = hv
    b = hv * lax.rsqrt(jnp.mean(hv * hv, axis=-1, keepdims=True) + EPS_NORM) * g2[...]
    b = b.astype(BF)
    b_out[...] = b
    dyv = dy[...]
    step = 512
    y = db = None
    for at in range(0, FW, step):
        cols = slice(at, at + step)
        gate = dot(b, wg[:, cols])
        up = dot(b, wu[:, cols])
        dhid = dot_t(dyv, wd[cols, :])
        sig = 1.0 / (1.0 + jnp.exp(-gate))
        act = gate * sig
        hid = (act * up).astype(BF)
        dgate = (dhid * up * (sig * (1.0 + gate * (1.0 - sig)))).astype(BF)
        dup = (dhid * act).astype(BF)
        hid_out[:, cols] = hid
        dg_out[:, cols] = dgate
        du_out[:, cols] = dup
        y_part = dot(hid, wd[cols, :])
        db_part = dot_t(dgate, wg[:, cols]) + dot_t(dup, wu[:, cols])
        y = y_part if y is None else y + y_part
        db = db_part if db is None else db + db_part
    y_out[...] = y.astype(BF)
    db_out[...] = db.astype(BF)


def feed(filled, base, total, x, part, got, dy, g2, wg, wu, wd):
    rows = part.shape[0]
    bm = 256
    base //= bm
    row = lambda width: pl.BlockSpec((bm, width), lambda i: (i, 0))
    later = lambda width: pl.BlockSpec((bm, width), lambda i: (base + i, 0))
    anywhere = pl.BlockSpec(memory_space=pl.ANY)
    return pl.pallas_call(
        feed_kernel,
        out_shape=[
            jax.ShapeDtypeStruct((total, D), F32),
            jax.ShapeDtypeStruct((total, D), BF),
            jax.ShapeDtypeStruct((total, FW), BF),
            jax.ShapeDtypeStruct((total, FW), BF),
            jax.ShapeDtypeStruct((total, FW), BF),
            jax.ShapeDtypeStruct((rows, D), BF),
            jax.ShapeDtypeStruct((rows, D), BF),
        ],
        grid=(rows // bm,),
        in_specs=[
            later(D), row(D), row(D), later(D), whole((1, D)), whole((D, FW)), whole((D, FW)), whole((FW, D)),
        ]
        + [anywhere] * len(filled),
        out_specs=[later(D), later(D), later(FW), later(FW), later(FW), row(D), row(D)],
        input_output_aliases={8 + n: n for n in range(len(filled))},
        compiler_params=params(),
        cost_estimate=SMALL,
    )(x, part, got, dy, g2, wg, wu, wd, *filled)


def back_kernel(h1, dy, mine, got, g2, wo, *rest):
    dh_out, da_out, do_out, dg_out = rest[-4:]
    hv = h1[...]
    db = mine[...].astype(F32) + got[...].astype(F32)
    r = lax.rsqrt(jnp.mean(hv * hv, axis=-1, keepdims=True) + EPS_NORM)
    xh = hv * r
    dg = db * g2[...]
    dh = dy[...].astype(F32) + r * (dg - xh * jnp.mean(dg * xh, axis=-1, keepdims=True))
    dh_out[...] = dh
    da = dh.astype(BF)
    da_out[...] = da
    do_out[...] = dot_t(da, wo[...]).astype(BF)
    gain = jnp.sum((db * xh).reshape(hv.shape[0] // 8, 8, D), axis=0)

    @pl.when(pl.program_id(0) == 0)
    def _():
        dg_out[...] = jnp.zeros_like(dg_out)

    dg_out[...] += gain


def back_norm(filled, base, h1, dy, mine, got, g2, wo):
    rows, total = mine.shape[0], h1.shape[0]
    bm = 256
    base //= bm
    row = lambda width: pl.BlockSpec((bm, width), lambda i: (i, 0))
    later = lambda width: pl.BlockSpec((bm, width), lambda i: (base + i, 0))
    anywhere = pl.BlockSpec(memory_space=pl.ANY)
    return pl.pallas_call(
        back_kernel,
        out_shape=[
            jax.ShapeDtypeStruct((total, D), F32),
            jax.ShapeDtypeStruct((total, D), BF),
            jax.ShapeDtypeStruct((total, QW), BF),
            jax.ShapeDtypeStruct((8, D), F32),
        ],
        grid=(rows // bm,),
        in_specs=[later(D), later(D), row(D), row(D), whole((1, D)), whole((QW, D))]
        + [anywhere] * len(filled),
        out_specs=[later(D), later(D), later(QW), whole((8, D))],
        input_output_aliases={6 + n: n for n in range(len(filled))},
        compiler_params=params(),
        cost_estimate=SMALL,
    )(h1, dy, mine, got, g2, wo, *filled)


def layout():
    q_width = HEADS * HEAD_DIM
    kv_width = KV_HEADS * HEAD_DIM
    return [
        (D,),
        (D, q_width),
        (D, kv_width),
        (D, kv_width),
        (HEAD_DIM,),
        (HEAD_DIM,),
        (q_width, D),
        (D,),
        (D, FF),
        (D, FF),
        (FF, D),
    ]


LANES = 128
SHARD = 491592
FLAT_AT = {"g1": 0, "wq": 8, "wk": 16392, "wv": 24584, "gqk": 32776, "wo": 32778,
           "g2": 49162, "wg": 49170, "wu": 73746, "wd": 98322}
PER_ROW = {"wq": 16, "wk": 8, "wv": 8, "wo": 8, "wg": 24, "wu": 24, "wd": 8}


def matrix_kernel(per, split, place, main, extra, out, wide):
    count = main.shape[0]
    wide[:count, :] = main[...].astype(F32)
    wide[count:, :] = extra[...].astype(F32)
    rows = out.shape[0]
    first = place[1]
    if split:
        first = first + place[0] * (out.shape[1] // LANES)
    for at in range(out.shape[1] // LANES):
        cols = slice(at * LANES, (at + 1) * LANES)
        out[:, cols] = wide[pl.ds(first + at, rows, stride=per), :].astype(BF)


def matrix(lanes, name, split, rows, step, core):
    per = PER_ROW[name]
    count = step * per
    at = FLAT_AT[name]
    base = at // count
    width = per * LANES // (CORES if split else 1)
    blocks = (rows if split else rows // CORES) // step
    place = jnp.stack([core, jnp.full_like(core, at - base * count)]).astype(jnp.int32)

    def block(i, place):
        return base + i + (0 if split else place[0] * blocks)

    return pl.pallas_call(
        functools.partial(matrix_kernel, per, split),
        out_shape=jax.ShapeDtypeStruct((blocks * step, width), BF),
        grid_spec=pltpu.PrefetchScalarGridSpec(
            num_scalar_prefetch=1,
            grid=(blocks,),
            in_specs=[
                pl.BlockSpec((count, LANES), lambda i, place: (block(i, place), 0)),
                pl.BlockSpec(
                    (32, LANES), lambda i, place: ((block(i, place) + 1) * (count // 32), 0)
                ),
            ],
            out_specs=pl.BlockSpec((step, width), lambda i, place: (i, 0)),
            scratch_shapes=[pltpu.VMEM((count + 32, LANES), F32)],
        ),
        compiler_params=params(),
        cost_estimate=SMALL,
    )(place, lanes, lanes)


def gain_vectors(flat_vec):
    take = lambda name, skip, size: lax.slice(
        flat_vec, (FLAT_AT[name] * LANES + skip,), (FLAT_AT[name] * LANES + skip + size,)
    )
    gains = take("g1", 0, D), take("g2", 0, D), take("gqk", 0, LANES), take("gqk", LANES, LANES)
    return [gain.astype(F32).reshape(1, -1) for gain in gains]


def plain_grads(
    pick, a, a_far, b, o, hid, dgate, dup, dy, da_out, dq, dk, dv, dg1, dgq, dgk, dg2
):
    a_all = jnp.concatenate([a, a_far])
    grads = [
        dg1,
        t_dot(a, dq),
        t_dot(a_all, jnp.concatenate(dk)),
        t_dot(a_all, jnp.concatenate(dv)),
        jnp.sum(dgq, axis=0),
        jnp.sum(dgk, axis=0),
        t_dot(o, da_out),
        0.5 * dg2,
        t_dot(b, dgate),
        t_dot(b, dup),
        t_dot(hid, dy),
    ]
    flat = []
    for number, (grad, shape) in enumerate(zip(grads, layout())):
        if len(shape) == 2:
            axis = 0 if number in (6, 10) else 1
            blank = jnp.zeros_like(grad)
            grad = jnp.concatenate([pick(grad, blank), pick(blank, grad)], axis=axis)
        flat.append(grad.reshape(-1).astype(F32))
    return lax.psum_scatter(
        jnp.concatenate(flat), ("dp", "seq"), scatter_dimension=0, tiled=True
    )


X_FIRST = ("wq", "wg", "wd")
FEED_PARTS = {
    (1, 0): [("wo", 0, 704)],
    (1, 1): [("wo", 704, 1664)],
    (1, 2): [("wo", 1664, 2048), ("wg", 0, 192)],
    (1, 3): [("wg", 192, 512)],
    (2, 0): [("wg", 512, 832)],
    (2, 1): [("wg", 832, 1024), ("wu", 0, 128)],
    (2, 2): [("wu", 128, 448)],
    (2, 3): [("wu", 448, 768)],
    (3, 0): [("wu", 768, 1024), ("wd", 0, 192)],
    (3, 1): [("wd", 192, 1152)],
    (3, 2): [("wd", 1152, 2112)],
    (3, 3): [("wd", 2112, 3072)],
}
HEAD_PARTS = {0: ("wq", 0, 512), 1: ("wq", 512, 1024), 2: ("wk", 0, 1024), 3: ("wv", 0, 1024)}
TAIL = 288


def plane_pairs(distance, wanted=lambda dp, seq: True):
    pairs = []
    for dp in range(4):
        for seq in range(8):
            to = dp ^ distance
            if wanted(to, seq):
                pairs.append((dp * 8 + seq, to * 8 + seq))
    return pairs


def swap_dp(block, distance):
    return lax.ppermute(block, "dp", [(i, i ^ distance) for i in range(4)])


def cut(block, index, axis=1):
    width = block.shape[axis] // 2
    return lax.dynamic_slice_in_dim(block, index * width, width, axis)


def plane_order(name):
    dp = lax.axis_index("dp")
    order = ((dp % 2, 1), (dp // 2, 2))
    return order if name in X_FIRST else order[::-1]


def plane_step(grad, name, step):
    mine, distance = plane_order(name)[step]
    return cut(grad, mine), swap_dp(cut(grad, 1 - mine), distance)


def kept(*stages):
    return [stage[0] for stage in stages]


def added(stage):
    return (stage[0].astype(F32) + stage[1].astype(F32)).astype(BF)


def line_start(parts):
    low = lax.axis_index("seq") // 2 % 2
    parts = parts.reshape((2, 2) + parts.shape[1:])
    keep = lax.dynamic_index_in_dim(parts, low, 1, keepdims=False)
    send = lax.dynamic_index_in_dim(parts, 1 - low, 1, keepdims=False)
    return keep, xor_seq(send, 2)


def line_next(stage):
    high = lax.axis_index("seq") // 4
    parts = added(stage)
    keep = lax.dynamic_index_in_dim(parts, high, 0, keepdims=False)
    send = lax.dynamic_index_in_dim(parts, 1 - high, 0, keepdims=False)
    return keep, xor_seq(send, 4)


def stack_rows(grad, low, high):
    return [grad[low:high, at : at + LANES] for at in range(0, grad.shape[1], LANES)]


def feed_line(sums):
    spare = jnp.zeros((256, LANES), BF)
    per_line = []
    for z in range(4):
        blocks = [spare] if z == 0 else []
        for d in (1, 2, 3):
            for name, low, high in FEED_PARTS[d, z]:
                blocks += stack_rows(sums[name], low, high)
        per_line.append(jnp.concatenate(blocks))
    return line_start(jnp.stack(per_line))


ROWS = 3872
PART = 176
BEFORE = TAIL * 8


def spread(who, other, core, dp, name, at, rows, into, to):
    per = PER_ROW[name] // 8
    for source, side in ((who, core), (other, 1 - core)):
        for place in range(4):
            chip = (place % 2) * 2 + place // 2 if name in X_FIRST else place
            for col in range(per):
                first = to + side * (4 * per) + place * per + col
                block = source[chip ^ dp, at + col * rows : at + (col + 1) * rows, :]
                into[pl.ds(first, rows, stride=8 * per), :] = block.astype(F32)


def feed_flat_kernel(info, who, other, out):
    core, spot = info[0], info[1]

    @pl.when((spot < 4) | (spot == 4))
    def _():
        out[...] = jnp.zeros_like(out)

    for (d, z), blocks in FEED_PARTS.items():

        @pl.when(spot == d * 4 + z)
        def _(d=d, z=z, blocks=blocks):
            at, to = (256, 2048) if (d, z) == (1, 0) else (0, 0)
            for name, low, high in blocks:
                rows = high - low
                spread(who, other, core, 0, name, at, rows, out, to)
                at += rows * PER_ROW[name] // 8
                to += rows * PER_ROW[name]


def main_row(d, z):
    if (d, z) == (1, 0):
        return FLAT_AT["gqk"]
    name, low, _ = HEAD_PARTS[z] if d == 0 else FEED_PARTS[d, z][0]
    return FLAT_AT[name] + low * PER_ROW[name]


STARTS = [
    (8 * d + 2 * z + c) * SHARD // LANES - (main_row(d, z) - BEFORE)
    for d in range(4)
    for z in range(4)
    for c in range(2)
]
WIDE = max(BEFORE + 8192, (max(STARTS) + ROWS + 16) // 8 * 8)


def adam(grad, master, moment1, moment2):
    moment1_new = BETA_ONE * moment1 + (1.0 - BETA_ONE) * grad
    moment2_new = BETA_TWO * moment2 + (1.0 - BETA_TWO) * grad * grad
    update = moment1_new / CORRECT_ONE / (jnp.sqrt(moment2_new / CORRECT_TWO) + ADAM_EPS)
    return moment1_new, master - LEARN_RATE * (update + DECAY_RATE * master)


def finish_kernel(
    info, who, other, flat, before, gains, master, moment1, moment2,
    grad_out, moment1_out, master_out, block_out, wide, work,
):
    core, spot, start, skip, ahead, rest = [info[i] for i in range(6)]

    def put_before(name, dp):
        spread(who, other, core, dp, name, 1024, TAIL * 8 // PER_ROW[name], wide, 0)

    @pl.when(spot == 0)
    def _():
        wide[BEFORE - 8 : BEFORE, :] = gains[0:8, :]

    @pl.when((spot == 1) | (spot == 2))
    def _():
        put_before("wq", 0)

    @pl.when(spot == 3)
    def _():
        put_before("wk", 0)

    @pl.when(spot == 4)
    def _():
        put_before("wv", 1)
        wide[BEFORE : BEFORE + 2, :] = gains[8:10, :]
        wide[BEFORE + 2 : BEFORE + 2 + 5632, :] = flat[2048:, :]

    @pl.when(spot < 2)
    def _():
        spread(who, other, core, 0, "wq", 0, 512, wide, BEFORE)

    @pl.when((spot == 2) | (spot == 3))
    def _():
        spread(who, other, core, 0, "wk", 0, 1024, wide, BEFORE)

    @pl.when(spot > 4)
    def _():
        wide[BEFORE - 16 : BEFORE, :] = before[...]

    @pl.when(spot == 6)
    def _():
        wide[BEFORE : BEFORE + 3072, :] = flat[:3072, :]
        wide[BEFORE + 3072 : BEFORE + 3080, :] = gains[10:18, :]
        wide[BEFORE + 3080 : BEFORE + 7688, :] = flat[3072:, :]

    @pl.when((spot == 5) | (spot > 6))
    def _():
        wide[BEFORE : BEFORE + 7680, :] = flat[...]

    col = lax.broadcasted_iota(jnp.int32, (PART, LANES), 1)
    row = lax.broadcasted_iota(jnp.int32, (PART, LANES), 0)
    work[0:8, :] = jnp.zeros((8, LANES), F32)
    work[ROWS + 8 :, :] = jnp.zeros((8, LANES), F32)
    turn = lax.rem(LANES - skip, LANES)

    @pl.loop(0, ROWS // PART)
    def _(j):
        at = pl.multiple_of(j * PART, 8)
        here = pl.ds(at, PART)
        now = pltpu.roll(wide[pl.ds(start + at, PART), :], turn, 1)
        after_it = pltpu.roll(wide[pl.ds(start + at + 1, PART), :], turn, 1)
        grad = jnp.where(col < LANES - skip, now, after_it)
        moment1_new, master_new = adam(grad, master[here, :], moment1[here, :], moment2[here, :])
        grad_out[here, :] = grad
        moment1_out[here, :] = moment1_new
        master_out[here, :] = master_new
        inside = (at + row) * LANES + col < SHARD
        work[pl.ds(at + 8, PART), :] = jnp.where(inside, master_new, 0.0)

    @pl.loop(0, ROWS // PART)
    def _(j):
        at = pl.multiple_of(j * PART, 16)
        now = pltpu.roll(work[pl.ds(7 - ahead + at, PART), :], rest, 1)
        after_it = pltpu.roll(work[pl.ds(8 - ahead + at, PART), :], rest, 1)
        block_out[pl.ds(at, PART), :] = jnp.where(col < rest, now, after_it).astype(BF)


def local(kernel, shapes, scratch, info, *arrays):
    vmem = pl.BlockSpec(memory_space=pltpu.VMEM)
    return pl.pallas_call(
        kernel,
        out_shape=shapes,
        in_specs=[pl.BlockSpec(memory_space=pltpu.SMEM)] + [vmem] * len(arrays),
        out_specs=jax.tree.map(lambda _: vmem, shapes),
        scratch_shapes=scratch,
        compiler_params=params(),
        cost_estimate=SMALL,
    )(jnp.stack(info).astype(jnp.int32), *arrays)


def fast_grads(core, feed_stage, head_q, head_kv, gains, states, da, to_home):
    dp = lax.axis_index("dp")
    rank = lax.axis_index("seq")
    line = rank // 2
    spot = dp * 4 + line
    gains = jnp.concatenate(gains).reshape(1, -1, LANES)
    gains = jnp.broadcast_to(gains, (32,) + gains.shape[1:])
    gains = lax.all_to_all(gains, ("dp", "seq"), 0, 0, tiled=True)
    head_q, head_kv = added(head_q), added(head_kv)
    head_stage = line_start(
        jnp.stack(
            [
                jnp.concatenate(stack_rows(head_q, 0, 512)),
                jnp.concatenate(stack_rows(head_q, 512, 1024)),
                head_kv[:1024],
                head_kv[1024:],
            ]
        )
    )
    feed_part = added(feed_stage).reshape(3, 960, LANES)
    feed_part = after(feed_part, head_stage[0])
    feed_got = jnp.concatenate([feed_part[:1], feed_part])
    feed_got = lax.all_to_all(feed_got, "dp", 0, 0, tiled=True)
    head_stage, da, gains = after((head_stage, da, gains))
    head_stage = line_next(head_stage)
    feed_got = after(feed_got, head_stage[0])
    feed_far = xor_seq(feed_got, 1)
    dx_rows = to_home(after(da, head_stage[0]))
    head_part = added(head_stage)
    tail = jnp.where(
        line < 2,
        jnp.concatenate([head_part[512 - TAIL // 2 : 512], head_part[1024 - TAIL // 2 :]]),
        head_part[1024 - TAIL :],
    )
    ring = [(8 * d + s, 8 * d + (s + 2) % 8) for d in range(4) for s in range(8)]
    head_all = jnp.concatenate([head_part, lax.ppermute(tail, ("dp", "seq"), ring)])
    head_got = [head_all]
    for distance in (1, 2, 3):
        pairs = plane_pairs(distance, lambda d, s: d == 0 or (d == 1 and s < 2))
        head_got.append(lax.ppermute(head_all, ("dp", "seq"), pairs))
    feed_flat = local(
        feed_flat_kernel,
        jax.ShapeDtypeStruct((7680, LANES), F32),
        [],
        (core, spot),
        feed_got,
        after(feed_far, head_all),
    )
    chain = [(8 * d + s, 8 * d + s + 2) for d in range(4) for s in range(8) if 8 * d + s < 30]
    before = lax.ppermute(feed_flat[-16:], ("dp", "seq"), chain)
    gains = jnp.sum(gains, axis=0)
    head_got, dx_rows, before = after((head_got, dx_rows, before))
    head_got = jnp.stack(head_got)
    head_far = xor_seq(head_got, 1)

    index = spot * 2 + core
    start = jnp.asarray(STARTS, jnp.int32)[index]
    info = (core, spot, start, index * (SHARD % LANES) % LANES, rank * 72 // LANES, rank * 72 % LANES)
    rows = jax.ShapeDtypeStruct((ROWS, LANES), F32)
    results = local(
        finish_kernel,
        [rows, rows, rows, jax.ShapeDtypeStruct((ROWS, LANES), BF)],
        [pltpu.VMEM((WIDE, LANES), F32), pltpu.VMEM((ROWS + 16, LANES), F32)],
        info, head_got, head_far, feed_flat, before, gains, *states,
    )
    return *results, dx_rows


def gather_weights(block):
    blocks = lax.all_gather(block, "seq", axis=0)
    body, ends = blocks[:, :3840], blocks[:, 3840:3848]
    heads = body[1:, :8] + ends[:-1]
    heads = jnp.concatenate([body[:1, :8], heads])
    rows = jnp.concatenate([heads, body[:, 8:]], axis=1).reshape(-1, LANES)
    rows = jnp.concatenate([rows, ends[-1]])
    return rows.reshape(-1)[: 8 * SHARD]


def norm_back(x, gain, grad):
    r = lax.rsqrt(jnp.mean(x * x, axis=-1, keepdims=True) + EPS_NORM)
    xh = x * r
    dg = grad * gain
    return r * (dg - xh * jnp.mean(dg * xh, axis=-1, keepdims=True))


def gain_sum(x, grad):
    x = x.astype(F32)
    r = lax.rsqrt(jnp.mean(x * x, axis=-1, keepdims=True) + EPS_NORM)
    return jnp.sum(grad.astype(F32) * x * r, axis=0)


def tables(positions):
    half_dim = HEAD_DIM // 2
    frequency = ROPE_BASE ** (-jnp.arange(half_dim, dtype=F32) * 2.0 / HEAD_DIM)
    angles = positions.astype(F32)[:, None] * frequency[None, :]
    cosine, sine = jnp.cos(angles), jnp.sin(angles)
    return jnp.concatenate([cosine, cosine], 1), jnp.concatenate([-sine, sine], 1)


def shards(x_prompt, x_cont, dy_prompt, dy_cont, prompt_pos, weights, master, moment1, moment2):
    count = lax.axis_size("seq")
    rank = lax.axis_index("seq")
    half = count // 2
    side = rank // half
    core = rank % CORES
    chips = half // CORES
    p = x_prompt.shape[1]
    c = x_cont.shape[1]
    prompt_len = p * count
    own_p = 4 * p
    first = core == 0

    def pick(lo, hi):
        return jnp.where(first, lo, hi)

    def share(mine, got):
        return pick(mine, got), pick(got, mine)

    def far_rows(block):
        rows = block[None]
        mask = 2
        while mask < half:
            rows = jnp.concatenate([rows, xor_seq(rows, mask)])
            mask *= 2
        return rows[1:]

    def sides(prompt, cont):
        rows = jnp.concatenate([prompt, cont], axis=1)
        own = lax.dynamic_index_in_dim(rows, side, 0, keepdims=False)
        other = lax.dynamic_index_in_dim(rows, 1 - side, 0, keepdims=False)
        return own, other

    def join(own, recv, own_got, recv_got):
        lo, hi = share(own, own_got)
        lo2, hi2 = share(recv, recv_got)
        rows_p = [lo[:p], lo2[:p], hi[:p], hi2[:p]]
        rows_c = [lo[p:], lo2[p:], hi[p:], hi2[p:]]
        return jnp.concatenate(rows_p + rows_c, axis=0)

    x_own, x_other = sides(x_prompt, x_cont)
    x_recv = xor_seq(x_other, half)
    far_one = far_rows(x_own[:p])
    x_own_got = xor_seq(x_own, 1)

    lanes = weights.reshape(-1, LANES)
    g1, g2, gq, gk = gain_vectors(weights)
    w_q = matrix(lanes, "wq", True, D, 128, core)
    w_k = matrix(lanes, "wk", True, D, 256, core)
    w_v = matrix(lanes, "wv", True, D, 256, core)
    x_recv = after(x_recv, w_q, w_k, w_v)
    far_two = far_rows(x_recv[:p])
    x_recv_got = xor_seq(x_recv, 1)
    far_one = after(far_one, x_recv)
    far_one_got = xor_seq(far_one, 1)
    lanes = after(lanes, x_recv)
    w_g = matrix(lanes, "wg", True, D, 128, core)
    w_u = matrix(lanes, "wu", True, D, 128, core)
    x_recv_got = after(x_recv_got, w_g, w_u)
    x = join(x_own, x_recv, x_own_got, x_recv_got)

    chip_ids = (rank - core) ^ (CORES * jnp.arange(chips)[:, None, None])
    ids = (chip_ids + jnp.arange(CORES)[None, :, None]) ^ (half * jnp.arange(2)[None, None, :])
    own_group = lax.dynamic_index_in_dim(prompt_pos, side, 0, keepdims=False)
    key_pos = jnp.take(own_group.reshape(count, p), ids.reshape(-1), axis=0).reshape(-1)
    quarter = c // 2
    steps = jnp.arange(quarter, dtype=jnp.int32)
    own_half = [
        prompt_len + jnp.concatenate([k * quarter + steps, (3 - k) * quarter + steps])
        for k in range(CORES)
    ]
    cont_pos = jnp.concatenate([own_half[0], own_half[0], own_half[1], own_half[1]])
    seg = jnp.tile(jnp.repeat(jnp.arange(2, dtype=jnp.int32), c), CORES)
    big = 2 * prompt_len + 4 * c
    cont_code = seg * big + cont_pos
    query_pos = jnp.concatenate([key_pos[:own_p], cont_pos])
    cont_q = jnp.stack([cont_code, seg * big])
    pos = {
        "q_col": query_pos[:, None], "q_row": query_pos[None, :],
        "k_col": key_pos[:, None], "k_row": key_pos[None, :],
        "cq_col": cont_q.T, "cq_row": cont_q,
        "ck_col": cont_code[:, None], "ck_row": cont_code[None, :],
    }
    cos_own, sin_own = tables(query_pos)
    cos_far, sin_far = tables(key_pos[own_p:])

    a, q, qraw, k_own, kraw_own, v_own = project(x, g1, cos_own, sin_own, w_q, w_k, w_v, gq, gk, True)
    far_two = after(far_two, a)
    far_two_got = xor_seq(far_two, 1)
    lanes = after(lanes, a)
    w_d = matrix(lanes, "wd", False, FF, 384, core)
    w_o = matrix(lanes, "wo", False, HEADS * HEAD_DIM, 256, core)
    far_two_got = after(far_two_got, w_d, w_o)
    dy_own, dy_other = after(sides(dy_prompt, dy_cont), far_two)
    dy_recv = xor_seq(dy_other, half)
    dy_own_got = xor_seq(dy_own, 1)
    lo, hi = share(far_one, far_one_got)
    lo2, hi2 = share(far_two, far_two_got)
    x_far = jnp.stack([lo, lo2, hi, hi2], axis=1).reshape(-1, D)
    a_far, k_far, kraw_far, v_far = project(x_far, g1, cos_far, sin_far, w_q, w_k, w_v, gq, gk, False)
    rows = x.shape[0]
    o_p, level_p = attend(q, k_own, v_own, k_far, v_far, pos, own_p, False)
    part_p = dot(o_p, w_o).astype(BF)
    part_p_got = xor_seq(part_p, 1)
    q, part_p, dy_recv = after((q, part_p, dy_recv))
    dy_recv_got = xor_seq(dy_recv, 1)
    o_c, level_c = attend(q, k_own, v_own, k_far, v_far, pos, own_p, True)
    o_c, dy_recv_got = after((o_c, dy_recv_got))
    part_c = dot(o_c, w_o).astype(BF)
    part_c_got = xor_seq(part_c, 1)
    part_p_got = after(part_p_got, part_c)
    dy = join(dy_own, dy_recv, dy_own_got, dy_recv_got)
    *filled, y_p, db_p = feed((), 0, rows, x, part_p, part_p_got, dy, g2, w_g, w_u, w_d)
    db_p_got = xor_seq(db_p, 1)
    o = jnp.concatenate([o_p, o_c])
    o_got = xor_seq(o, 1)
    part_c_got, o_got = after((part_c_got, o_got), db_p)
    *filled, y_c, db_c = feed(filled, own_p, rows, x, part_c, part_c_got, dy, g2, w_g, w_u, w_d)
    h1, b, hid, dgate, dup = filled
    db_c_got = xor_seq(db_c, 1)
    hid_got = xor_seq(hid, 1)
    level = jnp.concatenate([level_p, level_c], axis=2)
    y_part = jnp.concatenate([y_p, y_c])
    fast = count == 8 and lax.axis_size("dp") == 4
    def core_rows(rows, which):
        return jnp.concatenate(
            [
                lax.dynamic_slice_in_dim(rows, which * 2 * p, 2 * p),
                lax.dynamic_slice_in_dim(rows, own_p + which * 2 * c, 2 * c),
            ]
        )

    y_got = xor_seq(core_rows(y_part, 1 - core), 1)
    if fast:
        flow = {"wg": plane_step(t_dot(b, dgate).astype(BF), "wg", 0)}
        flow["wu"] = plane_step(t_dot(b, dup).astype(BF), "wu", 0)
        dy_cols = cut(dy, core)
        grad_d = t_dot(hid, dy_cols).astype(BF)
        hid_got, y_got = after((hid_got, y_got), kept(flow["wg"], flow["wu"]))
        grad_d = share(grad_d, t_dot(hid_got, dy_cols).astype(BF))
        flow["wd"] = plane_step(jnp.concatenate(grad_d), "wd", 0)
        db_p_got, db_c_got = after((db_p_got, db_c_got), kept(flow["wd"]))
    y_core = core_rows(h1, core) + core_rows(y_part, core).astype(F32) + y_got.astype(F32)
    *filled, dg2_p = back_norm((), 0, h1, dy, db_p, db_p_got, g2, w_o)
    *filled, dg2_c = back_norm(filled, own_p, h1, dy, db_c, db_c_got, g2, w_o)
    dh1, da_out, d_o = filled
    dg2 = jnp.sum(dg2_p + dg2_c, axis=0)

    filled, waits = (), [y_core]
    back = []
    if fast:
        cols = cut(da_out, core)
        grad_o = share(t_dot(o, cols).astype(BF), t_dot(o_got, cols).astype(BF))
        flow["wo"] = plane_step(jnp.concatenate(grad_o), "wo", 0)
        flow["wg"], flow["wu"] = after((flow["wg"], flow["wu"]), flow["wo"][0])
        for name in ("wg", "wu"):
            flow[name] = plane_step(added(flow[name]), name, 1)
        waits += kept(*flow.values())
    for head in range(KV_HEADS_C):
        *filled, dgq, dgk = attend_back(
            head, filled, waits, q, qraw, d_o, o, level,
            (k_own, v_own, kraw_own), (k_far, v_far, kraw_far),
            (cos_own, sin_own, cos_far, sin_far), gq, gk, pos, own_p,
        )
        waits = []
        back.append((dgq, dgk))
        if head == 2:
            y_rows = after(y_rows, dgq)
            waits = [y_rows[1]]
        if fast and head == 1:
            flow = after(flow, dgq)
            flow["wg"], flow["wu"] = added(flow["wg"]), added(flow["wu"])
            for name in ("wd", "wo"):
                flow[name] = plane_step(added(flow[name]), name, 1)
            waits += [flow["wg"], flow["wu"]] + kept(flow["wd"], flow["wo"])
        if head == 1:
            y_rows = home_start(after(y_core, dgq, waits), half, p, c)
            waits.append(y_rows[0])
        if fast and head == 2:
            flow = after(flow, dgq)
            flow["wd"], flow["wo"] = added(flow["wd"]), added(flow["wo"])
            feed_stage = feed_line(flow)
            waits += kept(feed_stage)
    dq, dk_own, dv_own, dk_far, dv_far = filled
    dgq, dgk = [sum(parts) for parts in zip(*back)]
    y_prompt, y_cont = home_end(y_rows, side, p)

    if fast:
        dq, feed_stage = after((dq, feed_stage))
        head_q = plane_step(t_dot(a, dq).astype(BF), "wq", 0)
        a_all = jnp.concatenate([a, a_far])
        pair = [(dk_own, dk_far), (dv_own, dv_far)]
        pair = [t_dot(a_all, jnp.concatenate(part)).astype(BF) for part in pair]
        head_kv = plane_step(jnp.concatenate(pair), "wk", 0)
        feed_stage = line_next(feed_stage)
        dk_own, dk_far = after((dk_own, dk_far), kept(feed_stage, head_q, head_kv))

    da_far = (dot_t(dk_far, w_k) + dot_t(dv_far, w_v)).astype(BF)
    da_far = da_far.reshape(chips - 1, CORES, 2 * p, D)
    da_own = (dot_t(dq, w_q) + dot_t(dk_own, w_k) + dot_t(dv_own, w_v)).astype(BF)
    far_keep = lax.dynamic_index_in_dim(da_far, core, 1, keepdims=False)
    far_send = lax.dynamic_index_in_dim(da_far, 1 - core, 1, keepdims=False)
    sent = jnp.concatenate([core_rows(da_own, 1 - core), far_send.reshape(-1, D)])
    got = xor_seq(sent, 1)
    dg1 = gain_sum(x, da_own) + gain_sum(x_far, da_far.reshape(-1, D))
    if fast:
        head_q, head_kv, feed_stage = after((head_q, head_kv, feed_stage))
        head_q = plane_step(added(head_q), "wq", 1)
        head_kv = plane_step(added(head_kv), "wk", 1)
        got = after(got, kept(head_q, head_kv))
    mine = core_rows(da_own, core).astype(F32) + got[: rows // 2].astype(F32)
    far_sum = far_keep.astype(F32) + got[rows // 2 :].reshape(far_keep.shape).astype(F32)
    blocks = jnp.concatenate([mine[None, : 2 * p], far_sum])
    mask = half // 2
    while mask > 1:
        near, away = blocks[: mask // 2], blocks[mask // 2 :]
        blocks = near + xor_seq(away.astype(BF), mask).astype(F32)
        mask //= 2
    da = jnp.concatenate([blocks[0], mine[2 * p :]])

    def to_dx(da):
        return core_rows(dh1, core) + norm_back(core_rows(x, core).astype(F32), g1, da)

    if fast:
        gains = [dg1, jnp.sum(dgq, 0), jnp.sum(dgk, 0), 0.5 * dg2]
        states = [
            jnp.concatenate([state, jnp.zeros((ROWS * LANES - SHARD,), F32)]).reshape(ROWS, LANES)
            for state in (master, moment1, moment2)
        ]
        states = after(states, x)
        *results, block, dx_rows = fast_grads(
            core, feed_stage, head_q, head_kv, gains, states, da, lambda da: home_start(to_dx(da), half, p, c)
        )
        weights_new = gather_weights(block)
        grad_shard, moment1_new, master_new = [one.reshape(-1)[:SHARD] for one in results]
    else:
        grad_shard = plain_grads(
            pick, a, a_far, b, o, hid, dgate, dup, dy, da_out, dq,
            (dk_own, dk_far), (dv_own, dv_far), dg1, dgq, dgk, dg2,
        )
        dx_rows = home_start(to_dx(da), half, p, c)
        moment1_new, master_new = adam(grad_shard, master, moment1, moment2)
        weights_new = lax.all_gather(master_new.astype(BF), "seq", axis=0, tiled=True)
    dx_prompt, dx_cont = home_end(dx_rows, side, p)
    return (y_prompt, y_cont, dx_prompt, dx_cont, grad_shard, master_new, moment1_new, weights_new)


def solution(mesh):
    placed = (
        P("dp", "seq", None),
        P("dp", "seq", None),
        P("dp", "seq", None),
        P("dp", "seq", None),
        P("dp", None),
        P(),
        P(("dp", "seq")),
        P(("dp", "seq")),
        P(("dp", "seq")),
    )
    return jax.shard_map(
        shards,
        mesh=mesh,
        in_specs=placed,
        out_specs=(
            P("dp", "seq", None),
            P("dp", "seq", None),
            P("dp", "seq", None),
            P("dp", "seq", None),
            P(("dp", "seq")),
            P(("dp", "seq")),
            P(("dp", "seq")),
            P("dp"),
        ),
        check_vma=False,
    )
```

```python
import functools

import jax
import jax.numpy as jnp
from jax import lax
from jax.experimental import pallas as pl
from jax.experimental.pallas import tpu as pltpu
from jax.sharding import PartitionSpec as P

D = 1024
FF = 3072
HEADS = 16
KV_HEADS = 8
HEAD_DIM = 128

EPS_NORM = 1e-06
ROPE_BASE = 1000000.0
BETA_ONE = 0.9
BETA_TWO = 0.95
ADAM_EPS = 1e-08
LEARN_RATE = 0.0003
DECAY_RATE = 0.1
CORRECT_ONE = 1.0 - 2.656139888758747e-05
CORRECT_TWO = 1.0 - 0.005920529220333996

CORES = 2
Q_HEADS_C = HEADS // CORES
KV_HEADS_C = KV_HEADS // CORES
QW = Q_HEADS_C * HEAD_DIM
KW = KV_HEADS_C * HEAD_DIM
FW = FF // CORES
GROUP = HEADS // KV_HEADS
LOG2E = 1.4426950408889634
SCORE_FOLD = HEAD_DIM ** (-0.5) * LOG2E
VMEM_LIMIT = 52 * 1024 * 1024
SMALL = pl.CostEstimate(flops=1000, bytes_accessed=1000, transcendentals=0)
BF = jnp.bfloat16
F32 = jnp.float32


def dot(left, right):
    return jnp.dot(left, right, preferred_element_type=F32)


def dot_t(left, right):
    return lax.dot_general(left, right, (((1,), (1,)), ((), ())), preferred_element_type=F32)


def t_dot(left, right):
    return lax.dot_general(left, right, (((0,), (0,)), ((), ())), preferred_element_type=F32)


def turned(block):
    return block.astype(F32).T.astype(BF)


def xor_seq(block, mask):
    count = lax.axis_size("seq")
    return lax.ppermute(block, "seq", [(i, i ^ mask) for i in range(count)])


def after(values, *earlier):
    return lax.optimization_barrier((values, earlier))[0]


def home_start(rows, half, p, c):
    rows_p, rows_c = rows[: 2 * p], rows[2 * p :]
    own = jnp.concatenate([rows_p[:p], rows_c[:c]])
    away = jnp.concatenate([rows_p[p:], rows_c[c:]]).astype(BF)
    return own, xor_seq(away, half)


def home_end(both, side, p):
    own, back = both[0], both[1].astype(F32)
    zero = side == 0
    out = jnp.stack([jnp.where(zero, own, back), jnp.where(zero, back, own)])
    return out[:, :p], out[:, p:]


def params(*semantics):
    return pltpu.CompilerParams(vmem_limit_bytes=VMEM_LIMIT)


def whole(shape):
    return pl.BlockSpec(shape, lambda *ids: (0,) * len(shape))


def head_norm_rot(raw, gain, cos, sin):
    r = lax.rsqrt(jnp.mean(raw * raw, axis=-1, keepdims=True) + EPS_NORM)
    n = raw * r * gain
    return n * cos + pltpu.roll(n, HEAD_DIM // 2, 1) * sin


def head_norm_rot_back(raw, gain, cos, sin, grad):
    dn = grad * cos - pltpu.roll(grad, HEAD_DIM // 2, 1) * sin
    r = lax.rsqrt(jnp.mean(raw * raw, axis=-1, keepdims=True) + EPS_NORM)
    xh = raw * r
    gain_rows = dn * xh
    dg = dn * gain
    return r * (dg - xh * jnp.mean(dg * xh, axis=-1, keepdims=True)), gain_rows


def project_kernel(with_q, *refs):
    if with_q:
        (x, g1, cos, sin, wq, wk, wv, gq, gk, a_out, q_out, qraw_out, k_out, kraw_out, v_out) = refs
    else:
        (x, g1, cos, sin, wk, wv, gk, a_out, k_out, kraw_out, v_out) = refs
    xv = x[...].astype(F32)
    a = xv * lax.rsqrt(jnp.mean(xv * xv, axis=-1, keepdims=True) + EPS_NORM) * g1[...]
    a = a.astype(BF)
    a_out[...] = a
    cosv, sinv = cos[...], sin[...]
    kv = dot(a, wk[...])
    for head in range(KV_HEADS_C):
        cols = slice(head * HEAD_DIM, (head + 1) * HEAD_DIM)
        raw = kv[:, cols]
        kraw_out[:, cols] = raw.astype(BF)
        k_out[:, cols] = head_norm_rot(raw, gk[...], cosv, sinv).astype(BF)
    v_out[...] = dot(a, wv[...]).astype(BF)
    if with_q:
        qv = dot(a, wq[...])
        for head in range(Q_HEADS_C):
            cols = slice(head * HEAD_DIM, (head + 1) * HEAD_DIM)
            raw = qv[:, cols]
            qraw_out[:, cols] = raw.astype(BF)
            rot = head_norm_rot(raw, gq[...], cosv, sinv)
            q_out[:, cols] = (rot * SCORE_FOLD).astype(BF)


def project(x, g1, cos, sin, wq, wk, wv, gq, gk, with_q):
    rows = x.shape[0]
    bm = 256
    row = lambda width: pl.BlockSpec((bm, width), lambda i: (i, 0))
    ins = [x, g1, cos, sin] + ([wq] if with_q else []) + [wk, wv] + ([gq] if with_q else []) + [gk]
    specs = [row(D), whole((1, D)), row(HEAD_DIM), row(HEAD_DIM)]
    specs += [whole((D, QW))] if with_q else []
    specs += [whole((D, KW))] * 2
    specs += [whole((1, HEAD_DIM))] * (2 if with_q else 1)
    widths = [D] + ([QW, QW] if with_q else []) + [KW, KW, KW]
    return pl.pallas_call(
        functools.partial(project_kernel, with_q),
        out_shape=[jax.ShapeDtypeStruct((rows, w), BF) for w in widths],
        grid=(rows // bm,),
        in_specs=specs,
        out_specs=[row(w) for w in widths],
        compiler_params=params(),
        cost_estimate=SMALL,
    )(*ins)


def attend_kernel(own_p, oth, cont, q, k_own, v_own, k_oth, v_oth, qpos, kpos, cqc, ckc, o_out, l_out):
    bq = q.shape[0]

    def run(kind):
        for head in range(GROUP):
            cols = slice(head * HEAD_DIM, (head + 1) * HEAD_DIM)
            qh = q[:, cols]
            parts = [(dot_t(qh, k_own[:own_p, :]), v_own[:own_p, :])]
            if oth:
                parts.append((dot_t(qh, k_oth[...]), v_oth[...]))
            if kind == 0:
                at = 0
                masked = []
                for s, v in parts:
                    n = s.shape[1]
                    ok = kpos[:, at : at + n] <= qpos[...]
                    masked.append((jnp.where(ok, s, -1e30), v))
                    at += n
                parts = masked
            else:
                s = dot_t(qh, k_own[own_p:, :])
                code, lowest = cqc[:, 0:1], cqc[:, 1:2]
                ok = (ckc[...] <= code) & (ckc[...] >= lowest)
                parts.append((jnp.where(ok, s, -1e30), v_own[own_p:, :]))
            top = functools.reduce(
                jnp.maximum, [jnp.max(s, axis=-1, keepdims=True) for s, _ in parts]
            )
            total = jnp.zeros((bq, 1), F32)
            acc = jnp.zeros((bq, HEAD_DIM), F32)
            for s, v in parts:
                e = jnp.exp2(s - top)
                total += jnp.sum(e, axis=-1, keepdims=True)
                acc += dot(e.astype(BF), v)
            o_out[:, cols] = (acc / total).astype(BF)
            level = jnp.broadcast_to(top + jnp.log2(total), (bq, HEAD_DIM))
            l_out[0, head : head + 1, :] = level.T[0:1, :]

    run(1 if cont else 0)


def attend_wide_kernel(
    own_p, oth, cont, q, k_own, v_own, k_oth, v_oth, qpos, kpos, cqc, ckc,
    o_out, l_out, vt_own, vt_oth,
):
    bq = q.shape[0]

    @pl.when(pl.program_id(1) == 0)
    def _():
        vt_own[...] = turned(v_own[...])
        vt_oth[...] = turned(v_oth[...])

    def twice(row):
        return jnp.concatenate([row] * GROUP, axis=1)

    heads = [slice(g * HEAD_DIM, (g + 1) * HEAD_DIM) for g in range(GROUP)]
    q2 = jnp.concatenate([q[:, c] for c in heads], axis=0)
    parts = [(dot_t(k_own[:own_p, :], q2), vt_own[:, :own_p])]
    parts.append((dot_t(k_oth[...], q2), vt_oth[...]))
    if cont:
        s = dot_t(k_own[own_p:, :], q2)
        code, lowest = twice(cqc[0:1, :]), twice(cqc[1:2, :])
        ok = (ckc[...] <= code) & (ckc[...] >= lowest)
        parts.append((jnp.where(ok, s, -1e30), vt_own[:, own_p:]))
    else:
        at = 0
        for n, (s, v) in enumerate(parts):
            ok = kpos[at : at + s.shape[0], :] <= twice(qpos[...])
            parts[n] = (jnp.where(ok, s, -1e30), v)
            at += s.shape[0]
    top = functools.reduce(jnp.maximum, [jnp.max(s, axis=0, keepdims=True) for s, _ in parts])
    total = jnp.zeros((1, GROUP * bq), F32)
    acc = jnp.zeros((HEAD_DIM, GROUP * bq), F32)
    for s, v in parts:
        e = jnp.exp2(s - top)
        total += jnp.sum(e, axis=0, keepdims=True)
        acc += dot(v, e.astype(BF))
    level = top + jnp.log2(total)
    out = acc / total
    for g, c in enumerate(heads):
        rows = slice(g * bq, (g + 1) * bq)
        o_out[:, c] = out[:, rows].T.astype(BF)
        l_out[0, g : g + 1, :] = level[:, rows]


def attend(q, k_own, v_own, k_oth, v_oth, pos, own_p, cont):
    rows = q.shape[0]
    oth = k_oth.shape[0]
    keys = own_p + oth
    bq = 256 if cont else min(512, own_p)
    base = own_p // bq if cont else 0
    here = rows - own_p if cont else own_p
    head_col = lambda n: pl.BlockSpec((n, HEAD_DIM), lambda h, i: (0, h))
    if cont:
        masks = [
            pl.BlockSpec((bq, 1), lambda h, i: (base + i, 0)),
            whole((1, keys)),
            pl.BlockSpec((bq, 2), lambda h, i: (i, 0)),
            whole((1, rows - own_p)),
        ]
        names, scratch = ("q_col", "k_row", "cq_col", "ck_row"), []
    else:
        masks = [
            pl.BlockSpec((1, bq), lambda h, i: (0, i)),
            whole((keys, 1)),
            whole((2, rows - own_p)),
            whole((rows - own_p, 1)),
        ]
        names = ("q_row", "k_col", "cq_row", "ck_col")
        scratch = [pltpu.VMEM((HEAD_DIM, rows), BF), pltpu.VMEM((HEAD_DIM, oth), BF)]
    return pl.pallas_call(
        functools.partial(attend_kernel if cont else attend_wide_kernel, own_p, oth, cont),
        out_shape=[
            jax.ShapeDtypeStruct((here, QW), BF),
            jax.ShapeDtypeStruct((KV_HEADS_C, GROUP, here), F32),
        ],
        grid=(KV_HEADS_C, here // bq),
        in_specs=[
            pl.BlockSpec((bq, GROUP * HEAD_DIM), lambda h, i: (base + i, h)),
            head_col(rows),
            head_col(rows),
            head_col(oth),
            head_col(oth),
            *masks,
        ],
        out_specs=[
            pl.BlockSpec((bq, GROUP * HEAD_DIM), lambda h, i: (i, h)),
            pl.BlockSpec((1, GROUP, bq), lambda h, i: (h, 0, i)),
        ],
        scratch_shapes=scratch,
        compiler_params=params(),
        cost_estimate=SMALL,
    )(q, k_own, v_own, k_oth, v_oth, *[pos[name] for name in names])


def attend_back_kernel(
    own_p, oth, chunk,
    q, qraw, do, o, level, cos_q, sin_q, gq, gk,
    k_own, v_own, kraw_own, cos_o, sin_o, k_oth, v_oth, kraw_oth, cos_t, sin_t,
    qpos, kpos, cqc, ckc, *rest,
):
    (dq_out, dk_own_out, dv_own_out, dk_oth_out, dv_oth_out, dgq_out, dgk_out,
     dk_own, dv_own, dk_oth, dv_oth, dq_acc) = rest[-12:]
    i = pl.program_id(0)
    bq = q.shape[0]
    is_prompt = i * bq < own_p

    @pl.when(i == 0)
    def _():
        dk_own[...] = jnp.zeros_like(dk_own)
        dv_own[...] = jnp.zeros_like(dv_own)
        dk_oth[...] = jnp.zeros_like(dk_oth)
        dv_oth[...] = jnp.zeros_like(dv_oth)

    @pl.when(i == 0)
    def _():
        dgq_out[...] = jnp.zeros_like(dgq_out)
        dgk_out[...] = jnp.zeros_like(dgk_out)

    heads = [slice(g * HEAD_DIM, (g + 1) * HEAD_DIM) for g in range(GROUP)]
    q2 = jnp.concatenate([q[:, c] for c in heads], axis=0)
    do2 = jnp.concatenate([do[:, c] for c in heads], axis=0)
    lev = jnp.concatenate([level[0, g : g + 1, :] for g in range(GROUP)], axis=1)
    drows = []
    for c in heads:
        both = jnp.sum(do[:, c].astype(F32) * o[:, c].astype(F32), axis=-1, keepdims=True)
        drows.append(jnp.broadcast_to(both, (bq, HEAD_DIM)).T[0:1, :])
    drow = jnp.concatenate(drows, axis=1)

    def step(k, v, ok, dk, dv, rows):
        s = dot_t(k, q2)
        p = jnp.exp2(s - lev)
        if ok is not None:
            p = jnp.where(ok, p, 0.0)
        dp = dot_t(v, do2)
        ds = (p * (dp - drow)).astype(BF)
        dv[rows, :] += dot(p.astype(BF), do2)
        dk[rows, :] += dot(ds, q2)
        return t_dot(k, ds)

    def twice(row):
        return jnp.concatenate([row] * GROUP, axis=1)

    qrow = twice(qpos[...])
    dq = None
    for at in range(0, own_p, chunk):
        rows = slice(at, at + chunk)
        ok = kpos[rows, :] <= qrow
        part = step(k_own[rows, :], v_own[rows, :], ok, dk_own, dv_own, rows)
        dq = part if dq is None else dq + part
    dq_acc[...] = dq
    if oth // chunk <= 4:
        for at in range(0, oth, chunk):
            rows = slice(at, at + chunk)
            ok = kpos[own_p + at : own_p + at + chunk, :] <= qrow
            dq_acc[...] += step(k_oth[rows, :], v_oth[rows, :], ok, dk_oth, dv_oth, rows)
    else:

        @pl.loop(0, oth // chunk)
        def _(j):
            rows = pl.ds(pl.multiple_of(j * chunk, chunk), chunk)
            ok = kpos[pl.ds(pl.multiple_of(own_p + j * chunk, chunk), chunk), :] <= qrow
            dq_acc[...] += step(k_oth[rows, :], v_oth[rows, :], ok, dk_oth, dv_oth, rows)

    @pl.when(jnp.logical_not(is_prompt))
    def _():
        code, lowest = twice(cqc[0:1, :]), twice(cqc[1:2, :])
        rows = slice(own_p, k_own.shape[0])
        ok = (ckc[...] <= code) & (ckc[...] >= lowest)
        dq_acc[...] += step(k_own[rows, :], v_own[rows, :], ok, dk_own, dv_own, rows)

    scale = HEAD_DIM ** (-0.5)
    gain_sum = jnp.zeros((8, HEAD_DIM), F32)
    for g, c in enumerate(heads):
        grad = dq_acc[:, g * bq : (g + 1) * bq].T * scale
        raw, rows = head_norm_rot_back(
            qraw[:, c].astype(F32), gq[...], cos_q[...], sin_q[...], grad
        )
        dq_out[:, c] = raw.astype(BF)
        gain_sum += jnp.sum(rows.reshape(bq // 8, 8, HEAD_DIM), axis=0)
    dgq_out[...] += gain_sum

    @pl.when(i == pl.num_programs(0) - 1)
    def _():
        for total, raw_in, cos, sin, out in (
            (dk_own, kraw_own, cos_o, sin_o, dk_own_out),
            (dk_oth, kraw_oth, cos_t, sin_t, dk_oth_out),
        ):
            n = total.shape[0]
            part = 256

            def finish(rows, total=total, raw_in=raw_in, cos=cos, sin=sin, out=out):
                raw, gain_rows = head_norm_rot_back(
                    raw_in[rows, :].astype(F32),
                    gk[...],
                    cos[rows, :],
                    sin[rows, :],
                    total[rows, :] * (1.0 / LOG2E),
                )
                out[rows, :] = raw.astype(BF)
                dgk_out[...] += jnp.sum(gain_rows.reshape(part // 8, 8, HEAD_DIM), axis=0)

            @pl.loop(0, n // part)
            def _(j):
                finish(pl.ds(pl.multiple_of(j * part, part), part))

        dv_own_out[...] = dv_own[...].astype(BF)
        dv_oth_out[...] = dv_oth[...].astype(BF)


def attend_back(
    head, filled, waits, q, qraw, do, o, level, own, oth, tabs, gq, gk, pos, own_p, bq=256
):
    rows = q.shape[0]
    n_oth = oth[0].shape[0]
    keys = own_p + n_oth
    chunk = min(512, own_p)
    wide = pl.BlockSpec((bq, GROUP * HEAD_DIM), lambda i: (i, head))
    tab = pl.BlockSpec((bq, HEAD_DIM), lambda i: (i, 0))
    head_col = lambda n: pl.BlockSpec((n, HEAD_DIM), lambda i: (0, head))
    cont_block = lambda i: (0, jnp.maximum(i - own_p // bq, 0))
    one = whole((1, HEAD_DIM))
    full = lambda n: whole((n, HEAD_DIM))
    cos_own, sin_own, cos_oth, sin_oth = tabs
    ins = [
        q, qraw, do, o, level, cos_own, sin_own, gq, gk,
        own[0], own[1], own[2], cos_own, sin_own,
        oth[0], oth[1], oth[2], cos_oth, sin_oth,
        pos["q_row"], pos["k_col"], pos["cq_row"], pos["ck_col"],
    ]
    specs = [
        wide, wide, wide, wide,
        pl.BlockSpec((1, GROUP, bq), lambda i: (head, 0, i)),
        tab, tab, one, one,
        head_col(rows), head_col(rows), head_col(rows), full(rows), full(rows),
        head_col(n_oth), head_col(n_oth), head_col(n_oth), full(n_oth), full(n_oth),
        pl.BlockSpec((1, bq), lambda i: (0, i)),
        whole((keys, 1)),
        pl.BlockSpec((2, bq), cont_block),
        whole((rows - own_p, 1)),
    ]
    anywhere = pl.BlockSpec(memory_space=pl.ANY)
    aliases = {len(ins) + n: n for n in range(len(filled))}
    extra = list(filled) + list(waits)
    return pl.pallas_call(
        functools.partial(attend_back_kernel, own_p, n_oth, chunk),
        out_shape=[
            jax.ShapeDtypeStruct((rows, QW), BF),
            jax.ShapeDtypeStruct((rows, KW), BF),
            jax.ShapeDtypeStruct((rows, KW), BF),
            jax.ShapeDtypeStruct((n_oth, KW), BF),
            jax.ShapeDtypeStruct((n_oth, KW), BF),
            jax.ShapeDtypeStruct((8, HEAD_DIM), F32),
            jax.ShapeDtypeStruct((8, HEAD_DIM), F32),
        ],
        grid=(rows // bq,),
        in_specs=specs + [anywhere] * len(extra),
        out_specs=[
            wide, head_col(rows), head_col(rows), head_col(n_oth), head_col(n_oth),
            whole((8, HEAD_DIM)), whole((8, HEAD_DIM)),
        ],
        scratch_shapes=[
            pltpu.VMEM((rows, HEAD_DIM), F32),
            pltpu.VMEM((rows, HEAD_DIM), F32),
            pltpu.VMEM((n_oth, HEAD_DIM), F32),
            pltpu.VMEM((n_oth, HEAD_DIM), F32),
            pltpu.VMEM((HEAD_DIM, GROUP * bq), F32),
        ],
        input_output_aliases=aliases,
        compiler_params=params(),
        cost_estimate=SMALL,
    )(*ins, *extra)


def feed_kernel(x, part, got, dy, g2, wg, wu, wd, *rest):
    h1_out, b_out, hid_out, dg_out, du_out, y_out, db_out = rest[-7:]
    hv = x[...].astype(F32) + (part[...].astype(F32) + got[...].astype(F32))
    h1_out[...] = hv
    b = hv * lax.rsqrt(jnp.mean(hv * hv, axis=-1, keepdims=True) + EPS_NORM) * g2[...]
    b = b.astype(BF)
    b_out[...] = b
    dyv = dy[...]
    step = 512
    y = db = None
    for at in range(0, FW, step):
        cols = slice(at, at + step)
        gate = dot(b, wg[:, cols])
        up = dot(b, wu[:, cols])
        dhid = dot_t(dyv, wd[cols, :])
        sig = 1.0 / (1.0 + jnp.exp(-gate))
        act = gate * sig
        hid = (act * up).astype(BF)
        dgate = (dhid * up * (sig * (1.0 + gate * (1.0 - sig)))).astype(BF)
        dup = (dhid * act).astype(BF)
        hid_out[:, cols] = hid
        dg_out[:, cols] = dgate
        du_out[:, cols] = dup
        y_part = dot(hid, wd[cols, :])
        db_part = dot_t(dgate, wg[:, cols]) + dot_t(dup, wu[:, cols])
        y = y_part if y is None else y + y_part
        db = db_part if db is None else db + db_part
    y_out[...] = y.astype(BF)
    db_out[...] = db.astype(BF)


def feed(filled, base, total, x, part, got, dy, g2, wg, wu, wd):
    rows = part.shape[0]
    bm = 256
    base //= bm
    row = lambda width: pl.BlockSpec((bm, width), lambda i: (i, 0))
    later = lambda width: pl.BlockSpec((bm, width), lambda i: (base + i, 0))
    anywhere = pl.BlockSpec(memory_space=pl.ANY)
    return pl.pallas_call(
        feed_kernel,
        out_shape=[
            jax.ShapeDtypeStruct((total, D), F32),
            jax.ShapeDtypeStruct((total, D), BF),
            jax.ShapeDtypeStruct((total, FW), BF),
            jax.ShapeDtypeStruct((total, FW), BF),
            jax.ShapeDtypeStruct((total, FW), BF),
            jax.ShapeDtypeStruct((rows, D), BF),
            jax.ShapeDtypeStruct((rows, D), BF),
        ],
        grid=(rows // bm,),
        in_specs=[
            later(D), row(D), row(D), later(D), whole((1, D)), whole((D, FW)), whole((D, FW)), whole((FW, D)),
        ]
        + [anywhere] * len(filled),
        out_specs=[later(D), later(D), later(FW), later(FW), later(FW), row(D), row(D)],
        input_output_aliases={8 + n: n for n in range(len(filled))},
        compiler_params=params(),
        cost_estimate=SMALL,
    )(x, part, got, dy, g2, wg, wu, wd, *filled)


def back_kernel(h1, dy, mine, got, g2, wo, *rest):
    dh_out, da_out, do_out, dg_out = rest[-4:]
    hv = h1[...]
    db = mine[...].astype(F32) + got[...].astype(F32)
    r = lax.rsqrt(jnp.mean(hv * hv, axis=-1, keepdims=True) + EPS_NORM)
    xh = hv * r
    dg = db * g2[...]
    dh = dy[...].astype(F32) + r * (dg - xh * jnp.mean(dg * xh, axis=-1, keepdims=True))
    dh_out[...] = dh
    da = dh.astype(BF)
    da_out[...] = da
    do_out[...] = dot_t(da, wo[...]).astype(BF)
    gain = jnp.sum((db * xh).reshape(hv.shape[0] // 8, 8, D), axis=0)

    @pl.when(pl.program_id(0) == 0)
    def _():
        dg_out[...] = jnp.zeros_like(dg_out)

    dg_out[...] += gain


def back_norm(filled, base, h1, dy, mine, got, g2, wo):
    rows, total = mine.shape[0], h1.shape[0]
    bm = 256
    base //= bm
    row = lambda width: pl.BlockSpec((bm, width), lambda i: (i, 0))
    later = lambda width: pl.BlockSpec((bm, width), lambda i: (base + i, 0))
    anywhere = pl.BlockSpec(memory_space=pl.ANY)
    return pl.pallas_call(
        back_kernel,
        out_shape=[
            jax.ShapeDtypeStruct((total, D), F32),
            jax.ShapeDtypeStruct((total, D), BF),
            jax.ShapeDtypeStruct((total, QW), BF),
            jax.ShapeDtypeStruct((8, D), F32),
        ],
        grid=(rows // bm,),
        in_specs=[later(D), later(D), row(D), row(D), whole((1, D)), whole((QW, D))]
        + [anywhere] * len(filled),
        out_specs=[later(D), later(D), later(QW), whole((8, D))],
        input_output_aliases={6 + n: n for n in range(len(filled))},
        compiler_params=params(),
        cost_estimate=SMALL,
    )(h1, dy, mine, got, g2, wo, *filled)


def layout():
    q_width = HEADS * HEAD_DIM
    kv_width = KV_HEADS * HEAD_DIM
    return [
        (D,),
        (D, q_width),
        (D, kv_width),
        (D, kv_width),
        (HEAD_DIM,),
        (HEAD_DIM,),
        (q_width, D),
        (D,),
        (D, FF),
        (D, FF),
        (FF, D),
    ]


LANES = 128
SHARD = 491592
FLAT_AT = {"g1": 0, "wq": 8, "wk": 16392, "wv": 24584, "gqk": 32776, "wo": 32778,
           "g2": 49162, "wg": 49170, "wu": 73746, "wd": 98322}
PER_ROW = {"wq": 16, "wk": 8, "wv": 8, "wo": 8, "wg": 24, "wu": 24, "wd": 8}


def matrix_kernel(per, split, place, main, extra, out, wide):
    count = main.shape[0]
    wide[:count, :] = main[...].astype(F32)
    wide[count:, :] = extra[...].astype(F32)
    rows = out.shape[0]
    first = place[1]
    if split:
        first = first + place[0] * (out.shape[1] // LANES)
    for at in range(out.shape[1] // LANES):
        cols = slice(at * LANES, (at + 1) * LANES)
        out[:, cols] = wide[pl.ds(first + at, rows, stride=per), :].astype(BF)


def matrix(lanes, name, split, rows, step, core):
    per = PER_ROW[name]
    count = step * per
    at = FLAT_AT[name]
    base = at // count
    width = per * LANES // (CORES if split else 1)
    blocks = (rows if split else rows // CORES) // step
    place = jnp.stack([core, jnp.full_like(core, at - base * count)]).astype(jnp.int32)

    def block(i, place):
        return base + i + (0 if split else place[0] * blocks)

    return pl.pallas_call(
        functools.partial(matrix_kernel, per, split),
        out_shape=jax.ShapeDtypeStruct((blocks * step, width), BF),
        grid_spec=pltpu.PrefetchScalarGridSpec(
            num_scalar_prefetch=1,
            grid=(blocks,),
            in_specs=[
                pl.BlockSpec((count, LANES), lambda i, place: (block(i, place), 0)),
                pl.BlockSpec(
                    (32, LANES), lambda i, place: ((block(i, place) + 1) * (count // 32), 0)
                ),
            ],
            out_specs=pl.BlockSpec((step, width), lambda i, place: (i, 0)),
            scratch_shapes=[pltpu.VMEM((count + 32, LANES), F32)],
        ),
        compiler_params=params(),
        cost_estimate=SMALL,
    )(place, lanes, lanes)


def gain_vectors(flat_vec):
    take = lambda name, skip, size: lax.slice(
        flat_vec, (FLAT_AT[name] * LANES + skip,), (FLAT_AT[name] * LANES + skip + size,)
    )
    gains = take("g1", 0, D), take("g2", 0, D), take("gqk", 0, LANES), take("gqk", LANES, LANES)
    return [gain.astype(F32).reshape(1, -1) for gain in gains]


def plain_grads(
    pick, a, a_far, b, o, hid, dgate, dup, dy, da_out, dq, dk, dv, dg1, dgq, dgk, dg2
):
    a_all = jnp.concatenate([a, a_far])
    grads = [
        dg1,
        t_dot(a, dq),
        t_dot(a_all, jnp.concatenate(dk)),
        t_dot(a_all, jnp.concatenate(dv)),
        jnp.sum(dgq, axis=0),
        jnp.sum(dgk, axis=0),
        t_dot(o, da_out),
        0.5 * dg2,
        t_dot(b, dgate),
        t_dot(b, dup),
        t_dot(hid, dy),
    ]
    flat = []
    for number, (grad, shape) in enumerate(zip(grads, layout())):
        if len(shape) == 2:
            axis = 0 if number in (6, 10) else 1
            blank = jnp.zeros_like(grad)
            grad = jnp.concatenate([pick(grad, blank), pick(blank, grad)], axis=axis)
        flat.append(grad.reshape(-1).astype(F32))
    return lax.psum_scatter(
        jnp.concatenate(flat), ("dp", "seq"), scatter_dimension=0, tiled=True
    )


X_FIRST = ("wq", "wg", "wd")
FEED_PARTS = {
    (1, 0): [("wo", 0, 704)],
    (1, 1): [("wo", 704, 1664)],
    (1, 2): [("wo", 1664, 2048), ("wg", 0, 192)],
    (1, 3): [("wg", 192, 512)],
    (2, 0): [("wg", 512, 832)],
    (2, 1): [("wg", 832, 1024), ("wu", 0, 128)],
    (2, 2): [("wu", 128, 448)],
    (2, 3): [("wu", 448, 768)],
    (3, 0): [("wu", 768, 1024), ("wd", 0, 192)],
    (3, 1): [("wd", 192, 1152)],
    (3, 2): [("wd", 1152, 2112)],
    (3, 3): [("wd", 2112, 3072)],
}
HEAD_PARTS = {0: ("wq", 0, 512), 1: ("wq", 512, 1024), 2: ("wk", 0, 1024), 3: ("wv", 0, 1024)}
TAIL = 288


def plane_pairs(distance, wanted=lambda dp, seq: True):
    pairs = []
    for dp in range(4):
        for seq in range(8):
            to = dp ^ distance
            if wanted(to, seq):
                pairs.append((dp * 8 + seq, to * 8 + seq))
    return pairs


def swap_dp(block, distance):
    return lax.ppermute(block, "dp", [(i, i ^ distance) for i in range(4)])


def cut(block, index, axis=1):
    width = block.shape[axis] // 2
    return lax.dynamic_slice_in_dim(block, index * width, width, axis)


def plane_order(name):
    dp = lax.axis_index("dp")
    order = ((dp % 2, 1), (dp // 2, 2))
    return order if name in X_FIRST else order[::-1]


def plane_step(grad, name, step):
    mine, distance = plane_order(name)[step]
    return cut(grad, mine), swap_dp(cut(grad, 1 - mine), distance)


def kept(*stages):
    return [stage[0] for stage in stages]


def added(stage):
    return (stage[0].astype(F32) + stage[1].astype(F32)).astype(BF)


def line_start(parts):
    low = lax.axis_index("seq") // 2 % 2
    parts = parts.reshape((2, 2) + parts.shape[1:])
    keep = lax.dynamic_index_in_dim(parts, low, 1, keepdims=False)
    send = lax.dynamic_index_in_dim(parts, 1 - low, 1, keepdims=False)
    return keep, xor_seq(send, 2)


def line_next(stage):
    high = lax.axis_index("seq") // 4
    parts = added(stage)
    keep = lax.dynamic_index_in_dim(parts, high, 0, keepdims=False)
    send = lax.dynamic_index_in_dim(parts, 1 - high, 0, keepdims=False)
    return keep, xor_seq(send, 4)


def stack_rows(grad, low, high):
    return [grad[low:high, at : at + LANES] for at in range(0, grad.shape[1], LANES)]


def feed_line(sums):
    spare = jnp.zeros((256, LANES), BF)
    per_line = []
    for z in range(4):
        blocks = [spare] if z == 0 else []
        for d in (1, 2, 3):
            for name, low, high in FEED_PARTS[d, z]:
                blocks += stack_rows(sums[name], low, high)
        per_line.append(jnp.concatenate(blocks))
    return line_start(jnp.stack(per_line))


ROWS = 3872
PART = 176
BEFORE = TAIL * 8


def spread(who, other, core, dp, name, at, rows, into, to):
    per = PER_ROW[name] // 8
    for source, side in ((who, core), (other, 1 - core)):
        for place in range(4):
            chip = (place % 2) * 2 + place // 2 if name in X_FIRST else place
            for col in range(per):
                first = to + side * (4 * per) + place * per + col
                block = source[chip ^ dp, at + col * rows : at + (col + 1) * rows, :]
                into[pl.ds(first, rows, stride=8 * per), :] = block.astype(F32)


def feed_flat_kernel(info, who, other, out):
    core, spot = info[0], info[1]

    @pl.when((spot < 4) | (spot == 4))
    def _():
        out[...] = jnp.zeros_like(out)

    for (d, z), blocks in FEED_PARTS.items():

        @pl.when(spot == d * 4 + z)
        def _(d=d, z=z, blocks=blocks):
            at, to = (256, 2048) if (d, z) == (1, 0) else (0, 0)
            for name, low, high in blocks:
                rows = high - low
                spread(who, other, core, 0, name, at, rows, out, to)
                at += rows * PER_ROW[name] // 8
                to += rows * PER_ROW[name]


def main_row(d, z):
    if (d, z) == (1, 0):
        return FLAT_AT["gqk"]
    name, low, _ = HEAD_PARTS[z] if d == 0 else FEED_PARTS[d, z][0]
    return FLAT_AT[name] + low * PER_ROW[name]


STARTS = [
    (8 * d + 2 * z + c) * SHARD // LANES - (main_row(d, z) - BEFORE)
    for d in range(4)
    for z in range(4)
    for c in range(2)
]
WIDE = max(BEFORE + 8192, (max(STARTS) + ROWS + 16) // 8 * 8)


def adam(grad, master, moment1, moment2):
    moment1_new = BETA_ONE * moment1 + (1.0 - BETA_ONE) * grad
    moment2_new = BETA_TWO * moment2 + (1.0 - BETA_TWO) * grad * grad
    update = moment1_new / CORRECT_ONE / (jnp.sqrt(moment2_new / CORRECT_TWO) + ADAM_EPS)
    return moment1_new, master - LEARN_RATE * (update + DECAY_RATE * master)


def finish_kernel(
    info, who, other, flat, before, gains, master, moment1, moment2,
    grad_out, moment1_out, master_out, block_out, wide, work,
):
    core, spot, start, skip, ahead, rest = [info[i] for i in range(6)]

    def put_before(name, dp):
        spread(who, other, core, dp, name, 1024, TAIL * 8 // PER_ROW[name], wide, 0)

    @pl.when(spot == 0)
    def _():
        wide[BEFORE - 8 : BEFORE, :] = gains[0:8, :]

    @pl.when((spot == 1) | (spot == 2))
    def _():
        put_before("wq", 0)

    @pl.when(spot == 3)
    def _():
        put_before("wk", 0)

    @pl.when(spot == 4)
    def _():
        put_before("wv", 1)
        wide[BEFORE : BEFORE + 2, :] = gains[8:10, :]
        wide[BEFORE + 2 : BEFORE + 2 + 5632, :] = flat[2048:, :]

    @pl.when(spot < 2)
    def _():
        spread(who, other, core, 0, "wq", 0, 512, wide, BEFORE)

    @pl.when((spot == 2) | (spot == 3))
    def _():
        spread(who, other, core, 0, "wk", 0, 1024, wide, BEFORE)

    @pl.when(spot > 4)
    def _():
        wide[BEFORE - 16 : BEFORE, :] = before[...]

    @pl.when(spot == 6)
    def _():
        wide[BEFORE : BEFORE + 3072, :] = flat[:3072, :]
        wide[BEFORE + 3072 : BEFORE + 3080, :] = gains[10:18, :]
        wide[BEFORE + 3080 : BEFORE + 7688, :] = flat[3072:, :]

    @pl.when((spot == 5) | (spot > 6))
    def _():
        wide[BEFORE : BEFORE + 7680, :] = flat[...]

    col = lax.broadcasted_iota(jnp.int32, (PART, LANES), 1)
    row = lax.broadcasted_iota(jnp.int32, (PART, LANES), 0)
    work[0:8, :] = jnp.zeros((8, LANES), F32)
    work[ROWS + 8 :, :] = jnp.zeros((8, LANES), F32)
    turn = lax.rem(LANES - skip, LANES)

    @pl.loop(0, ROWS // PART)
    def _(j):
        at = pl.multiple_of(j * PART, 8)
        here = pl.ds(at, PART)
        now = pltpu.roll(wide[pl.ds(start + at, PART), :], turn, 1)
        after_it = pltpu.roll(wide[pl.ds(start + at + 1, PART), :], turn, 1)
        grad = jnp.where(col < LANES - skip, now, after_it)
        moment1_new, master_new = adam(grad, master[here, :], moment1[here, :], moment2[here, :])
        grad_out[here, :] = grad
        moment1_out[here, :] = moment1_new
        master_out[here, :] = master_new
        inside = (at + row) * LANES + col < SHARD
        work[pl.ds(at + 8, PART), :] = jnp.where(inside, master_new, 0.0)

    @pl.loop(0, ROWS // PART)
    def _(j):
        at = pl.multiple_of(j * PART, 16)
        now = pltpu.roll(work[pl.ds(7 - ahead + at, PART), :], rest, 1)
        after_it = pltpu.roll(work[pl.ds(8 - ahead + at, PART), :], rest, 1)
        block_out[pl.ds(at, PART), :] = jnp.where(col < rest, now, after_it).astype(BF)


def local(kernel, shapes, scratch, info, *arrays):
    vmem = pl.BlockSpec(memory_space=pltpu.VMEM)
    return pl.pallas_call(
        kernel,
        out_shape=shapes,
        in_specs=[pl.BlockSpec(memory_space=pltpu.SMEM)] + [vmem] * len(arrays),
        out_specs=jax.tree.map(lambda _: vmem, shapes),
        scratch_shapes=scratch,
        compiler_params=params(),
        cost_estimate=SMALL,
    )(jnp.stack(info).astype(jnp.int32), *arrays)


def fast_grads(core, feed_stage, head_q, head_kv, gains, states, da, to_home):
    dp = lax.axis_index("dp")
    rank = lax.axis_index("seq")
    line = rank // 2
    spot = dp * 4 + line
    gains = jnp.concatenate(gains).reshape(1, -1, LANES)
    gains = jnp.broadcast_to(gains, (32,) + gains.shape[1:])
    gains = lax.all_to_all(gains, ("dp", "seq"), 0, 0, tiled=True)
    feed_part = added(feed_stage).reshape(3, 960, LANES)
    feed_part = after(feed_part, kept(head_q, head_kv))

    feed_got = jnp.concatenate([feed_part[:1], feed_part])
    feed_got = lax.all_to_all(feed_got, "dp", 0, 0, tiled=True)
    head_q, head_kv = added(head_q), added(head_kv)
    head_q, head_kv, da = after((head_q, head_kv, da))
    head_stage = line_start(
        jnp.stack(
            [
                jnp.concatenate(stack_rows(head_q, 0, 512)),
                jnp.concatenate(stack_rows(head_q, 512, 1024)),
                head_kv[:1024],
                head_kv[1024:],
            ]
        )
    )
    feed_flat = local(
        feed_flat_kernel,
        jax.ShapeDtypeStruct((7680, LANES), F32),
        [],
        (core, spot),
        feed_got,
        xor_seq(feed_got, 1),
    )
    chain = [(8 * d + s, 8 * d + s + 2) for d in range(4) for s in range(8) if 8 * d + s < 30]
    before = lax.ppermute(feed_flat[-16:], ("dp", "seq"), chain)
    head_stage, gains, before = after((head_stage, gains, before))
    head_part = added(line_next(head_stage))
    tail = jnp.where(
        line < 2,
        jnp.concatenate([head_part[512 - TAIL // 2 : 512], head_part[1024 - TAIL // 2 :]]),
        head_part[1024 - TAIL :],
    )
    ring = [(8 * d + s, 8 * d + (s + 2) % 8) for d in range(4) for s in range(8)]
    tail = lax.ppermute(tail, ("dp", "seq"), ring)
    tail, da = after((tail, da))
    dx_rows = to_home(da)
    head_all = after(jnp.concatenate([head_part, tail]), dx_rows[0])
    head_got = [head_all]
    for distance in (1, 2, 3):
        pairs = plane_pairs(distance, lambda d, s: d == 0 or (d == 1 and s < 2))
        head_got.append(lax.ppermute(head_all, ("dp", "seq"), pairs))
    gains = jnp.sum(gains, axis=0)
    head_got = jnp.stack(head_got)
    head_far = xor_seq(head_got, 1)

    index = spot * 2 + core
    start = jnp.asarray(STARTS, jnp.int32)[index]
    info = (core, spot, start, index * (SHARD % LANES) % LANES, rank * 72 // LANES, rank * 72 % LANES)
    rows = jax.ShapeDtypeStruct((ROWS, LANES), F32)
    results = local(
        finish_kernel,
        [rows, rows, rows, jax.ShapeDtypeStruct((ROWS, LANES), BF)],
        [pltpu.VMEM((WIDE, LANES), F32), pltpu.VMEM((ROWS + 16, LANES), F32)],
        info, head_got, head_far, feed_flat, before, gains, *states,
    )
    results, dx_rows = after((results, dx_rows))
    return *results, dx_rows


def gather_weights(block):
    blocks = lax.all_gather(block, "seq", axis=0)
    body, ends = blocks[:, :3840], blocks[:, 3840:3848]
    heads = body[1:, :8] + ends[:-1]
    heads = jnp.concatenate([body[:1, :8], heads])
    rows = jnp.concatenate([heads, body[:, 8:]], axis=1).reshape(-1, LANES)
    rows = jnp.concatenate([rows, ends[-1]])
    return rows.reshape(-1)[: 8 * SHARD]


def norm_back(x, gain, grad):
    r = lax.rsqrt(jnp.mean(x * x, axis=-1, keepdims=True) + EPS_NORM)
    xh = x * r
    dg = grad * gain
    return r * (dg - xh * jnp.mean(dg * xh, axis=-1, keepdims=True))


def into_kernel(count, *refs):
    grads, weights = refs[:count], refs[count : 2 * count]
    x, out, gain_out = refs[2 * count :]
    total = None
    for grad, weight in zip(grads, weights):
        part = dot_t(grad[...], weight[...])
        total = part if total is None else total + part
    out[...] = total.astype(BF)
    xv = x[...].astype(F32)
    xh = xv * lax.rsqrt(jnp.mean(xv * xv, axis=-1, keepdims=True) + EPS_NORM)

    @pl.when(pl.program_id(0) == 0)
    def _():
        gain_out[...] = jnp.zeros_like(gain_out)

    gain_out[...] += jnp.sum((total * xh).reshape(xv.shape[0] // 8, 8, D), axis=0)


def into_input(grads, weights, x):
    rows = x.shape[0]
    bm = 256
    row = lambda width: pl.BlockSpec((bm, width), lambda i: (i, 0))
    return pl.pallas_call(
        functools.partial(into_kernel, len(grads)),
        out_shape=[jax.ShapeDtypeStruct((rows, D), BF), jax.ShapeDtypeStruct((8, D), F32)],
        grid=(rows // bm,),
        in_specs=[row(grad.shape[1]) for grad in grads]
        + [whole(weight.shape) for weight in weights]
        + [row(D)],
        out_specs=[row(D), whole((8, D))],
        compiler_params=params(),
        cost_estimate=SMALL,
    )(*grads, *weights, x)


def tables(positions):
    half_dim = HEAD_DIM // 2
    frequency = ROPE_BASE ** (-jnp.arange(half_dim, dtype=F32) * 2.0 / HEAD_DIM)
    angles = positions.astype(F32)[:, None] * frequency[None, :]
    cosine, sine = jnp.cos(angles), jnp.sin(angles)
    return jnp.concatenate([cosine, cosine], 1), jnp.concatenate([-sine, sine], 1)


def shards(x_prompt, x_cont, dy_prompt, dy_cont, prompt_pos, weights, master, moment1, moment2):
    count = lax.axis_size("seq")
    rank = lax.axis_index("seq")
    half = count // 2
    side = rank // half
    core = rank % CORES
    chips = half // CORES
    p = x_prompt.shape[1]
    c = x_cont.shape[1]
    prompt_len = p * count
    own_p = 4 * p
    first = core == 0

    def pick(lo, hi):
        return jnp.where(first, lo, hi)

    def share(mine, got):
        return pick(mine, got), pick(got, mine)

    def far_rows(block):
        rows = block[None]
        mask = 2
        while mask < half:
            rows = jnp.concatenate([rows, xor_seq(rows, mask)])
            mask *= 2
        return rows[1:]

    def sides(prompt, cont):
        rows = jnp.concatenate([prompt, cont], axis=1)
        own = lax.dynamic_index_in_dim(rows, side, 0, keepdims=False)
        other = lax.dynamic_index_in_dim(rows, 1 - side, 0, keepdims=False)
        return own, other

    def join(own, recv, own_got, recv_got):
        lo, hi = share(own, own_got)
        lo2, hi2 = share(recv, recv_got)
        rows_p = [lo[:p], lo2[:p], hi[:p], hi2[:p]]
        rows_c = [lo[p:], lo2[p:], hi[p:], hi2[p:]]
        return jnp.concatenate(rows_p + rows_c, axis=0)

    x_own, x_other = sides(x_prompt, x_cont)
    x_recv = xor_seq(x_other, half)
    far_one = far_rows(x_own[:p])
    x_own_got = xor_seq(x_own, 1)

    lanes = weights.reshape(-1, LANES)
    g1, g2, gq, gk = gain_vectors(weights)
    w_q = matrix(lanes, "wq", True, D, 128, core)
    w_k = matrix(lanes, "wk", True, D, 256, core)
    w_v = matrix(lanes, "wv", True, D, 256, core)
    x_recv = after(x_recv, w_q, w_k, w_v)
    far_two = far_rows(x_recv[:p])
    x_recv_got = xor_seq(x_recv, 1)
    far_one = after(far_one, x_recv)
    far_one_got = xor_seq(far_one, 1)
    lanes = after(lanes, x_recv)
    w_g = matrix(lanes, "wg", True, D, 128, core)
    w_u = matrix(lanes, "wu", True, D, 128, core)
    x_recv_got = after(x_recv_got, w_g, w_u)
    x = join(x_own, x_recv, x_own_got, x_recv_got)

    chip_ids = (rank - core) ^ (CORES * jnp.arange(chips)[:, None, None])
    ids = (chip_ids + jnp.arange(CORES)[None, :, None]) ^ (half * jnp.arange(2)[None, None, :])
    own_group = lax.dynamic_index_in_dim(prompt_pos, side, 0, keepdims=False)
    key_pos = jnp.take(own_group.reshape(count, p), ids.reshape(-1), axis=0).reshape(-1)
    quarter = c // 2
    steps = jnp.arange(quarter, dtype=jnp.int32)
    own_half = [
        prompt_len + jnp.concatenate([k * quarter + steps, (3 - k) * quarter + steps])
        for k in range(CORES)
    ]
    cont_pos = jnp.concatenate([own_half[0], own_half[0], own_half[1], own_half[1]])
    seg = jnp.tile(jnp.repeat(jnp.arange(2, dtype=jnp.int32), c), CORES)
    big = 2 * prompt_len + 4 * c
    cont_code = seg * big + cont_pos
    query_pos = jnp.concatenate([key_pos[:own_p], cont_pos])
    cont_q = jnp.stack([cont_code, seg * big])
    pos = {
        "q_col": query_pos[:, None], "q_row": query_pos[None, :],
        "k_col": key_pos[:, None], "k_row": key_pos[None, :],
        "cq_col": cont_q.T, "cq_row": cont_q,
        "ck_col": cont_code[:, None], "ck_row": cont_code[None, :],
    }
    cos_own, sin_own = tables(query_pos)
    cos_far, sin_far = tables(key_pos[own_p:])

    a, q, qraw, k_own, kraw_own, v_own = project(x, g1, cos_own, sin_own, w_q, w_k, w_v, gq, gk, True)
    far_two = after(far_two, a)
    far_two_got = xor_seq(far_two, 1)
    lanes = after(lanes, a)
    w_d = matrix(lanes, "wd", False, FF, 384, core)
    w_o = matrix(lanes, "wo", False, HEADS * HEAD_DIM, 256, core)
    far_two_got = after(far_two_got, w_d, w_o)
    dy_own, dy_other = after(sides(dy_prompt, dy_cont), far_two)
    dy_recv = xor_seq(dy_other, half)
    dy_own_got = xor_seq(dy_own, 1)
    lo, hi = share(far_one, far_one_got)
    lo2, hi2 = share(far_two, far_two_got)
    x_far = jnp.stack([lo, lo2, hi, hi2], axis=1).reshape(-1, D)
    a_far, k_far, kraw_far, v_far = project(x_far, g1, cos_far, sin_far, w_q, w_k, w_v, gq, gk, False)
    rows = x.shape[0]
    o_p, level_p = attend(q, k_own, v_own, k_far, v_far, pos, own_p, False)
    part_p = dot(o_p, w_o).astype(BF)
    part_p_got = xor_seq(part_p, 1)
    q, part_p, dy_recv = after((q, part_p, dy_recv))
    dy_recv_got = xor_seq(dy_recv, 1)
    o_c, level_c = attend(q, k_own, v_own, k_far, v_far, pos, own_p, True)
    o_c, dy_recv_got = after((o_c, dy_recv_got))
    part_c = dot(o_c, w_o).astype(BF)
    part_c_got = xor_seq(part_c, 1)
    part_p_got = after(part_p_got, part_c)
    dy = join(dy_own, dy_recv, dy_own_got, dy_recv_got)
    *filled, y_p, db_p = feed((), 0, rows, x, part_p, part_p_got, dy, g2, w_g, w_u, w_d)
    db_p_got = xor_seq(db_p, 1)
    o = jnp.concatenate([o_p, o_c])
    o_got = xor_seq(o, 1)
    part_c_got, o_got = after((part_c_got, o_got), db_p)
    *filled, y_c, db_c = feed(filled, own_p, rows, x, part_c, part_c_got, dy, g2, w_g, w_u, w_d)
    h1, b, hid, dgate, dup = filled
    db_c_got = xor_seq(db_c, 1)
    hid_got = xor_seq(hid, 1)
    level = jnp.concatenate([level_p, level_c], axis=2)
    y_part = jnp.concatenate([y_p, y_c])
    fast = count == 8 and lax.axis_size("dp") == 4
    def core_rows(rows, which):
        return jnp.concatenate(
            [
                lax.dynamic_slice_in_dim(rows, which * 2 * p, 2 * p),
                lax.dynamic_slice_in_dim(rows, own_p + which * 2 * c, 2 * c),
            ]
        )

    y_got = xor_seq(core_rows(y_part, 1 - core), 1)
    if fast:
        grad_g, grad_u = t_dot(b, dgate).astype(BF), t_dot(b, dup).astype(BF)
        grad_g, db_p_got, db_c_got = after((grad_g, db_p_got, db_c_got))
        flow = {"wg": plane_step(grad_g, "wg", 0)}
        flow["wu"] = plane_step(after(grad_u, kept(flow["wg"])), "wu", 0)
        dy_cols = cut(dy, core)
        grad_d = t_dot(hid, dy_cols).astype(BF)
        hid_got, y_got = after((hid_got, y_got), kept(flow["wg"], flow["wu"]))
        grad_d = share(grad_d, t_dot(hid_got, dy_cols).astype(BF))
        flow["wd"] = plane_step(jnp.concatenate(grad_d), "wd", 0)
        db_p_got, db_c_got = after((db_p_got, db_c_got), kept(flow["wd"]))
    y_core = core_rows(h1, core) + core_rows(y_part, core).astype(F32) + y_got.astype(F32)
    *filled, dg2_p = back_norm((), 0, h1, dy, db_p, db_p_got, g2, w_o)
    *filled, dg2_c = back_norm(filled, own_p, h1, dy, db_c, db_c_got, g2, w_o)
    dh1, da_out, d_o = filled
    dg2 = jnp.sum(dg2_p + dg2_c, axis=0)

    filled, waits = (), [y_core]
    back = []
    if fast:
        cols = cut(da_out, core)
        grad_o = share(t_dot(o, cols).astype(BF), t_dot(o_got, cols).astype(BF))
        flow["wo"] = plane_step(jnp.concatenate(grad_o), "wo", 0)
        flow["wg"], flow["wu"] = after((flow["wg"], flow["wu"]), flow["wo"][0])
        for name in ("wg", "wu"):
            flow[name] = plane_step(added(flow[name]), name, 1)
        waits += kept(*flow.values())
    for head in range(KV_HEADS_C):
        *filled, dgq, dgk = attend_back(
            head, filled, waits, q, qraw, d_o, o, level,
            (k_own, v_own, kraw_own), (k_far, v_far, kraw_far),
            (cos_own, sin_own, cos_far, sin_far), gq, gk, pos, own_p,
        )
        waits = []
        back.append((dgq, dgk))
        if head == 2:
            y_rows = after(y_rows, dgq)
            waits = [y_rows[1]]
        if fast and head == 1:
            flow = after(flow, dgq)
            flow["wg"], flow["wu"] = added(flow["wg"]), added(flow["wu"])
            for name in ("wd", "wo"):
                flow[name] = plane_step(added(flow[name]), name, 1)
            waits += [flow["wg"], flow["wu"]] + kept(flow["wd"], flow["wo"])
        if head == 1:
            y_rows = home_start(after(y_core, dgq, waits), half, p, c)
            waits.append(y_rows[0])
        if fast and head == 2:
            flow = after(flow, dgq)
            flow["wd"], flow["wo"] = added(flow["wd"]), added(flow["wo"])
            feed_stage = feed_line(flow)
            waits += kept(feed_stage)
    dq, dk_own, dv_own, dk_far, dv_far = filled
    dgq, dgk = [sum(parts) for parts in zip(*back)]
    y_prompt, y_cont = home_end(y_rows, side, p)

    if fast:
        grad_q = t_dot(a, dq).astype(BF)
        grad_q, feed_stage = after((grad_q, feed_stage))
        head_q = plane_step(grad_q, "wq", 0)
        a_all = after(jnp.concatenate([a, a_far]), kept(head_q))
        pair = [(dk_own, dk_far), (dv_own, dv_far)]
        pair = [t_dot(a_all, jnp.concatenate(part)).astype(BF) for part in pair]
        head_kv = plane_step(jnp.concatenate(pair), "wk", 0)
        feed_stage = line_next(feed_stage)
        dk_own, dk_far = after((dk_own, dk_far), kept(feed_stage, head_q, head_kv))

    da_far, gain_far = into_input((dk_far, dv_far), (w_k, w_v), x_far)
    da_far = da_far.reshape(chips - 1, CORES, 2 * p, D)
    da_own, gain_own = into_input((dq, dk_own, dv_own), (w_q, w_k, w_v), x)
    dg1 = jnp.sum(gain_far + gain_own, axis=0)
    far_keep = lax.dynamic_index_in_dim(da_far, core, 1, keepdims=False)
    far_send = lax.dynamic_index_in_dim(da_far, 1 - core, 1, keepdims=False)
    sent = jnp.concatenate([core_rows(da_own, 1 - core), far_send.reshape(-1, D)])
    got = xor_seq(sent, 1)
    if fast:
        head_q, head_kv, feed_stage = after((head_q, head_kv, feed_stage))
        head_q = plane_step(added(head_q), "wq", 1)
        head_kv = plane_step(added(head_kv), "wk", 1)
        got = after(got, kept(head_q, head_kv))
    mine = core_rows(da_own, core).astype(F32) + got[: rows // 2].astype(F32)
    far_sum = far_keep.astype(F32) + got[rows // 2 :].reshape(far_keep.shape).astype(F32)
    blocks = jnp.concatenate([mine[None, : 2 * p], far_sum])
    mask = half // 2
    while mask > 1:
        near, away = blocks[: mask // 2], blocks[mask // 2 :].astype(BF)
        if fast:
            head_q, head_kv = after((head_q, head_kv), away)
        blocks = near + xor_seq(away, mask).astype(F32)
        mask //= 2
    da = jnp.concatenate([blocks[0], mine[2 * p :]])

    def to_dx(da):
        return core_rows(dh1, core) + norm_back(core_rows(x, core).astype(F32), g1, da)

    if fast:
        gains = [dg1, jnp.sum(dgq, 0), jnp.sum(dgk, 0), 0.5 * dg2]
        states = [
            jnp.concatenate([state, jnp.zeros((ROWS * LANES - SHARD,), F32)]).reshape(ROWS, LANES)
            for state in (master, moment1, moment2)
        ]
        states = after(states, x)
        *results, block, dx_rows = fast_grads(
            core, feed_stage, head_q, head_kv, gains, states, da, lambda da: home_start(to_dx(da), half, p, c)
        )
        weights_new = gather_weights(block)
        grad_shard, moment1_new, master_new = [one.reshape(-1)[:SHARD] for one in results]
    else:
        grad_shard = plain_grads(
            pick, a, a_far, b, o, hid, dgate, dup, dy, da_out, dq,
            (dk_own, dk_far), (dv_own, dv_far), dg1, dgq, dgk, dg2,
        )
        dx_rows = home_start(to_dx(da), half, p, c)
        moment1_new, master_new = adam(grad_shard, master, moment1, moment2)
        weights_new = lax.all_gather(master_new.astype(BF), "seq", axis=0, tiled=True)
    dx_prompt, dx_cont = home_end(dx_rows, side, p)
    return (y_prompt, y_cont, dx_prompt, dx_cont, grad_shard, master_new, moment1_new, weights_new)


def solution(mesh):
    placed = (
        P("dp", "seq", None),
        P("dp", "seq", None),
        P("dp", "seq", None),
        P("dp", "seq", None),
        P("dp", None),
        P(),
        P(("dp", "seq")),
        P(("dp", "seq")),
        P(("dp", "seq")),
    )
    return jax.shard_map(
        shards,
        mesh=mesh,
        in_specs=placed,
        out_specs=(
            P("dp", "seq", None),
            P("dp", "seq", None),
            P("dp", "seq", None),
            P("dp", "seq", None),
            P(("dp", "seq")),
            P(("dp", "seq")),
            P(("dp", "seq")),
            P("dp"),
        ),
        check_vma=False,
    )
```

```python
import functools

import jax
import jax.numpy as jnp
from jax import lax
from jax.experimental import pallas as pl
from jax.experimental.pallas import tpu as pltpu
from jax.sharding import PartitionSpec as P

D = 1024
FF = 3072
HEADS = 16
KV_HEADS = 8
HEAD_DIM = 128

EPS_NORM = 1e-06
ROPE_BASE = 1000000.0
BETA_ONE = 0.9
BETA_TWO = 0.95
ADAM_EPS = 1e-08
LEARN_RATE = 0.0003
DECAY_RATE = 0.1
CORRECT_ONE = 1.0 - 2.656139888758747e-05
CORRECT_TWO = 1.0 - 0.005920529220333996

CORES = 2
Q_HEADS_C = HEADS // CORES
KV_HEADS_C = KV_HEADS // CORES
QW = Q_HEADS_C * HEAD_DIM
KW = KV_HEADS_C * HEAD_DIM
FW = FF // CORES
GROUP = HEADS // KV_HEADS
LOG2E = 1.4426950408889634
SCORE_FOLD = HEAD_DIM ** (-0.5) * LOG2E
VMEM_LIMIT = 52 * 1024 * 1024
SMALL = pl.CostEstimate(flops=1000, bytes_accessed=1000, transcendentals=0)
BF = jnp.bfloat16
F32 = jnp.float32


def dot(left, right):
    return jnp.dot(left, right, preferred_element_type=F32)


def dot_t(left, right):
    return lax.dot_general(left, right, (((1,), (1,)), ((), ())), preferred_element_type=F32)


def t_dot(left, right):
    return lax.dot_general(left, right, (((0,), (0,)), ((), ())), preferred_element_type=F32)


def turned(block):
    return block.astype(F32).T.astype(BF)


def xor_seq(block, mask):
    count = lax.axis_size("seq")
    return lax.ppermute(block, "seq", [(i, i ^ mask) for i in range(count)])


def after(values, *earlier):
    return lax.optimization_barrier((values, earlier))[0]


def home_start(rows, half, p, c):
    rows_p, rows_c = rows[: 2 * p], rows[2 * p :]
    own = jnp.concatenate([rows_p[:p], rows_c[:c]])
    away = jnp.concatenate([rows_p[p:], rows_c[c:]]).astype(BF)
    return own, xor_seq(away, half)


def home_end(both, side, p):
    own, back = both[0], both[1].astype(F32)
    zero = side == 0
    out = jnp.stack([jnp.where(zero, own, back), jnp.where(zero, back, own)])
    return out[:, :p], out[:, p:]


def params(*semantics):
    return pltpu.CompilerParams(vmem_limit_bytes=VMEM_LIMIT)


def whole(shape):
    return pl.BlockSpec(shape, lambda *ids: (0,) * len(shape))


def head_norm_rot(raw, gain, cos, sin):
    r = lax.rsqrt(jnp.mean(raw * raw, axis=-1, keepdims=True) + EPS_NORM)
    n = raw * r * gain
    return n * cos + pltpu.roll(n, HEAD_DIM // 2, 1) * sin


def head_norm_rot_back(raw, gain, cos, sin, grad):
    dn = grad * cos - pltpu.roll(grad, HEAD_DIM // 2, 1) * sin
    r = lax.rsqrt(jnp.mean(raw * raw, axis=-1, keepdims=True) + EPS_NORM)
    xh = raw * r
    gain_rows = dn * xh
    dg = dn * gain
    return r * (dg - xh * jnp.mean(dg * xh, axis=-1, keepdims=True)), gain_rows


def project_kernel(with_q, *refs):
    if with_q:
        (x, g1, cos, sin, wq, wk, wv, gq, gk, a_out, q_out, qraw_out, k_out, kraw_out, v_out) = refs
    else:
        (x, g1, cos, sin, wk, wv, gk, a_out, k_out, kraw_out, v_out) = refs
    xv = x[...].astype(F32)
    a = xv * lax.rsqrt(jnp.mean(xv * xv, axis=-1, keepdims=True) + EPS_NORM) * g1[...]
    a = a.astype(BF)
    a_out[...] = a
    cosv, sinv = cos[...], sin[...]
    kv = dot(a, wk[...])
    for head in range(KV_HEADS_C):
        cols = slice(head * HEAD_DIM, (head + 1) * HEAD_DIM)
        raw = kv[:, cols]
        kraw_out[:, cols] = raw.astype(BF)
        k_out[:, cols] = head_norm_rot(raw, gk[...], cosv, sinv).astype(BF)
    v_out[...] = dot(a, wv[...]).astype(BF)
    if with_q:
        qv = dot(a, wq[...])
        for head in range(Q_HEADS_C):
            cols = slice(head * HEAD_DIM, (head + 1) * HEAD_DIM)
            raw = qv[:, cols]
            qraw_out[:, cols] = raw.astype(BF)
            rot = head_norm_rot(raw, gq[...], cosv, sinv)
            q_out[:, cols] = (rot * SCORE_FOLD).astype(BF)


def project(x, g1, cos, sin, wq, wk, wv, gq, gk, with_q):
    rows = x.shape[0]
    bm = 256
    row = lambda width: pl.BlockSpec((bm, width), lambda i: (i, 0))
    ins = [x, g1, cos, sin] + ([wq] if with_q else []) + [wk, wv] + ([gq] if with_q else []) + [gk]
    specs = [row(D), whole((1, D)), row(HEAD_DIM), row(HEAD_DIM)]
    specs += [whole((D, QW))] if with_q else []
    specs += [whole((D, KW))] * 2
    specs += [whole((1, HEAD_DIM))] * (2 if with_q else 1)
    widths = [D] + ([QW, QW] if with_q else []) + [KW, KW, KW]
    return pl.pallas_call(
        functools.partial(project_kernel, with_q),
        out_shape=[jax.ShapeDtypeStruct((rows, w), BF) for w in widths],
        grid=(rows // bm,),
        in_specs=specs,
        out_specs=[row(w) for w in widths],
        compiler_params=params(),
        cost_estimate=SMALL,
    )(*ins)


def attend_kernel(own_p, oth, cont, q, k_own, v_own, k_oth, v_oth, qpos, kpos, cqc, ckc, o_out, l_out):
    bq = q.shape[0]

    def run(kind):
        for head in range(GROUP):
            cols = slice(head * HEAD_DIM, (head + 1) * HEAD_DIM)
            qh = q[:, cols]
            parts = [(dot_t(qh, k_own[:own_p, :]), v_own[:own_p, :])]
            if oth:
                parts.append((dot_t(qh, k_oth[...]), v_oth[...]))
            if kind == 0:
                at = 0
                masked = []
                for s, v in parts:
                    n = s.shape[1]
                    ok = kpos[:, at : at + n] <= qpos[...]
                    masked.append((jnp.where(ok, s, -1e30), v))
                    at += n
                parts = masked
            else:
                s = dot_t(qh, k_own[own_p:, :])
                code, lowest = cqc[:, 0:1], cqc[:, 1:2]
                ok = (ckc[...] <= code) & (ckc[...] >= lowest)
                parts.append((jnp.where(ok, s, -1e30), v_own[own_p:, :]))
            top = functools.reduce(
                jnp.maximum, [jnp.max(s, axis=-1, keepdims=True) for s, _ in parts]
            )
            total = jnp.zeros((bq, 1), F32)
            acc = jnp.zeros((bq, HEAD_DIM), F32)
            for s, v in parts:
                e = jnp.exp2(s - top)
                total += jnp.sum(e, axis=-1, keepdims=True)
                acc += dot(e.astype(BF), v)
            o_out[:, cols] = (acc / total).astype(BF)
            level = jnp.broadcast_to(top + jnp.log2(total), (bq, HEAD_DIM))
            l_out[0, head : head + 1, :] = level.T[0:1, :]

    run(1 if cont else 0)


def attend_wide_kernel(
    own_p, oth, cont, q, k_own, v_own, k_oth, v_oth, qpos, kpos, cqc, ckc,
    o_out, l_out, vt_own, vt_oth,
):
    bq = q.shape[0]

    @pl.when(pl.program_id(1) == 0)
    def _():
        vt_own[...] = turned(v_own[...])
        vt_oth[...] = turned(v_oth[...])

    def twice(row):
        return jnp.concatenate([row] * GROUP, axis=1)

    heads = [slice(g * HEAD_DIM, (g + 1) * HEAD_DIM) for g in range(GROUP)]
    q2 = jnp.concatenate([q[:, c] for c in heads], axis=0)
    parts = [(dot_t(k_own[:own_p, :], q2), vt_own[:, :own_p])]
    parts.append((dot_t(k_oth[...], q2), vt_oth[...]))
    if cont:
        s = dot_t(k_own[own_p:, :], q2)
        code, lowest = twice(cqc[0:1, :]), twice(cqc[1:2, :])
        ok = (ckc[...] <= code) & (ckc[...] >= lowest)
        parts.append((jnp.where(ok, s, -1e30), vt_own[:, own_p:]))
    else:
        at = 0
        for n, (s, v) in enumerate(parts):
            ok = kpos[at : at + s.shape[0], :] <= twice(qpos[...])
            parts[n] = (jnp.where(ok, s, -1e30), v)
            at += s.shape[0]
    top = functools.reduce(jnp.maximum, [jnp.max(s, axis=0, keepdims=True) for s, _ in parts])
    total = jnp.zeros((1, GROUP * bq), F32)
    acc = jnp.zeros((HEAD_DIM, GROUP * bq), F32)
    for s, v in parts:
        e = jnp.exp2(s - top)
        total += jnp.sum(e, axis=0, keepdims=True)
        acc += dot(v, e.astype(BF))
    level = top + jnp.log2(total)
    out = acc / total
    for g, c in enumerate(heads):
        rows = slice(g * bq, (g + 1) * bq)
        o_out[:, c] = out[:, rows].T.astype(BF)
        l_out[0, g : g + 1, :] = level[:, rows]


def attend(q, k_own, v_own, k_oth, v_oth, pos, own_p, cont):
    rows = q.shape[0]
    oth = k_oth.shape[0]
    keys = own_p + oth
    bq = 256 if cont else min(512, own_p)
    base = own_p // bq if cont else 0
    here = rows - own_p if cont else own_p
    head_col = lambda n: pl.BlockSpec((n, HEAD_DIM), lambda h, i: (0, h))
    if cont:
        masks = [
            pl.BlockSpec((bq, 1), lambda h, i: (base + i, 0)),
            whole((1, keys)),
            pl.BlockSpec((bq, 2), lambda h, i: (i, 0)),
            whole((1, rows - own_p)),
        ]
        names, scratch = ("q_col", "k_row", "cq_col", "ck_row"), []
    else:
        masks = [
            pl.BlockSpec((1, bq), lambda h, i: (0, i)),
            whole((keys, 1)),
            whole((2, rows - own_p)),
            whole((rows - own_p, 1)),
        ]
        names = ("q_row", "k_col", "cq_row", "ck_col")
        scratch = [pltpu.VMEM((HEAD_DIM, rows), BF), pltpu.VMEM((HEAD_DIM, oth), BF)]
    return pl.pallas_call(
        functools.partial(attend_kernel if cont else attend_wide_kernel, own_p, oth, cont),
        out_shape=[
            jax.ShapeDtypeStruct((here, QW), BF),
            jax.ShapeDtypeStruct((KV_HEADS_C, GROUP, here), F32),
        ],
        grid=(KV_HEADS_C, here // bq),
        in_specs=[
            pl.BlockSpec((bq, GROUP * HEAD_DIM), lambda h, i: (base + i, h)),
            head_col(rows),
            head_col(rows),
            head_col(oth),
            head_col(oth),
            *masks,
        ],
        out_specs=[
            pl.BlockSpec((bq, GROUP * HEAD_DIM), lambda h, i: (i, h)),
            pl.BlockSpec((1, GROUP, bq), lambda h, i: (h, 0, i)),
        ],
        scratch_shapes=scratch,
        compiler_params=params(),
        cost_estimate=SMALL,
    )(q, k_own, v_own, k_oth, v_oth, *[pos[name] for name in names])


def attend_back_kernel(
    own_p, oth, chunk,
    q, qraw, do, o, level, cos_q, sin_q, gq, gk,
    k_own, v_own, kraw_own, cos_o, sin_o, k_oth, v_oth, kraw_oth, cos_t, sin_t,
    qpos, kpos, cqc, ckc, *rest,
):
    (dq_out, dk_own_out, dv_own_out, dk_oth_out, dv_oth_out, dgq_out, dgk_out,
     dk_own, dv_own, dk_oth, dv_oth, dq_acc) = rest[-12:]
    i = pl.program_id(0)
    bq = q.shape[0]
    is_prompt = i * bq < own_p

    @pl.when(i == 0)
    def _():
        dk_own[...] = jnp.zeros_like(dk_own)
        dv_own[...] = jnp.zeros_like(dv_own)
        dk_oth[...] = jnp.zeros_like(dk_oth)
        dv_oth[...] = jnp.zeros_like(dv_oth)

    @pl.when(i == 0)
    def _():
        dgq_out[...] = jnp.zeros_like(dgq_out)
        dgk_out[...] = jnp.zeros_like(dgk_out)

    heads = [slice(g * HEAD_DIM, (g + 1) * HEAD_DIM) for g in range(GROUP)]
    q2 = jnp.concatenate([q[:, c] for c in heads], axis=0)
    do2 = jnp.concatenate([do[:, c] for c in heads], axis=0)
    lev = jnp.concatenate([level[0, g : g + 1, :] for g in range(GROUP)], axis=1)
    drows = []
    for c in heads:
        both = jnp.sum(do[:, c].astype(F32) * o[:, c].astype(F32), axis=-1, keepdims=True)
        drows.append(jnp.broadcast_to(both, (bq, HEAD_DIM)).T[0:1, :])
    drow = jnp.concatenate(drows, axis=1)

    def step(k, v, ok, dk, dv, rows):
        s = dot_t(k, q2)
        p = jnp.exp2(s - lev)
        if ok is not None:
            p = jnp.where(ok, p, 0.0)
        dp = dot_t(v, do2)
        ds = (p * (dp - drow)).astype(BF)
        dv[rows, :] += dot(p.astype(BF), do2)
        dk[rows, :] += dot(ds, q2)
        return t_dot(k, ds)

    def twice(row):
        return jnp.concatenate([row] * GROUP, axis=1)

    qrow = twice(qpos[...])
    dq = None
    for at in range(0, own_p, chunk):
        rows = slice(at, at + chunk)
        ok = kpos[rows, :] <= qrow
        part = step(k_own[rows, :], v_own[rows, :], ok, dk_own, dv_own, rows)
        dq = part if dq is None else dq + part
    dq_acc[...] = dq
    if oth // chunk <= 4:
        for at in range(0, oth, chunk):
            rows = slice(at, at + chunk)
            ok = kpos[own_p + at : own_p + at + chunk, :] <= qrow
            dq_acc[...] += step(k_oth[rows, :], v_oth[rows, :], ok, dk_oth, dv_oth, rows)
    else:

        @pl.loop(0, oth // chunk)
        def _(j):
            rows = pl.ds(pl.multiple_of(j * chunk, chunk), chunk)
            ok = kpos[pl.ds(pl.multiple_of(own_p + j * chunk, chunk), chunk), :] <= qrow
            dq_acc[...] += step(k_oth[rows, :], v_oth[rows, :], ok, dk_oth, dv_oth, rows)

    @pl.when(jnp.logical_not(is_prompt))
    def _():
        code, lowest = twice(cqc[0:1, :]), twice(cqc[1:2, :])
        rows = slice(own_p, k_own.shape[0])
        ok = (ckc[...] <= code) & (ckc[...] >= lowest)
        dq_acc[...] += step(k_own[rows, :], v_own[rows, :], ok, dk_own, dv_own, rows)

    scale = HEAD_DIM ** (-0.5)
    gain_sum = jnp.zeros((8, HEAD_DIM), F32)
    for g, c in enumerate(heads):
        grad = dq_acc[:, g * bq : (g + 1) * bq].T * scale
        raw, rows = head_norm_rot_back(
            qraw[:, c].astype(F32), gq[...], cos_q[...], sin_q[...], grad
        )
        dq_out[:, c] = raw.astype(BF)
        gain_sum += jnp.sum(rows.reshape(bq // 8, 8, HEAD_DIM), axis=0)
    dgq_out[...] += gain_sum

    @pl.when(i == pl.num_programs(0) - 1)
    def _():
        for total, raw_in, cos, sin, out in (
            (dk_own, kraw_own, cos_o, sin_o, dk_own_out),
            (dk_oth, kraw_oth, cos_t, sin_t, dk_oth_out),
        ):
            n = total.shape[0]
            part = 256

            def finish(rows, total=total, raw_in=raw_in, cos=cos, sin=sin, out=out):
                raw, gain_rows = head_norm_rot_back(
                    raw_in[rows, :].astype(F32),
                    gk[...],
                    cos[rows, :],
                    sin[rows, :],
                    total[rows, :] * (1.0 / LOG2E),
                )
                out[rows, :] = raw.astype(BF)
                dgk_out[...] += jnp.sum(gain_rows.reshape(part // 8, 8, HEAD_DIM), axis=0)

            @pl.loop(0, n // part)
            def _(j):
                finish(pl.ds(pl.multiple_of(j * part, part), part))

        dv_own_out[...] = dv_own[...].astype(BF)
        dv_oth_out[...] = dv_oth[...].astype(BF)


def attend_back(
    head, filled, waits, q, qraw, do, o, level, own, oth, tabs, gq, gk, pos, own_p, bq=256
):
    rows = q.shape[0]
    n_oth = oth[0].shape[0]
    keys = own_p + n_oth
    chunk = min(512, own_p)
    wide = pl.BlockSpec((bq, GROUP * HEAD_DIM), lambda i: (i, head))
    tab = pl.BlockSpec((bq, HEAD_DIM), lambda i: (i, 0))
    head_col = lambda n: pl.BlockSpec((n, HEAD_DIM), lambda i: (0, head))
    cont_block = lambda i: (0, jnp.maximum(i - own_p // bq, 0))
    one = whole((1, HEAD_DIM))
    full = lambda n: whole((n, HEAD_DIM))
    cos_own, sin_own, cos_oth, sin_oth = tabs
    ins = [
        q, qraw, do, o, level, cos_own, sin_own, gq, gk,
        own[0], own[1], own[2], cos_own, sin_own,
        oth[0], oth[1], oth[2], cos_oth, sin_oth,
        pos["q_row"], pos["k_col"], pos["cq_row"], pos["ck_col"],
    ]
    specs = [
        wide, wide, wide, wide,
        pl.BlockSpec((1, GROUP, bq), lambda i: (head, 0, i)),
        tab, tab, one, one,
        head_col(rows), head_col(rows), head_col(rows), full(rows), full(rows),
        head_col(n_oth), head_col(n_oth), head_col(n_oth), full(n_oth), full(n_oth),
        pl.BlockSpec((1, bq), lambda i: (0, i)),
        whole((keys, 1)),
        pl.BlockSpec((2, bq), cont_block),
        whole((rows - own_p, 1)),
    ]
    anywhere = pl.BlockSpec(memory_space=pl.ANY)
    aliases = {len(ins) + n: n for n in range(len(filled))}
    extra = list(filled) + list(waits)
    return pl.pallas_call(
        functools.partial(attend_back_kernel, own_p, n_oth, chunk),
        out_shape=[
            jax.ShapeDtypeStruct((rows, QW), BF),
            jax.ShapeDtypeStruct((rows, KW), BF),
            jax.ShapeDtypeStruct((rows, KW), BF),
            jax.ShapeDtypeStruct((n_oth, KW), BF),
            jax.ShapeDtypeStruct((n_oth, KW), BF),
            jax.ShapeDtypeStruct((8, HEAD_DIM), F32),
            jax.ShapeDtypeStruct((8, HEAD_DIM), F32),
        ],
        grid=(rows // bq,),
        in_specs=specs + [anywhere] * len(extra),
        out_specs=[
            wide, head_col(rows), head_col(rows), head_col(n_oth), head_col(n_oth),
            whole((8, HEAD_DIM)), whole((8, HEAD_DIM)),
        ],
        scratch_shapes=[
            pltpu.VMEM((rows, HEAD_DIM), F32),
            pltpu.VMEM((rows, HEAD_DIM), F32),
            pltpu.VMEM((n_oth, HEAD_DIM), F32),
            pltpu.VMEM((n_oth, HEAD_DIM), F32),
            pltpu.VMEM((HEAD_DIM, GROUP * bq), F32),
        ],
        input_output_aliases=aliases,
        compiler_params=params(),
        cost_estimate=SMALL,
    )(*ins, *extra)


def feed_kernel(x, part, got, dy, g2, wg, wu, wd, *rest):
    h1_out, b_out, hid_out, dg_out, du_out, y_out, db_out = rest[-7:]
    hv = x[...].astype(F32) + (part[...].astype(F32) + got[...].astype(F32))
    h1_out[...] = hv
    b = hv * lax.rsqrt(jnp.mean(hv * hv, axis=-1, keepdims=True) + EPS_NORM) * g2[...]
    b = b.astype(BF)
    b_out[...] = b
    dyv = dy[...]
    step = 512
    y = db = None
    for at in range(0, FW, step):
        cols = slice(at, at + step)
        gate = dot(b, wg[:, cols])
        up = dot(b, wu[:, cols])
        dhid = dot_t(dyv, wd[cols, :])
        sig = 1.0 / (1.0 + jnp.exp(-gate))
        act = gate * sig
        hid = (act * up).astype(BF)
        dgate = (dhid * up * (sig * (1.0 + gate * (1.0 - sig)))).astype(BF)
        dup = (dhid * act).astype(BF)
        hid_out[:, cols] = hid
        dg_out[:, cols] = dgate
        du_out[:, cols] = dup
        y_part = dot(hid, wd[cols, :])
        db_part = dot_t(dgate, wg[:, cols]) + dot_t(dup, wu[:, cols])
        y = y_part if y is None else y + y_part
        db = db_part if db is None else db + db_part
    y_out[...] = y.astype(BF)
    db_out[...] = db.astype(BF)


def feed(filled, base, total, x, part, got, dy, g2, wg, wu, wd):
    rows = part.shape[0]
    bm = 256
    base //= bm
    row = lambda width: pl.BlockSpec((bm, width), lambda i: (i, 0))
    later = lambda width: pl.BlockSpec((bm, width), lambda i: (base + i, 0))
    anywhere = pl.BlockSpec(memory_space=pl.ANY)
    return pl.pallas_call(
        feed_kernel,
        out_shape=[
            jax.ShapeDtypeStruct((total, D), F32),
            jax.ShapeDtypeStruct((total, D), BF),
            jax.ShapeDtypeStruct((total, FW), BF),
            jax.ShapeDtypeStruct((total, FW), BF),
            jax.ShapeDtypeStruct((total, FW), BF),
            jax.ShapeDtypeStruct((rows, D), BF),
            jax.ShapeDtypeStruct((rows, D), BF),
        ],
        grid=(rows // bm,),
        in_specs=[
            later(D), row(D), row(D), later(D), whole((1, D)), whole((D, FW)), whole((D, FW)), whole((FW, D)),
        ]
        + [anywhere] * len(filled),
        out_specs=[later(D), later(D), later(FW), later(FW), later(FW), row(D), row(D)],
        input_output_aliases={8 + n: n for n in range(len(filled))},
        compiler_params=params(),
        cost_estimate=SMALL,
    )(x, part, got, dy, g2, wg, wu, wd, *filled)


def back_kernel(h1, dy, mine, got, g2, wo, *rest):
    dh_out, da_out, do_out, dg_out = rest[-4:]
    hv = h1[...]
    db = mine[...].astype(F32) + got[...].astype(F32)
    r = lax.rsqrt(jnp.mean(hv * hv, axis=-1, keepdims=True) + EPS_NORM)
    xh = hv * r
    dg = db * g2[...]
    dh = dy[...].astype(F32) + r * (dg - xh * jnp.mean(dg * xh, axis=-1, keepdims=True))
    dh_out[...] = dh
    da = dh.astype(BF)
    da_out[...] = da
    do_out[...] = dot_t(da, wo[...]).astype(BF)
    gain = jnp.sum((db * xh).reshape(hv.shape[0] // 8, 8, D), axis=0)

    @pl.when(pl.program_id(0) == 0)
    def _():
        dg_out[...] = jnp.zeros_like(dg_out)

    dg_out[...] += gain


def back_norm(filled, base, h1, dy, mine, got, g2, wo):
    rows, total = mine.shape[0], h1.shape[0]
    bm = 256
    base //= bm
    row = lambda width: pl.BlockSpec((bm, width), lambda i: (i, 0))
    later = lambda width: pl.BlockSpec((bm, width), lambda i: (base + i, 0))
    anywhere = pl.BlockSpec(memory_space=pl.ANY)
    return pl.pallas_call(
        back_kernel,
        out_shape=[
            jax.ShapeDtypeStruct((total, D), F32),
            jax.ShapeDtypeStruct((total, D), BF),
            jax.ShapeDtypeStruct((total, QW), BF),
            jax.ShapeDtypeStruct((8, D), F32),
        ],
        grid=(rows // bm,),
        in_specs=[later(D), later(D), row(D), row(D), whole((1, D)), whole((QW, D))]
        + [anywhere] * len(filled),
        out_specs=[later(D), later(D), later(QW), whole((8, D))],
        input_output_aliases={6 + n: n for n in range(len(filled))},
        compiler_params=params(),
        cost_estimate=SMALL,
    )(h1, dy, mine, got, g2, wo, *filled)


def layout():
    q_width = HEADS * HEAD_DIM
    kv_width = KV_HEADS * HEAD_DIM
    return [
        (D,),
        (D, q_width),
        (D, kv_width),
        (D, kv_width),
        (HEAD_DIM,),
        (HEAD_DIM,),
        (q_width, D),
        (D,),
        (D, FF),
        (D, FF),
        (FF, D),
    ]


LANES = 128
SHARD = 491592
FLAT_AT = {"g1": 0, "wq": 8, "wk": 16392, "wv": 24584, "gqk": 32776, "wo": 32778,
           "g2": 49162, "wg": 49170, "wu": 73746, "wd": 98322}
PER_ROW = {"wq": 16, "wk": 8, "wv": 8, "wo": 8, "wg": 24, "wu": 24, "wd": 8}


def matrix_kernel(per, split, place, main, extra, out, wide):
    count = main.shape[0]
    wide[:count, :] = main[...].astype(F32)
    wide[count:, :] = extra[...].astype(F32)
    rows = out.shape[0]
    first = place[1]
    if split:
        first = first + place[0] * (out.shape[1] // LANES)
    for at in range(out.shape[1] // LANES):
        cols = slice(at * LANES, (at + 1) * LANES)
        out[:, cols] = wide[pl.ds(first + at, rows, stride=per), :].astype(BF)


def matrix(lanes, name, split, rows, step, core):
    per = PER_ROW[name]
    count = step * per
    at = FLAT_AT[name]
    base = at // count
    width = per * LANES // (CORES if split else 1)
    blocks = (rows if split else rows // CORES) // step
    place = jnp.stack([core, jnp.full_like(core, at - base * count)]).astype(jnp.int32)

    def block(i, place):
        return base + i + (0 if split else place[0] * blocks)

    return pl.pallas_call(
        functools.partial(matrix_kernel, per, split),
        out_shape=jax.ShapeDtypeStruct((blocks * step, width), BF),
        grid_spec=pltpu.PrefetchScalarGridSpec(
            num_scalar_prefetch=1,
            grid=(blocks,),
            in_specs=[
                pl.BlockSpec((count, LANES), lambda i, place: (block(i, place), 0)),
                pl.BlockSpec(
                    (32, LANES), lambda i, place: ((block(i, place) + 1) * (count // 32), 0)
                ),
            ],
            out_specs=pl.BlockSpec((step, width), lambda i, place: (i, 0)),
            scratch_shapes=[pltpu.VMEM((count + 32, LANES), F32)],
        ),
        compiler_params=params(),
        cost_estimate=SMALL,
    )(place, lanes, lanes)


def gain_vectors(flat_vec):
    take = lambda name, skip, size: lax.slice(
        flat_vec, (FLAT_AT[name] * LANES + skip,), (FLAT_AT[name] * LANES + skip + size,)
    )
    gains = take("g1", 0, D), take("g2", 0, D), take("gqk", 0, LANES), take("gqk", LANES, LANES)
    return [gain.astype(F32).reshape(1, -1) for gain in gains]


def plain_grads(
    pick, a, a_far, b, o, hid, dgate, dup, dy, da_out, dq, dk, dv, dg1, dgq, dgk, dg2
):
    a_all = jnp.concatenate([a, a_far])
    grads = [
        dg1,
        t_dot(a, dq),
        t_dot(a_all, jnp.concatenate(dk)),
        t_dot(a_all, jnp.concatenate(dv)),
        jnp.sum(dgq, axis=0),
        jnp.sum(dgk, axis=0),
        t_dot(o, da_out),
        0.5 * dg2,
        t_dot(b, dgate),
        t_dot(b, dup),
        t_dot(hid, dy),
    ]
    flat = []
    for number, (grad, shape) in enumerate(zip(grads, layout())):
        if len(shape) == 2:
            axis = 0 if number in (6, 10) else 1
            blank = jnp.zeros_like(grad)
            grad = jnp.concatenate([pick(grad, blank), pick(blank, grad)], axis=axis)
        flat.append(grad.reshape(-1).astype(F32))
    return lax.psum_scatter(
        jnp.concatenate(flat), ("dp", "seq"), scatter_dimension=0, tiled=True
    )


X_FIRST = ("wq", "wg", "wd")
FEED_PARTS = {
    (1, 0): [("wo", 0, 704)],
    (1, 1): [("wo", 704, 1664)],
    (1, 2): [("wo", 1664, 2048), ("wg", 0, 192)],
    (1, 3): [("wg", 192, 512)],
    (2, 0): [("wg", 512, 832)],
    (2, 1): [("wg", 832, 1024), ("wu", 0, 128)],
    (2, 2): [("wu", 128, 448)],
    (2, 3): [("wu", 448, 768)],
    (3, 0): [("wu", 768, 1024), ("wd", 0, 192)],
    (3, 1): [("wd", 192, 1152)],
    (3, 2): [("wd", 1152, 2112)],
    (3, 3): [("wd", 2112, 3072)],
}
HEAD_PARTS = {0: ("wq", 0, 512), 1: ("wq", 512, 1024), 2: ("wk", 0, 1024), 3: ("wv", 0, 1024)}
TAIL = 288


def plane_pairs(distance, wanted=lambda dp, seq: True):
    pairs = []
    for dp in range(4):
        for seq in range(8):
            to = dp ^ distance
            if wanted(to, seq):
                pairs.append((dp * 8 + seq, to * 8 + seq))
    return pairs


def swap_dp(block, distance):
    return lax.ppermute(block, "dp", [(i, i ^ distance) for i in range(4)])


def cut(block, index, axis=1):
    width = block.shape[axis] // 2
    return lax.dynamic_slice_in_dim(block, index * width, width, axis)


def plane_order(name):
    dp = lax.axis_index("dp")
    order = ((dp % 2, 1), (dp // 2, 2))
    return order if name in X_FIRST else order[::-1]


def plane_step(grad, name, step):
    mine, distance = plane_order(name)[step]
    return cut(grad, mine), swap_dp(cut(grad, 1 - mine), distance)


def kept(*stages):
    return [stage[0] for stage in stages]


def added(stage):
    return (stage[0].astype(F32) + stage[1].astype(F32)).astype(BF)


def line_start(parts):
    low = lax.axis_index("seq") // 2 % 2
    parts = parts.reshape((2, 2) + parts.shape[1:])
    keep = lax.dynamic_index_in_dim(parts, low, 1, keepdims=False)
    send = lax.dynamic_index_in_dim(parts, 1 - low, 1, keepdims=False)
    return keep, xor_seq(send, 2)


def line_next(stage):
    high = lax.axis_index("seq") // 4
    parts = added(stage)
    keep = lax.dynamic_index_in_dim(parts, high, 0, keepdims=False)
    send = lax.dynamic_index_in_dim(parts, 1 - high, 0, keepdims=False)
    return keep, xor_seq(send, 4)


def stack_rows(grad, low, high):
    return [grad[low:high, at : at + LANES] for at in range(0, grad.shape[1], LANES)]


def feed_line(sums):
    spare = jnp.zeros((256, LANES), BF)
    per_line = []
    for z in range(4):
        blocks = [spare] if z == 0 else []
        for d in (1, 2, 3):
            for name, low, high in FEED_PARTS[d, z]:
                blocks += stack_rows(sums[name], low, high)
        per_line.append(jnp.concatenate(blocks))
    return line_start(jnp.stack(per_line))


ROWS = 3872
PART = 176
BEFORE = TAIL * 8


def spread(who, other, core, dp, name, at, rows, into, to):
    per = PER_ROW[name] // 8
    for source, side in ((who, core), (other, 1 - core)):
        for place in range(4):
            chip = (place % 2) * 2 + place // 2 if name in X_FIRST else place
            for col in range(per):
                first = to + side * (4 * per) + place * per + col
                block = source[chip ^ dp, at + col * rows : at + (col + 1) * rows, :]
                into[pl.ds(first, rows, stride=8 * per), :] = block.astype(F32)


def feed_flat_kernel(info, who, other, out):
    core, spot = info[0], info[1]

    @pl.when((spot < 4) | (spot == 4))
    def _():
        out[...] = jnp.zeros_like(out)

    for (d, z), blocks in FEED_PARTS.items():

        @pl.when(spot == d * 4 + z)
        def _(d=d, z=z, blocks=blocks):
            at, to = (256, 2048) if (d, z) == (1, 0) else (0, 0)
            for name, low, high in blocks:
                rows = high - low
                spread(who, other, core, 0, name, at, rows, out, to)
                at += rows * PER_ROW[name] // 8
                to += rows * PER_ROW[name]


def main_row(d, z):
    if (d, z) == (1, 0):
        return FLAT_AT["gqk"]
    name, low, _ = HEAD_PARTS[z] if d == 0 else FEED_PARTS[d, z][0]
    return FLAT_AT[name] + low * PER_ROW[name]


STARTS = [
    (8 * d + 2 * z + c) * SHARD // LANES - (main_row(d, z) - BEFORE)
    for d in range(4)
    for z in range(4)
    for c in range(2)
]
WIDE = max(BEFORE + 8192, (max(STARTS) + ROWS + 16) // 8 * 8)


def adam(grad, master, moment1, moment2):
    moment1_new = BETA_ONE * moment1 + (1.0 - BETA_ONE) * grad
    moment2_new = BETA_TWO * moment2 + (1.0 - BETA_TWO) * grad * grad
    update = moment1_new / CORRECT_ONE / (jnp.sqrt(moment2_new / CORRECT_TWO) + ADAM_EPS)
    return moment1_new, master - LEARN_RATE * (update + DECAY_RATE * master)


def finish_kernel(
    info, who, other, flat, before, gains, master, moment1, moment2,
    grad_out, moment1_out, master_out, block_out, wide, work,
):
    core, spot, start, skip, ahead, rest = [info[i] for i in range(6)]

    def put_before(name, dp):
        spread(who, other, core, dp, name, 1024, TAIL * 8 // PER_ROW[name], wide, 0)

    @pl.when(spot == 0)
    def _():
        wide[BEFORE - 8 : BEFORE, :] = gains[0:8, :]

    @pl.when((spot == 1) | (spot == 2))
    def _():
        put_before("wq", 0)

    @pl.when(spot == 3)
    def _():
        put_before("wk", 0)

    @pl.when(spot == 4)
    def _():
        put_before("wv", 1)
        wide[BEFORE : BEFORE + 2, :] = gains[8:10, :]
        wide[BEFORE + 2 : BEFORE + 2 + 5632, :] = flat[2048:, :]

    @pl.when(spot < 2)
    def _():
        spread(who, other, core, 0, "wq", 0, 512, wide, BEFORE)

    @pl.when((spot == 2) | (spot == 3))
    def _():
        spread(who, other, core, 0, "wk", 0, 1024, wide, BEFORE)

    @pl.when(spot > 4)
    def _():
        wide[BEFORE - 16 : BEFORE, :] = before[...]

    @pl.when(spot == 6)
    def _():
        wide[BEFORE : BEFORE + 3072, :] = flat[:3072, :]
        wide[BEFORE + 3072 : BEFORE + 3080, :] = gains[10:18, :]
        wide[BEFORE + 3080 : BEFORE + 7688, :] = flat[3072:, :]

    @pl.when((spot == 5) | (spot > 6))
    def _():
        wide[BEFORE : BEFORE + 7680, :] = flat[...]

    col = lax.broadcasted_iota(jnp.int32, (PART, LANES), 1)
    row = lax.broadcasted_iota(jnp.int32, (PART, LANES), 0)
    work[0:8, :] = jnp.zeros((8, LANES), F32)
    work[ROWS + 8 :, :] = jnp.zeros((8, LANES), F32)
    turn = lax.rem(LANES - skip, LANES)

    @pl.loop(0, ROWS // PART)
    def _(j):
        at = pl.multiple_of(j * PART, 8)
        here = pl.ds(at, PART)
        now = pltpu.roll(wide[pl.ds(start + at, PART), :], turn, 1)
        after_it = pltpu.roll(wide[pl.ds(start + at + 1, PART), :], turn, 1)
        grad = jnp.where(col < LANES - skip, now, after_it)
        moment1_new, master_new = adam(grad, master[here, :], moment1[here, :], moment2[here, :])
        grad_out[here, :] = grad
        moment1_out[here, :] = moment1_new
        master_out[here, :] = master_new
        inside = (at + row) * LANES + col < SHARD
        work[pl.ds(at + 8, PART), :] = jnp.where(inside, master_new, 0.0)

    @pl.loop(0, ROWS // PART)
    def _(j):
        at = pl.multiple_of(j * PART, 16)
        now = pltpu.roll(work[pl.ds(7 - ahead + at, PART), :], rest, 1)
        after_it = pltpu.roll(work[pl.ds(8 - ahead + at, PART), :], rest, 1)
        block_out[pl.ds(at, PART), :] = jnp.where(col < rest, now, after_it).astype(BF)


def local(kernel, shapes, scratch, info, *arrays):
    vmem = pl.BlockSpec(memory_space=pltpu.VMEM)
    return pl.pallas_call(
        kernel,
        out_shape=shapes,
        in_specs=[pl.BlockSpec(memory_space=pltpu.SMEM)] + [vmem] * len(arrays),
        out_specs=jax.tree.map(lambda _: vmem, shapes),
        scratch_shapes=scratch,
        compiler_params=params(),
        cost_estimate=SMALL,
    )(jnp.stack(info).astype(jnp.int32), *arrays)


def fast_grads(core, feed_stage, head_q, head_kv, gains, states, da, to_home):
    dp = lax.axis_index("dp")
    rank = lax.axis_index("seq")
    line = rank // 2
    spot = dp * 4 + line
    gains = jnp.concatenate(gains).reshape(1, -1, LANES)
    gains = jnp.broadcast_to(gains, (32,) + gains.shape[1:])
    gains = lax.all_to_all(gains, ("dp", "seq"), 0, 0, tiled=True)
    feed_part = added(feed_stage).reshape(3, 960, LANES)
    feed_part = after(feed_part, kept(head_q, head_kv))

    feed_got = jnp.concatenate([feed_part[:1], feed_part])
    feed_got = lax.all_to_all(feed_got, "dp", 0, 0, tiled=True)
    head_q, head_kv = added(head_q), added(head_kv)
    head_stage = line_start(
        jnp.stack(
            [
                jnp.concatenate(stack_rows(head_q, 0, 512)),
                jnp.concatenate(stack_rows(head_q, 512, 1024)),
                head_kv[:1024],
                head_kv[1024:],
            ]
        )
    )
    feed_flat = local(
        feed_flat_kernel,
        jax.ShapeDtypeStruct((7680, LANES), F32),
        [],
        (core, spot),
        feed_got,
        xor_seq(feed_got, 1),
    )
    chain = [(8 * d + s, 8 * d + s + 2) for d in range(4) for s in range(8) if 8 * d + s < 30]
    before = lax.ppermute(feed_flat[-16:], ("dp", "seq"), chain)
    head_part = added(line_next(head_stage))
    tail = jnp.where(
        line < 2,
        jnp.concatenate([head_part[512 - TAIL // 2 : 512], head_part[1024 - TAIL // 2 :]]),
        head_part[1024 - TAIL :],
    )
    ring = [(8 * d + s, 8 * d + (s + 2) % 8) for d in range(4) for s in range(8)]
    tail, gains, before = after((tail, gains, before))
    tail = lax.ppermute(tail, ("dp", "seq"), ring)
    tail, da = after((tail, da))
    dx_rows = to_home(da)
    head_all = after(jnp.concatenate([head_part, tail]), dx_rows[0])
    head_got = [head_all]
    for distance in (1, 2, 3):
        pairs = plane_pairs(distance, lambda d, s: d == 0 or (d == 1 and s < 2))
        head_got.append(lax.ppermute(head_all, ("dp", "seq"), pairs))
    gains = jnp.sum(gains, axis=0)
    head_got = jnp.stack(head_got)
    head_far = xor_seq(head_got, 1)

    index = spot * 2 + core
    start = jnp.asarray(STARTS, jnp.int32)[index]
    info = (core, spot, start, index * (SHARD % LANES) % LANES, rank * 72 // LANES, rank * 72 % LANES)
    rows = jax.ShapeDtypeStruct((ROWS, LANES), F32)
    results = local(
        finish_kernel,
        [rows, rows, rows, jax.ShapeDtypeStruct((ROWS, LANES), BF)],
        [pltpu.VMEM((WIDE, LANES), F32), pltpu.VMEM((ROWS + 16, LANES), F32)],
        info, head_got, head_far, feed_flat, before, gains, *states,
    )
    results, dx_rows = after((results, dx_rows))
    return *results, dx_rows


def gather_weights(block):
    blocks = lax.all_gather(block, "seq", axis=0)
    body, ends = blocks[:, :3840], blocks[:, 3840:3848]
    heads = body[1:, :8] + ends[:-1]
    heads = jnp.concatenate([body[:1, :8], heads])
    rows = jnp.concatenate([heads, body[:, 8:]], axis=1).reshape(-1, LANES)
    rows = jnp.concatenate([rows, ends[-1]])
    return rows.reshape(-1)[: 8 * SHARD]


def norm_back(x, gain, grad):
    r = lax.rsqrt(jnp.mean(x * x, axis=-1, keepdims=True) + EPS_NORM)
    xh = x * r
    dg = grad * gain
    return r * (dg - xh * jnp.mean(dg * xh, axis=-1, keepdims=True))


def into_kernel(own_blocks, dq, dk, dv, dk_far, dv_far, x, x_far, wq, wk, wv, own, far, gain_out):
    step = pl.program_id(0)

    @pl.when(step == 0)
    def _():
        gain_out[...] = jnp.zeros_like(gain_out)

    def finish(total, rows, out):
        out[...] = total.astype(BF)
        xv = rows[...].astype(F32)
        xh = xv * lax.rsqrt(jnp.mean(xv * xv, axis=-1, keepdims=True) + EPS_NORM)
        gain_out[...] += jnp.sum((total * xh).reshape(xv.shape[0] // 8, 8, D), axis=0)

    @pl.when(step < own_blocks)
    def _():
        total = dot_t(dk[...], wk[...]) + dot_t(dv[...], wv[...]) + dot_t(dq[...], wq[...])
        finish(total, x, own)

    @pl.when(step >= own_blocks)
    def _():
        finish(dot_t(dk_far[...], wk[...]) + dot_t(dv_far[...], wv[...]), x_far, far)


def into_input(dq, dk, dv, dk_far, dv_far, x, x_far, wq, wk, wv):
    bm = 256
    own_blocks, far_blocks = x.shape[0] // bm, x_far.shape[0] // bm
    near = lambda width: pl.BlockSpec((bm, width), lambda i: (jnp.minimum(i, own_blocks - 1), 0))
    away = lambda width: pl.BlockSpec((bm, width), lambda i: (jnp.maximum(i - own_blocks, 0), 0))
    return pl.pallas_call(
        functools.partial(into_kernel, own_blocks),
        out_shape=[
            jax.ShapeDtypeStruct(x.shape, BF),
            jax.ShapeDtypeStruct(x_far.shape, BF),
            jax.ShapeDtypeStruct((8, D), F32),
        ],
        grid=(own_blocks + far_blocks,),
        in_specs=[near(QW), near(KW), near(KW), away(KW), away(KW), near(D), away(D)]
        + [whole(weight.shape) for weight in (wq, wk, wv)],
        out_specs=[near(D), away(D), whole((8, D))],
        compiler_params=params(),
        cost_estimate=SMALL,
    )(dq, dk, dv, dk_far, dv_far, x, x_far, wq, wk, wv)


def tables(positions):
    half_dim = HEAD_DIM // 2
    frequency = ROPE_BASE ** (-jnp.arange(half_dim, dtype=F32) * 2.0 / HEAD_DIM)
    angles = positions.astype(F32)[:, None] * frequency[None, :]
    cosine, sine = jnp.cos(angles), jnp.sin(angles)
    return jnp.concatenate([cosine, cosine], 1), jnp.concatenate([-sine, sine], 1)


def shards(x_prompt, x_cont, dy_prompt, dy_cont, prompt_pos, weights, master, moment1, moment2):
    count = lax.axis_size("seq")
    rank = lax.axis_index("seq")
    half = count // 2
    side = rank // half
    core = rank % CORES
    chips = half // CORES
    p = x_prompt.shape[1]
    c = x_cont.shape[1]
    prompt_len = p * count
    own_p = 4 * p
    first = core == 0

    def pick(lo, hi):
        return jnp.where(first, lo, hi)

    def share(mine, got):
        return pick(mine, got), pick(got, mine)

    def far_rows(block):
        rows = block[None]
        mask = 2
        while mask < half:
            rows = jnp.concatenate([rows, xor_seq(rows, mask)])
            mask *= 2
        return rows[1:]

    def sides(prompt, cont):
        rows = jnp.concatenate([prompt, cont], axis=1)
        own = lax.dynamic_index_in_dim(rows, side, 0, keepdims=False)
        other = lax.dynamic_index_in_dim(rows, 1 - side, 0, keepdims=False)
        return own, other

    def join(own, recv, own_got, recv_got):
        lo, hi = share(own, own_got)
        lo2, hi2 = share(recv, recv_got)
        rows_p = [lo[:p], lo2[:p], hi[:p], hi2[:p]]
        rows_c = [lo[p:], lo2[p:], hi[p:], hi2[p:]]
        return jnp.concatenate(rows_p + rows_c, axis=0)

    x_own, x_other = sides(x_prompt, x_cont)
    x_recv = xor_seq(x_other, half)
    far_one = far_rows(x_own[:p])
    x_own_got = xor_seq(x_own, 1)

    lanes = weights.reshape(-1, LANES)
    g1, g2, gq, gk = gain_vectors(weights)
    w_q = matrix(lanes, "wq", True, D, 128, core)
    w_k = matrix(lanes, "wk", True, D, 256, core)
    w_v = matrix(lanes, "wv", True, D, 256, core)
    x_recv = after(x_recv, w_q, w_k, w_v)
    far_two = far_rows(x_recv[:p])
    x_recv_got = xor_seq(x_recv, 1)
    far_one = after(far_one, x_recv)
    far_one_got = xor_seq(far_one, 1)
    lanes = after(lanes, x_recv)
    w_g = matrix(lanes, "wg", True, D, 128, core)
    w_u = matrix(lanes, "wu", True, D, 128, core)
    x_recv_got = after(x_recv_got, w_g, w_u)
    x = join(x_own, x_recv, x_own_got, x_recv_got)

    chip_ids = (rank - core) ^ (CORES * jnp.arange(chips)[:, None, None])
    ids = (chip_ids + jnp.arange(CORES)[None, :, None]) ^ (half * jnp.arange(2)[None, None, :])
    own_group = lax.dynamic_index_in_dim(prompt_pos, side, 0, keepdims=False)
    key_pos = jnp.take(own_group.reshape(count, p), ids.reshape(-1), axis=0).reshape(-1)
    quarter = c // 2
    steps = jnp.arange(quarter, dtype=jnp.int32)
    own_half = [
        prompt_len + jnp.concatenate([k * quarter + steps, (3 - k) * quarter + steps])
        for k in range(CORES)
    ]
    cont_pos = jnp.concatenate([own_half[0], own_half[0], own_half[1], own_half[1]])
    seg = jnp.tile(jnp.repeat(jnp.arange(2, dtype=jnp.int32), c), CORES)
    big = 2 * prompt_len + 4 * c
    cont_code = seg * big + cont_pos
    query_pos = jnp.concatenate([key_pos[:own_p], cont_pos])
    cont_q = jnp.stack([cont_code, seg * big])
    pos = {
        "q_col": query_pos[:, None], "q_row": query_pos[None, :],
        "k_col": key_pos[:, None], "k_row": key_pos[None, :],
        "cq_col": cont_q.T, "cq_row": cont_q,
        "ck_col": cont_code[:, None], "ck_row": cont_code[None, :],
    }
    cos_own, sin_own = tables(query_pos)
    cos_far, sin_far = tables(key_pos[own_p:])

    a, q, qraw, k_own, kraw_own, v_own = project(x, g1, cos_own, sin_own, w_q, w_k, w_v, gq, gk, True)
    far_two = after(far_two, a)
    far_two_got = xor_seq(far_two, 1)
    lanes = after(lanes, a)
    w_d = matrix(lanes, "wd", False, FF, 384, core)
    w_o = matrix(lanes, "wo", False, HEADS * HEAD_DIM, 256, core)
    far_two_got = after(far_two_got, w_d, w_o)
    dy_own, dy_other = after(sides(dy_prompt, dy_cont), far_two)
    dy_recv = xor_seq(dy_other, half)
    dy_own_got = xor_seq(dy_own, 1)
    lo, hi = share(far_one, far_one_got)
    lo2, hi2 = share(far_two, far_two_got)
    x_far = jnp.stack([lo, lo2, hi, hi2], axis=1).reshape(-1, D)
    a_far, k_far, kraw_far, v_far = project(x_far, g1, cos_far, sin_far, w_q, w_k, w_v, gq, gk, False)
    rows = x.shape[0]
    o_p, level_p = attend(q, k_own, v_own, k_far, v_far, pos, own_p, False)
    part_p = dot(o_p, w_o).astype(BF)
    part_p_got = xor_seq(part_p, 1)
    q, part_p, dy_recv = after((q, part_p, dy_recv))
    dy_recv_got = xor_seq(dy_recv, 1)
    o_c, level_c = attend(q, k_own, v_own, k_far, v_far, pos, own_p, True)
    o_c, dy_recv_got = after((o_c, dy_recv_got))
    part_c = dot(o_c, w_o).astype(BF)
    part_c_got = xor_seq(part_c, 1)
    part_p_got = after(part_p_got, part_c)
    dy = join(dy_own, dy_recv, dy_own_got, dy_recv_got)
    *filled, y_p, db_p = feed((), 0, rows, x, part_p, part_p_got, dy, g2, w_g, w_u, w_d)
    db_p_got = xor_seq(db_p, 1)
    o = jnp.concatenate([o_p, o_c])
    o_got = xor_seq(o, 1)
    part_c_got, o_got = after((part_c_got, o_got), db_p)
    *filled, y_c, db_c = feed(filled, own_p, rows, x, part_c, part_c_got, dy, g2, w_g, w_u, w_d)
    h1, b, hid, dgate, dup = filled
    db_c_got = xor_seq(db_c, 1)
    hid_got = xor_seq(hid, 1)
    level = jnp.concatenate([level_p, level_c], axis=2)
    y_part = jnp.concatenate([y_p, y_c])
    fast = count == 8 and lax.axis_size("dp") == 4
    def core_rows(rows, which):
        return jnp.concatenate(
            [
                lax.dynamic_slice_in_dim(rows, which * 2 * p, 2 * p),
                lax.dynamic_slice_in_dim(rows, own_p + which * 2 * c, 2 * c),
            ]
        )

    y_got = xor_seq(core_rows(y_part, 1 - core), 1)
    if fast:
        grad_g, grad_u = t_dot(b, dgate).astype(BF), t_dot(b, dup).astype(BF)
        grad_g, db_p_got, db_c_got = after((grad_g, db_p_got, db_c_got))
        flow = {"wg": plane_step(grad_g, "wg", 0)}
        flow["wu"] = plane_step(after(grad_u, kept(flow["wg"])), "wu", 0)
        dy_cols = cut(dy, core)
        grad_d = t_dot(hid, dy_cols).astype(BF)
        hid_got, y_got = after((hid_got, y_got), kept(flow["wg"], flow["wu"]))
        grad_d = share(grad_d, t_dot(hid_got, dy_cols).astype(BF))
        flow["wd"] = plane_step(jnp.concatenate(grad_d), "wd", 0)
        db_p_got, db_c_got = after((db_p_got, db_c_got), kept(flow["wd"]))
    y_core = core_rows(h1, core) + core_rows(y_part, core).astype(F32) + y_got.astype(F32)
    *filled, dg2_p = back_norm((), 0, h1, dy, db_p, db_p_got, g2, w_o)
    *filled, dg2_c = back_norm(filled, own_p, h1, dy, db_c, db_c_got, g2, w_o)
    dh1, da_out, d_o = filled
    dg2 = jnp.sum(dg2_p + dg2_c, axis=0)

    filled, waits = (), [y_core]
    back = []
    if fast:
        states = [
            jnp.concatenate([state, jnp.zeros((ROWS * LANES - SHARD,), F32)]).reshape(ROWS, LANES)
            for state in (master, moment1, moment2)
        ]
        waits += states
        cols = cut(da_out, core)
        grad_o = share(t_dot(o, cols).astype(BF), t_dot(o_got, cols).astype(BF))
        flow["wo"] = plane_step(jnp.concatenate(grad_o), "wo", 0)
        flow["wg"], flow["wu"] = after((flow["wg"], flow["wu"]), flow["wo"][0])
        for name in ("wg", "wu"):
            flow[name] = plane_step(added(flow[name]), name, 1)
        waits += kept(*flow.values())
    for head in range(KV_HEADS_C):
        *filled, dgq, dgk = attend_back(
            head, filled, waits, q, qraw, d_o, o, level,
            (k_own, v_own, kraw_own), (k_far, v_far, kraw_far),
            (cos_own, sin_own, cos_far, sin_far), gq, gk, pos, own_p,
        )
        waits = []
        back.append((dgq, dgk))
        if head == 2:
            y_rows = after(y_rows, dgq)
            waits = [y_rows[1]]
        if fast and head == 1:
            flow = after(flow, dgq)
            flow["wg"], flow["wu"] = added(flow["wg"]), added(flow["wu"])
            for name in ("wd", "wo"):
                flow[name] = plane_step(added(flow[name]), name, 1)
            waits += [flow["wg"], flow["wu"]] + kept(flow["wd"], flow["wo"])
        if head == 1:
            y_rows = home_start(after(y_core, dgq, waits), half, p, c)
            waits.append(y_rows[0])
        if fast and head == 2:
            flow = after(flow, dgq)
            flow["wd"], flow["wo"] = added(flow["wd"]), added(flow["wo"])
            feed_stage = feed_line(flow)
            waits += kept(feed_stage)
    dq, dk_own, dv_own, dk_far, dv_far = filled
    dgq, dgk = [sum(parts) for parts in zip(*back)]
    y_prompt, y_cont = home_end(y_rows, side, p)

    if fast:
        grad_q = t_dot(a, dq).astype(BF)
        grad_q, feed_stage = after((grad_q, feed_stage))
        head_q = plane_step(grad_q, "wq", 0)
        a_all = after(jnp.concatenate([a, a_far]), kept(head_q))
        pair = [(dk_own, dk_far), (dv_own, dv_far)]
        pair = [t_dot(a_all, jnp.concatenate(part)).astype(BF) for part in pair]
        head_kv = plane_step(jnp.concatenate(pair), "wk", 0)
        feed_stage = line_next(feed_stage)
        dk_own, dk_far = after((dk_own, dk_far), kept(feed_stage, head_q, head_kv))

    da_own, da_far, gain_rows = into_input(
        dq, dk_own, dv_own, dk_far, dv_far, x, x_far, w_q, w_k, w_v
    )
    dg1 = jnp.sum(gain_rows, axis=0)
    da_far = da_far.reshape(chips - 1, CORES, 2 * p, D)
    far_keep = lax.dynamic_index_in_dim(da_far, core, 1, keepdims=False)
    far_send = lax.dynamic_index_in_dim(da_far, 1 - core, 1, keepdims=False)
    sent = jnp.concatenate([core_rows(da_own, 1 - core), far_send.reshape(-1, D)])
    got = xor_seq(sent, 1)
    if fast:
        head_q, head_kv, feed_stage = after((head_q, head_kv, feed_stage))
        head_q = plane_step(added(head_q), "wq", 1)
        head_kv = plane_step(added(head_kv), "wk", 1)
        got = after(got, kept(head_q, head_kv))
    mine = core_rows(da_own, core).astype(F32) + got[: rows // 2].astype(F32)
    far_sum = far_keep.astype(F32) + got[rows // 2 :].reshape(far_keep.shape).astype(F32)
    blocks = jnp.concatenate([mine[None, : 2 * p], far_sum])
    mask = half // 2
    while mask > 1:
        near, away = blocks[: mask // 2], blocks[mask // 2 :].astype(BF)
        if fast:
            head_q, head_kv = after((head_q, head_kv), away)
        blocks = near + xor_seq(away, mask).astype(F32)
        mask //= 2
    da = jnp.concatenate([blocks[0], mine[2 * p :]])

    def to_dx(da):
        return core_rows(dh1, core) + norm_back(core_rows(x, core).astype(F32), g1, da)

    if fast:
        gains = [dg1, jnp.sum(dgq, 0), jnp.sum(dgk, 0), 0.5 * dg2]
        *results, block, dx_rows = fast_grads(
            core, feed_stage, head_q, head_kv, gains, states, da, lambda da: home_start(to_dx(da), half, p, c)
        )
        weights_new = gather_weights(block)
        grad_shard, moment1_new, master_new = [one.reshape(-1)[:SHARD] for one in results]
    else:
        grad_shard = plain_grads(
            pick, a, a_far, b, o, hid, dgate, dup, dy, da_out, dq,
            (dk_own, dk_far), (dv_own, dv_far), dg1, dgq, dgk, dg2,
        )
        dx_rows = home_start(to_dx(da), half, p, c)
        moment1_new, master_new = adam(grad_shard, master, moment1, moment2)
        weights_new = lax.all_gather(master_new.astype(BF), "seq", axis=0, tiled=True)
    dx_prompt, dx_cont = home_end(dx_rows, side, p)
    return (y_prompt, y_cont, dx_prompt, dx_cont, grad_shard, master_new, moment1_new, weights_new)


def solution(mesh):
    placed = (
        P("dp", "seq", None),
        P("dp", "seq", None),
        P("dp", "seq", None),
        P("dp", "seq", None),
        P("dp", None),
        P(),
        P(("dp", "seq")),
        P(("dp", "seq")),
        P(("dp", "seq")),
    )
    return jax.shard_map(
        shards,
        mesh=mesh,
        in_specs=placed,
        out_specs=(
            P("dp", "seq", None),
            P("dp", "seq", None),
            P("dp", "seq", None),
            P("dp", "seq", None),
            P(("dp", "seq")),
            P(("dp", "seq")),
            P(("dp", "seq")),
            P("dp"),
        ),
        check_vma=False,
    )
```

```python
import functools

import jax
import jax.numpy as jnp
from jax import lax
from jax.experimental import pallas as pl
from jax.experimental.pallas import tpu as pltpu
from jax.sharding import PartitionSpec as P

D = 1024
FF = 3072
HEADS = 16
KV_HEADS = 8
HEAD_DIM = 128

EPS_NORM = 1e-06
ROPE_BASE = 1000000.0
BETA_ONE = 0.9
BETA_TWO = 0.95
ADAM_EPS = 1e-08
LEARN_RATE = 0.0003
DECAY_RATE = 0.1
CORRECT_ONE = 1.0 - 2.656139888758747e-05
CORRECT_TWO = 1.0 - 0.005920529220333996

CORES = 2
Q_HEADS_C = HEADS // CORES
KV_HEADS_C = KV_HEADS // CORES
QW = Q_HEADS_C * HEAD_DIM
KW = KV_HEADS_C * HEAD_DIM
FW = FF // CORES
GROUP = HEADS // KV_HEADS
LOG2E = 1.4426950408889634
SCORE_FOLD = HEAD_DIM ** (-0.5) * LOG2E
VMEM_LIMIT = 52 * 1024 * 1024
SMALL = pl.CostEstimate(flops=1000, bytes_accessed=1000, transcendentals=0)
BF = jnp.bfloat16
F32 = jnp.float32


def dot(left, right):
    return jnp.dot(left, right, preferred_element_type=F32)


def dot_t(left, right):
    return lax.dot_general(left, right, (((1,), (1,)), ((), ())), preferred_element_type=F32)


def t_dot(left, right):
    return lax.dot_general(left, right, (((0,), (0,)), ((), ())), preferred_element_type=F32)


def turned(block):
    return block.astype(F32).T.astype(BF)


def xor_seq(block, mask):
    count = lax.axis_size("seq")
    return lax.ppermute(block, "seq", [(i, i ^ mask) for i in range(count)])


def after(values, *earlier):
    return lax.optimization_barrier((values, earlier))[0]


def home_start(rows, half, p, c):
    rows_p, rows_c = rows[: 2 * p], rows[2 * p :]
    own = jnp.concatenate([rows_p[:p], rows_c[:c]])
    away = jnp.concatenate([rows_p[p:], rows_c[c:]]).astype(BF)
    return own, xor_seq(away, half)


def home_end(both, side, p):
    own, back = both[0], both[1].astype(F32)
    zero = side == 0
    out = jnp.stack([jnp.where(zero, own, back), jnp.where(zero, back, own)])
    return out[:, :p], out[:, p:]


def params(*semantics):
    return pltpu.CompilerParams(vmem_limit_bytes=VMEM_LIMIT)


def whole(shape):
    return pl.BlockSpec(shape, lambda *ids: (0,) * len(shape))


def head_norm_rot(raw, gain, cos, sin):
    r = lax.rsqrt(jnp.mean(raw * raw, axis=-1, keepdims=True) + EPS_NORM)
    n = raw * r * gain
    return n * cos + pltpu.roll(n, HEAD_DIM // 2, 1) * sin


def head_norm_rot_back(raw, gain, cos, sin, grad):
    dn = grad * cos - pltpu.roll(grad, HEAD_DIM // 2, 1) * sin
    r = lax.rsqrt(jnp.mean(raw * raw, axis=-1, keepdims=True) + EPS_NORM)
    xh = raw * r
    gain_rows = dn * xh
    dg = dn * gain
    return r * (dg - xh * jnp.mean(dg * xh, axis=-1, keepdims=True)), gain_rows


def project_kernel(with_q, *refs):
    if with_q:
        (x, g1, cos, sin, wq, wk, wv, gq, gk, a_out, q_out, qraw_out, k_out, kraw_out, v_out) = refs
    else:
        (x, g1, cos, sin, wk, wv, gk, a_out, k_out, kraw_out, v_out) = refs
    xv = x[...].astype(F32)
    a = xv * lax.rsqrt(jnp.mean(xv * xv, axis=-1, keepdims=True) + EPS_NORM) * g1[...]
    a = a.astype(BF)
    a_out[...] = a
    cosv, sinv = cos[...], sin[...]
    kv = dot(a, wk[...])
    for head in range(KV_HEADS_C):
        cols = slice(head * HEAD_DIM, (head + 1) * HEAD_DIM)
        raw = kv[:, cols]
        kraw_out[:, cols] = raw.astype(BF)
        k_out[:, cols] = head_norm_rot(raw, gk[...], cosv, sinv).astype(BF)
    v_out[...] = dot(a, wv[...]).astype(BF)
    if with_q:
        qv = dot(a, wq[...])
        for head in range(Q_HEADS_C):
            cols = slice(head * HEAD_DIM, (head + 1) * HEAD_DIM)
            raw = qv[:, cols]
            qraw_out[:, cols] = raw.astype(BF)
            rot = head_norm_rot(raw, gq[...], cosv, sinv)
            q_out[:, cols] = (rot * SCORE_FOLD).astype(BF)


def project(x, g1, cos, sin, wq, wk, wv, gq, gk, with_q):
    rows = x.shape[0]
    bm = 256
    row = lambda width: pl.BlockSpec((bm, width), lambda i: (i, 0))
    ins = [x, g1, cos, sin] + ([wq] if with_q else []) + [wk, wv] + ([gq] if with_q else []) + [gk]
    specs = [row(D), whole((1, D)), row(HEAD_DIM), row(HEAD_DIM)]
    specs += [whole((D, QW))] if with_q else []
    specs += [whole((D, KW))] * 2
    specs += [whole((1, HEAD_DIM))] * (2 if with_q else 1)
    widths = [D] + ([QW, QW] if with_q else []) + [KW, KW, KW]
    return pl.pallas_call(
        functools.partial(project_kernel, with_q),
        out_shape=[jax.ShapeDtypeStruct((rows, w), BF) for w in widths],
        grid=(rows // bm,),
        in_specs=specs,
        out_specs=[row(w) for w in widths],
        compiler_params=params(),
        cost_estimate=SMALL,
    )(*ins)


def attend_kernel(own_p, oth, cont, q, k_own, v_own, k_oth, v_oth, qpos, kpos, cqc, ckc, o_out, l_out):
    bq = q.shape[0]

    def run(kind):
        for head in range(GROUP):
            cols = slice(head * HEAD_DIM, (head + 1) * HEAD_DIM)
            qh = q[:, cols]
            parts = [(dot_t(qh, k_own[:own_p, :]), v_own[:own_p, :])]
            if oth:
                parts.append((dot_t(qh, k_oth[...]), v_oth[...]))
            if kind == 0:
                at = 0
                masked = []
                for s, v in parts:
                    n = s.shape[1]
                    ok = kpos[:, at : at + n] <= qpos[...]
                    masked.append((jnp.where(ok, s, -1e30), v))
                    at += n
                parts = masked
            else:
                s = dot_t(qh, k_own[own_p:, :])
                code, lowest = cqc[:, 0:1], cqc[:, 1:2]
                ok = (ckc[...] <= code) & (ckc[...] >= lowest)
                parts.append((jnp.where(ok, s, -1e30), v_own[own_p:, :]))
            top = functools.reduce(
                jnp.maximum, [jnp.max(s, axis=-1, keepdims=True) for s, _ in parts]
            )
            total = jnp.zeros((bq, 1), F32)
            acc = jnp.zeros((bq, HEAD_DIM), F32)
            for s, v in parts:
                e = jnp.exp2(s - top)
                total += jnp.sum(e, axis=-1, keepdims=True)
                acc += dot(e.astype(BF), v)
            o_out[:, cols] = (acc / total).astype(BF)
            level = jnp.broadcast_to(top + jnp.log2(total), (bq, HEAD_DIM))
            l_out[0, head : head + 1, :] = level.T[0:1, :]

    run(1 if cont else 0)


def attend_wide_kernel(
    own_p, oth, cont, q, k_own, v_own, k_oth, v_oth, qpos, kpos, cqc, ckc,
    o_out, l_out, vt_own, vt_oth,
):
    bq = q.shape[0]

    @pl.when(pl.program_id(1) == 0)
    def _():
        vt_own[...] = turned(v_own[...])
        vt_oth[...] = turned(v_oth[...])

    def twice(row):
        return jnp.concatenate([row] * GROUP, axis=1)

    heads = [slice(g * HEAD_DIM, (g + 1) * HEAD_DIM) for g in range(GROUP)]
    q2 = jnp.concatenate([q[:, c] for c in heads], axis=0)
    parts = [(dot_t(k_own[:own_p, :], q2), vt_own[:, :own_p])]
    parts.append((dot_t(k_oth[...], q2), vt_oth[...]))
    if cont:
        s = dot_t(k_own[own_p:, :], q2)
        code, lowest = twice(cqc[0:1, :]), twice(cqc[1:2, :])
        ok = (ckc[...] <= code) & (ckc[...] >= lowest)
        parts.append((jnp.where(ok, s, -1e30), vt_own[:, own_p:]))
    else:
        at = 0
        for n, (s, v) in enumerate(parts):
            ok = kpos[at : at + s.shape[0], :] <= twice(qpos[...])
            parts[n] = (jnp.where(ok, s, -1e30), v)
            at += s.shape[0]
    top = functools.reduce(jnp.maximum, [jnp.max(s, axis=0, keepdims=True) for s, _ in parts])
    total = jnp.zeros((1, GROUP * bq), F32)
    acc = jnp.zeros((HEAD_DIM, GROUP * bq), F32)
    for s, v in parts:
        e = jnp.exp2(s - top)
        total += jnp.sum(e, axis=0, keepdims=True)
        acc += dot(v, e.astype(BF))
    level = top + jnp.log2(total)
    out = acc / total
    for g, c in enumerate(heads):
        rows = slice(g * bq, (g + 1) * bq)
        o_out[:, c] = out[:, rows].T.astype(BF)
        l_out[0, g : g + 1, :] = level[:, rows]


def attend(q, k_own, v_own, k_oth, v_oth, pos, own_p, cont):
    rows = q.shape[0]
    oth = k_oth.shape[0]
    keys = own_p + oth
    bq = 256 if cont else min(512, own_p)
    base = own_p // bq if cont else 0
    here = rows - own_p if cont else own_p
    head_col = lambda n: pl.BlockSpec((n, HEAD_DIM), lambda h, i: (0, h))
    if cont:
        masks = [
            pl.BlockSpec((bq, 1), lambda h, i: (base + i, 0)),
            whole((1, keys)),
            pl.BlockSpec((bq, 2), lambda h, i: (i, 0)),
            whole((1, rows - own_p)),
        ]
        names, scratch = ("q_col", "k_row", "cq_col", "ck_row"), []
    else:
        masks = [
            pl.BlockSpec((1, bq), lambda h, i: (0, i)),
            whole((keys, 1)),
            whole((2, rows - own_p)),
            whole((rows - own_p, 1)),
        ]
        names = ("q_row", "k_col", "cq_row", "ck_col")
        scratch = [pltpu.VMEM((HEAD_DIM, rows), BF), pltpu.VMEM((HEAD_DIM, oth), BF)]
    return pl.pallas_call(
        functools.partial(attend_kernel if cont else attend_wide_kernel, own_p, oth, cont),
        out_shape=[
            jax.ShapeDtypeStruct((here, QW), BF),
            jax.ShapeDtypeStruct((KV_HEADS_C, GROUP, here), F32),
        ],
        grid=(KV_HEADS_C, here // bq),
        in_specs=[
            pl.BlockSpec((bq, GROUP * HEAD_DIM), lambda h, i: (base + i, h)),
            head_col(rows),
            head_col(rows),
            head_col(oth),
            head_col(oth),
            *masks,
        ],
        out_specs=[
            pl.BlockSpec((bq, GROUP * HEAD_DIM), lambda h, i: (i, h)),
            pl.BlockSpec((1, GROUP, bq), lambda h, i: (h, 0, i)),
        ],
        scratch_shapes=scratch,
        compiler_params=params(),
        cost_estimate=SMALL,
    )(q, k_own, v_own, k_oth, v_oth, *[pos[name] for name in names])


def attend_back_kernel(
    own_p, oth, chunk,
    q, qraw, do, o, level, cos_q, sin_q, gq, gk,
    k_own, v_own, kraw_own, cos_o, sin_o, k_oth, v_oth, kraw_oth, cos_t, sin_t,
    qpos, kpos, cqc, ckc, *rest,
):
    (dq_out, dk_own_out, dv_own_out, dk_oth_out, dv_oth_out, dgq_out, dgk_out,
     dk_own, dv_own, dk_oth, dv_oth, dq_acc) = rest[-12:]
    i = pl.program_id(0)
    bq = q.shape[0]
    is_prompt = i * bq < own_p

    @pl.when(i == 0)
    def _():
        dk_own[...] = jnp.zeros_like(dk_own)
        dv_own[...] = jnp.zeros_like(dv_own)
        dk_oth[...] = jnp.zeros_like(dk_oth)
        dv_oth[...] = jnp.zeros_like(dv_oth)

    @pl.when(i == 0)
    def _():
        dgq_out[...] = jnp.zeros_like(dgq_out)
        dgk_out[...] = jnp.zeros_like(dgk_out)

    heads = [slice(g * HEAD_DIM, (g + 1) * HEAD_DIM) for g in range(GROUP)]
    q2 = jnp.concatenate([q[:, c] for c in heads], axis=0)
    do2 = jnp.concatenate([do[:, c] for c in heads], axis=0)
    lev = jnp.concatenate([level[0, g : g + 1, :] for g in range(GROUP)], axis=1)
    drows = []
    for c in heads:
        both = jnp.sum(do[:, c].astype(F32) * o[:, c].astype(F32), axis=-1, keepdims=True)
        drows.append(jnp.broadcast_to(both, (bq, HEAD_DIM)).T[0:1, :])
    drow = jnp.concatenate(drows, axis=1)

    def step(k, v, ok, dk, dv, rows):
        s = dot_t(k, q2)
        p = jnp.exp2(s - lev)
        if ok is not None:
            p = jnp.where(ok, p, 0.0)
        dp = dot_t(v, do2)
        ds = (p * (dp - drow)).astype(BF)
        dv[rows, :] += dot(p.astype(BF), do2)
        dk[rows, :] += dot(ds, q2)
        return t_dot(k, ds)

    def twice(row):
        return jnp.concatenate([row] * GROUP, axis=1)

    qrow = twice(qpos[...])
    dq = None
    for at in range(0, own_p, chunk):
        rows = slice(at, at + chunk)
        ok = kpos[rows, :] <= qrow
        part = step(k_own[rows, :], v_own[rows, :], ok, dk_own, dv_own, rows)
        dq = part if dq is None else dq + part
    dq_acc[...] = dq
    if oth // chunk <= 4:
        for at in range(0, oth, chunk):
            rows = slice(at, at + chunk)
            ok = kpos[own_p + at : own_p + at + chunk, :] <= qrow
            dq_acc[...] += step(k_oth[rows, :], v_oth[rows, :], ok, dk_oth, dv_oth, rows)
    else:

        @pl.loop(0, oth // chunk)
        def _(j):
            rows = pl.ds(pl.multiple_of(j * chunk, chunk), chunk)
            ok = kpos[pl.ds(pl.multiple_of(own_p + j * chunk, chunk), chunk), :] <= qrow
            dq_acc[...] += step(k_oth[rows, :], v_oth[rows, :], ok, dk_oth, dv_oth, rows)

    @pl.when(jnp.logical_not(is_prompt))
    def _():
        code, lowest = twice(cqc[0:1, :]), twice(cqc[1:2, :])
        rows = slice(own_p, k_own.shape[0])
        ok = (ckc[...] <= code) & (ckc[...] >= lowest)
        dq_acc[...] += step(k_own[rows, :], v_own[rows, :], ok, dk_own, dv_own, rows)

    scale = HEAD_DIM ** (-0.5)
    gain_sum = jnp.zeros((8, HEAD_DIM), F32)
    for g, c in enumerate(heads):
        grad = dq_acc[:, g * bq : (g + 1) * bq].T * scale
        raw, rows = head_norm_rot_back(
            qraw[:, c].astype(F32), gq[...], cos_q[...], sin_q[...], grad
        )
        dq_out[:, c] = raw.astype(BF)
        gain_sum += jnp.sum(rows.reshape(bq // 8, 8, HEAD_DIM), axis=0)
    dgq_out[...] += gain_sum

    @pl.when(i == pl.num_programs(0) - 1)
    def _():
        for total, raw_in, cos, sin, out in (
            (dk_own, kraw_own, cos_o, sin_o, dk_own_out),
            (dk_oth, kraw_oth, cos_t, sin_t, dk_oth_out),
        ):
            n = total.shape[0]
            part = 256

            def finish(rows, total=total, raw_in=raw_in, cos=cos, sin=sin, out=out):
                raw, gain_rows = head_norm_rot_back(
                    raw_in[rows, :].astype(F32),
                    gk[...],
                    cos[rows, :],
                    sin[rows, :],
                    total[rows, :] * (1.0 / LOG2E),
                )
                out[rows, :] = raw.astype(BF)
                dgk_out[...] += jnp.sum(gain_rows.reshape(part // 8, 8, HEAD_DIM), axis=0)

            @pl.loop(0, n // part)
            def _(j):
                finish(pl.ds(pl.multiple_of(j * part, part), part))

        dv_own_out[...] = dv_own[...].astype(BF)
        dv_oth_out[...] = dv_oth[...].astype(BF)


def attend_back(
    head, filled, waits, q, qraw, do, o, level, own, oth, tabs, gq, gk, pos, own_p, bq=256
):
    rows = q.shape[0]
    n_oth = oth[0].shape[0]
    keys = own_p + n_oth
    chunk = min(512, own_p)
    wide = pl.BlockSpec((bq, GROUP * HEAD_DIM), lambda i: (i, head))
    tab = pl.BlockSpec((bq, HEAD_DIM), lambda i: (i, 0))
    head_col = lambda n: pl.BlockSpec((n, HEAD_DIM), lambda i: (0, head))
    cont_block = lambda i: (0, jnp.maximum(i - own_p // bq, 0))
    one = whole((1, HEAD_DIM))
    full = lambda n: whole((n, HEAD_DIM))
    cos_own, sin_own, cos_oth, sin_oth = tabs
    ins = [
        q, qraw, do, o, level, cos_own, sin_own, gq, gk,
        own[0], own[1], own[2], cos_own, sin_own,
        oth[0], oth[1], oth[2], cos_oth, sin_oth,
        pos["q_row"], pos["k_col"], pos["cq_row"], pos["ck_col"],
    ]
    specs = [
        wide, wide, wide, wide,
        pl.BlockSpec((1, GROUP, bq), lambda i: (head, 0, i)),
        tab, tab, one, one,
        head_col(rows), head_col(rows), head_col(rows), full(rows), full(rows),
        head_col(n_oth), head_col(n_oth), head_col(n_oth), full(n_oth), full(n_oth),
        pl.BlockSpec((1, bq), lambda i: (0, i)),
        whole((keys, 1)),
        pl.BlockSpec((2, bq), cont_block),
        whole((rows - own_p, 1)),
    ]
    anywhere = pl.BlockSpec(memory_space=pl.ANY)
    aliases = {len(ins) + n: n for n in range(len(filled))}
    extra = list(filled) + list(waits)
    return pl.pallas_call(
        functools.partial(attend_back_kernel, own_p, n_oth, chunk),
        out_shape=[
            jax.ShapeDtypeStruct((rows, QW), BF),
            jax.ShapeDtypeStruct((rows, KW), BF),
            jax.ShapeDtypeStruct((rows, KW), BF),
            jax.ShapeDtypeStruct((n_oth, KW), BF),
            jax.ShapeDtypeStruct((n_oth, KW), BF),
            jax.ShapeDtypeStruct((8, HEAD_DIM), F32),
            jax.ShapeDtypeStruct((8, HEAD_DIM), F32),
        ],
        grid=(rows // bq,),
        in_specs=specs + [anywhere] * len(extra),
        out_specs=[
            wide, head_col(rows), head_col(rows), head_col(n_oth), head_col(n_oth),
            whole((8, HEAD_DIM)), whole((8, HEAD_DIM)),
        ],
        scratch_shapes=[
            pltpu.VMEM((rows, HEAD_DIM), F32),
            pltpu.VMEM((rows, HEAD_DIM), F32),
            pltpu.VMEM((n_oth, HEAD_DIM), F32),
            pltpu.VMEM((n_oth, HEAD_DIM), F32),
            pltpu.VMEM((HEAD_DIM, GROUP * bq), F32),
        ],
        input_output_aliases=aliases,
        compiler_params=params(),
        cost_estimate=SMALL,
    )(*ins, *extra)


def feed_kernel(x, part, got, dy, g2, wg, wu, wd, *rest):
    h1_out, b_out, hid_out, dg_out, du_out, y_out, db_out = rest[-7:]
    hv = x[...].astype(F32) + (part[...].astype(F32) + got[...].astype(F32))
    h1_out[...] = hv
    b = hv * lax.rsqrt(jnp.mean(hv * hv, axis=-1, keepdims=True) + EPS_NORM) * g2[...]
    b = b.astype(BF)
    b_out[...] = b
    dyv = dy[...]
    step = 512
    y = db = None
    for at in range(0, FW, step):
        cols = slice(at, at + step)
        gate = dot(b, wg[:, cols])
        up = dot(b, wu[:, cols])
        dhid = dot_t(dyv, wd[cols, :])
        sig = 1.0 / (1.0 + jnp.exp(-gate))
        act = gate * sig
        hid = (act * up).astype(BF)
        dgate = (dhid * up * (sig * (1.0 + gate * (1.0 - sig)))).astype(BF)
        dup = (dhid * act).astype(BF)
        hid_out[:, cols] = hid
        dg_out[:, cols] = dgate
        du_out[:, cols] = dup
        y_part = dot(hid, wd[cols, :])
        db_part = dot_t(dgate, wg[:, cols]) + dot_t(dup, wu[:, cols])
        y = y_part if y is None else y + y_part
        db = db_part if db is None else db + db_part
    y_out[...] = y.astype(BF)
    db_out[...] = db.astype(BF)


def feed(filled, base, total, x, part, got, dy, g2, wg, wu, wd):
    rows = part.shape[0]
    bm = 256
    base //= bm
    row = lambda width: pl.BlockSpec((bm, width), lambda i: (i, 0))
    later = lambda width: pl.BlockSpec((bm, width), lambda i: (base + i, 0))
    anywhere = pl.BlockSpec(memory_space=pl.ANY)
    return pl.pallas_call(
        feed_kernel,
        out_shape=[
            jax.ShapeDtypeStruct((total, D), F32),
            jax.ShapeDtypeStruct((total, D), BF),
            jax.ShapeDtypeStruct((total, FW), BF),
            jax.ShapeDtypeStruct((total, FW), BF),
            jax.ShapeDtypeStruct((total, FW), BF),
            jax.ShapeDtypeStruct((rows, D), BF),
            jax.ShapeDtypeStruct((rows, D), BF),
        ],
        grid=(rows // bm,),
        in_specs=[
            later(D), row(D), row(D), later(D), whole((1, D)), whole((D, FW)), whole((D, FW)), whole((FW, D)),
        ]
        + [anywhere] * len(filled),
        out_specs=[later(D), later(D), later(FW), later(FW), later(FW), row(D), row(D)],
        input_output_aliases={8 + n: n for n in range(len(filled))},
        compiler_params=params(),
        cost_estimate=SMALL,
    )(x, part, got, dy, g2, wg, wu, wd, *filled)


def back_kernel(h1, dy, mine, got, g2, wo, *rest):
    dh_out, da_out, do_out, dg_out = rest[-4:]
    hv = h1[...]
    db = mine[...].astype(F32) + got[...].astype(F32)
    r = lax.rsqrt(jnp.mean(hv * hv, axis=-1, keepdims=True) + EPS_NORM)
    xh = hv * r
    dg = db * g2[...]
    dh = dy[...].astype(F32) + r * (dg - xh * jnp.mean(dg * xh, axis=-1, keepdims=True))
    dh_out[...] = dh
    da = dh.astype(BF)
    da_out[...] = da
    do_out[...] = dot_t(da, wo[...]).astype(BF)
    gain = jnp.sum((db * xh).reshape(hv.shape[0] // 8, 8, D), axis=0)

    @pl.when(pl.program_id(0) == 0)
    def _():
        dg_out[...] = jnp.zeros_like(dg_out)

    dg_out[...] += gain


def back_norm(filled, base, h1, dy, mine, got, g2, wo):
    rows, total = mine.shape[0], h1.shape[0]
    bm = 256
    base //= bm
    row = lambda width: pl.BlockSpec((bm, width), lambda i: (i, 0))
    later = lambda width: pl.BlockSpec((bm, width), lambda i: (base + i, 0))
    anywhere = pl.BlockSpec(memory_space=pl.ANY)
    return pl.pallas_call(
        back_kernel,
        out_shape=[
            jax.ShapeDtypeStruct((total, D), F32),
            jax.ShapeDtypeStruct((total, D), BF),
            jax.ShapeDtypeStruct((total, QW), BF),
            jax.ShapeDtypeStruct((8, D), F32),
        ],
        grid=(rows // bm,),
        in_specs=[later(D), later(D), row(D), row(D), whole((1, D)), whole((QW, D))]
        + [anywhere] * len(filled),
        out_specs=[later(D), later(D), later(QW), whole((8, D))],
        input_output_aliases={6 + n: n for n in range(len(filled))},
        compiler_params=params(),
        cost_estimate=SMALL,
    )(h1, dy, mine, got, g2, wo, *filled)


def layout():
    q_width = HEADS * HEAD_DIM
    kv_width = KV_HEADS * HEAD_DIM
    return [
        (D,),
        (D, q_width),
        (D, kv_width),
        (D, kv_width),
        (HEAD_DIM,),
        (HEAD_DIM,),
        (q_width, D),
        (D,),
        (D, FF),
        (D, FF),
        (FF, D),
    ]


LANES = 128
SHARD = 491592
FLAT_AT = {"g1": 0, "wq": 8, "wk": 16392, "wv": 24584, "gqk": 32776, "wo": 32778,
           "g2": 49162, "wg": 49170, "wu": 73746, "wd": 98322}
PER_ROW = {"wq": 16, "wk": 8, "wv": 8, "wo": 8, "wg": 24, "wu": 24, "wd": 8}


def matrix_kernel(per, split, place, main, extra, out, wide):
    count = main.shape[0]
    wide[:count, :] = main[...].astype(F32)
    wide[count:, :] = extra[...].astype(F32)
    rows = out.shape[0]
    first = place[1]
    if split:
        first = first + place[0] * (out.shape[1] // LANES)
    for at in range(out.shape[1] // LANES):
        cols = slice(at * LANES, (at + 1) * LANES)
        out[:, cols] = wide[pl.ds(first + at, rows, stride=per), :].astype(BF)


def matrix(lanes, name, split, rows, step, core):
    per = PER_ROW[name]
    count = step * per
    at = FLAT_AT[name]
    base = at // count
    width = per * LANES // (CORES if split else 1)
    blocks = (rows if split else rows // CORES) // step
    place = jnp.stack([core, jnp.full_like(core, at - base * count)]).astype(jnp.int32)

    def block(i, place):
        return base + i + (0 if split else place[0] * blocks)

    return pl.pallas_call(
        functools.partial(matrix_kernel, per, split),
        out_shape=jax.ShapeDtypeStruct((blocks * step, width), BF),
        grid_spec=pltpu.PrefetchScalarGridSpec(
            num_scalar_prefetch=1,
            grid=(blocks,),
            in_specs=[
                pl.BlockSpec((count, LANES), lambda i, place: (block(i, place), 0)),
                pl.BlockSpec(
                    (32, LANES), lambda i, place: ((block(i, place) + 1) * (count // 32), 0)
                ),
            ],
            out_specs=pl.BlockSpec((step, width), lambda i, place: (i, 0)),
            scratch_shapes=[pltpu.VMEM((count + 32, LANES), F32)],
        ),
        compiler_params=params(),
        cost_estimate=SMALL,
    )(place, lanes, lanes)


def gain_vectors(flat_vec):
    take = lambda name, skip, size: lax.slice(
        flat_vec, (FLAT_AT[name] * LANES + skip,), (FLAT_AT[name] * LANES + skip + size,)
    )
    gains = take("g1", 0, D), take("g2", 0, D), take("gqk", 0, LANES), take("gqk", LANES, LANES)
    return [gain.astype(F32).reshape(1, -1) for gain in gains]


def plain_grads(
    pick, a, a_far, b, o, hid, dgate, dup, dy, da_out, dq, dk, dv, dg1, dgq, dgk, dg2
):
    a_all = jnp.concatenate([a, a_far])
    grads = [
        dg1,
        t_dot(a, dq),
        t_dot(a_all, jnp.concatenate(dk)),
        t_dot(a_all, jnp.concatenate(dv)),
        jnp.sum(dgq, axis=0),
        jnp.sum(dgk, axis=0),
        t_dot(o, da_out),
        0.5 * dg2,
        t_dot(b, dgate),
        t_dot(b, dup),
        t_dot(hid, dy),
    ]
    flat = []
    for number, (grad, shape) in enumerate(zip(grads, layout())):
        if len(shape) == 2:
            axis = 0 if number in (6, 10) else 1
            blank = jnp.zeros_like(grad)
            grad = jnp.concatenate([pick(grad, blank), pick(blank, grad)], axis=axis)
        flat.append(grad.reshape(-1).astype(F32))
    return lax.psum_scatter(
        jnp.concatenate(flat), ("dp", "seq"), scatter_dimension=0, tiled=True
    )


X_FIRST = ("wq", "wg", "wd")
FEED_PARTS = {
    (1, 0): [("wo", 0, 704)],
    (1, 1): [("wo", 704, 1664)],
    (1, 2): [("wo", 1664, 2048), ("wg", 0, 192)],
    (1, 3): [("wg", 192, 512)],
    (2, 0): [("wg", 512, 832)],
    (2, 1): [("wg", 832, 1024), ("wu", 0, 128)],
    (2, 2): [("wu", 128, 448)],
    (2, 3): [("wu", 448, 768)],
    (3, 0): [("wu", 768, 1024), ("wd", 0, 192)],
    (3, 1): [("wd", 192, 1152)],
    (3, 2): [("wd", 1152, 2112)],
    (3, 3): [("wd", 2112, 3072)],
}
HEAD_PARTS = {0: ("wq", 0, 512), 1: ("wq", 512, 1024), 2: ("wk", 0, 1024), 3: ("wv", 0, 1024)}
TAIL = 288


def plane_pairs(distance, wanted=lambda dp, seq: True):
    pairs = []
    for dp in range(4):
        for seq in range(8):
            to = dp ^ distance
            if wanted(to, seq):
                pairs.append((dp * 8 + seq, to * 8 + seq))
    return pairs


def swap_dp(block, distance):
    return lax.ppermute(block, "dp", [(i, i ^ distance) for i in range(4)])


def cut(block, index, axis=1):
    width = block.shape[axis] // 2
    return lax.dynamic_slice_in_dim(block, index * width, width, axis)


def plane_order(name):
    dp = lax.axis_index("dp")
    order = ((dp % 2, 1), (dp // 2, 2))
    return order if name in X_FIRST else order[::-1]


def plane_step(grad, name, step):
    mine, distance = plane_order(name)[step]
    return cut(grad, mine), swap_dp(cut(grad, 1 - mine), distance)


def kept(*stages):
    return [stage[0] for stage in stages]


def added(stage):
    return (stage[0].astype(F32) + stage[1].astype(F32)).astype(BF)


def line_start(parts):
    low = lax.axis_index("seq") // 2 % 2
    parts = parts.reshape((2, 2) + parts.shape[1:])
    keep = lax.dynamic_index_in_dim(parts, low, 1, keepdims=False)
    send = lax.dynamic_index_in_dim(parts, 1 - low, 1, keepdims=False)
    return keep, xor_seq(send, 2)


def line_next(stage):
    high = lax.axis_index("seq") // 4
    parts = added(stage)
    keep = lax.dynamic_index_in_dim(parts, high, 0, keepdims=False)
    send = lax.dynamic_index_in_dim(parts, 1 - high, 0, keepdims=False)
    return keep, xor_seq(send, 4)


def stack_rows(grad, low, high):
    return [grad[low:high, at : at + LANES] for at in range(0, grad.shape[1], LANES)]


def feed_line(sums):
    spare = jnp.zeros((256, LANES), BF)
    per_line = []
    for z in range(4):
        blocks = [spare] if z == 0 else []
        for d in (1, 2, 3):
            for name, low, high in FEED_PARTS[d, z]:
                blocks += stack_rows(sums[name], low, high)
        per_line.append(jnp.concatenate(blocks))
    return line_start(jnp.stack(per_line))


ROWS = 3872
PART = 176
BEFORE = TAIL * 8


def spread(who, other, core, dp, name, at, rows, into, to):
    per = PER_ROW[name] // 8
    for source, side in ((who, core), (other, 1 - core)):
        for place in range(4):
            chip = (place % 2) * 2 + place // 2 if name in X_FIRST else place
            for col in range(per):
                first = to + side * (4 * per) + place * per + col
                block = source[chip ^ dp, at + col * rows : at + (col + 1) * rows, :]
                into[pl.ds(first, rows, stride=8 * per), :] = block.astype(F32)


def feed_flat_kernel(info, who, other, out):
    core, spot = info[0], info[1]

    @pl.when((spot < 4) | (spot == 4))
    def _():
        out[...] = jnp.zeros_like(out)

    for (d, z), blocks in FEED_PARTS.items():

        @pl.when(spot == d * 4 + z)
        def _(d=d, z=z, blocks=blocks):
            at, to = (256, 2048) if (d, z) == (1, 0) else (0, 0)
            for name, low, high in blocks:
                rows = high - low
                spread(who, other, core, 0, name, at, rows, out, to)
                at += rows * PER_ROW[name] // 8
                to += rows * PER_ROW[name]


def main_row(d, z):
    if (d, z) == (1, 0):
        return FLAT_AT["gqk"]
    name, low, _ = HEAD_PARTS[z] if d == 0 else FEED_PARTS[d, z][0]
    return FLAT_AT[name] + low * PER_ROW[name]


STARTS = [
    (8 * d + 2 * z + c) * SHARD // LANES - (main_row(d, z) - BEFORE)
    for d in range(4)
    for z in range(4)
    for c in range(2)
]
WIDE = max(BEFORE + 8192, (max(STARTS) + ROWS + 16) // 8 * 8)


def adam(grad, master, moment1, moment2):
    moment1_new = BETA_ONE * moment1 + (1.0 - BETA_ONE) * grad
    moment2_new = BETA_TWO * moment2 + (1.0 - BETA_TWO) * grad * grad
    update = moment1_new / CORRECT_ONE / (jnp.sqrt(moment2_new / CORRECT_TWO) + ADAM_EPS)
    return moment1_new, master - LEARN_RATE * (update + DECAY_RATE * master)


def finish_kernel(
    info, who, other, flat, before, gains, master, moment1, moment2,
    grad_out, moment1_out, master_out, block_out, wide, work,
):
    core, spot, start, skip, ahead, rest = [info[i] for i in range(6)]

    def put_before(name, dp):
        spread(who, other, core, dp, name, 1024, TAIL * 8 // PER_ROW[name], wide, 0)

    @pl.when(spot == 0)
    def _():
        wide[BEFORE - 8 : BEFORE, :] = gains[0:8, :]

    @pl.when((spot == 1) | (spot == 2))
    def _():
        put_before("wq", 0)

    @pl.when(spot == 3)
    def _():
        put_before("wk", 0)

    @pl.when(spot == 4)
    def _():
        put_before("wv", 1)
        wide[BEFORE : BEFORE + 2, :] = gains[8:10, :]
        wide[BEFORE + 2 : BEFORE + 2 + 5632, :] = flat[2048:, :]

    @pl.when(spot < 2)
    def _():
        spread(who, other, core, 0, "wq", 0, 512, wide, BEFORE)

    @pl.when((spot == 2) | (spot == 3))
    def _():
        spread(who, other, core, 0, "wk", 0, 1024, wide, BEFORE)

    @pl.when(spot > 4)
    def _():
        wide[BEFORE - 16 : BEFORE, :] = before[...]

    @pl.when(spot == 6)
    def _():
        wide[BEFORE : BEFORE + 3072, :] = flat[:3072, :]
        wide[BEFORE + 3072 : BEFORE + 3080, :] = gains[10:18, :]
        wide[BEFORE + 3080 : BEFORE + 7688, :] = flat[3072:, :]

    @pl.when((spot == 5) | (spot > 6))
    def _():
        wide[BEFORE : BEFORE + 7680, :] = flat[...]

    col = lax.broadcasted_iota(jnp.int32, (PART, LANES), 1)
    row = lax.broadcasted_iota(jnp.int32, (PART, LANES), 0)
    work[0:8, :] = jnp.zeros((8, LANES), F32)
    work[ROWS + 8 :, :] = jnp.zeros((8, LANES), F32)
    turn = lax.rem(LANES - skip, LANES)

    @pl.loop(0, ROWS // PART)
    def _(j):
        at = pl.multiple_of(j * PART, 8)
        here = pl.ds(at, PART)
        now = pltpu.roll(wide[pl.ds(start + at, PART), :], turn, 1)
        after_it = pltpu.roll(wide[pl.ds(start + at + 1, PART), :], turn, 1)
        grad = jnp.where(col < LANES - skip, now, after_it)
        moment1_new, master_new = adam(grad, master[here, :], moment1[here, :], moment2[here, :])
        grad_out[here, :] = grad
        moment1_out[here, :] = moment1_new
        master_out[here, :] = master_new
        inside = (at + row) * LANES + col < SHARD
        work[pl.ds(at + 8, PART), :] = jnp.where(inside, master_new, 0.0)

    @pl.loop(0, ROWS // PART)
    def _(j):
        at = pl.multiple_of(j * PART, 16)
        now = pltpu.roll(work[pl.ds(7 - ahead + at, PART), :], rest, 1)
        after_it = pltpu.roll(work[pl.ds(8 - ahead + at, PART), :], rest, 1)
        block_out[pl.ds(at, PART), :] = jnp.where(col < rest, now, after_it).astype(BF)


def local(kernel, shapes, scratch, info, *arrays):
    vmem = pl.BlockSpec(memory_space=pltpu.VMEM)
    return pl.pallas_call(
        kernel,
        out_shape=shapes,
        in_specs=[pl.BlockSpec(memory_space=pltpu.SMEM)] + [vmem] * len(arrays),
        out_specs=jax.tree.map(lambda _: vmem, shapes),
        scratch_shapes=scratch,
        compiler_params=params(),
        cost_estimate=SMALL,
    )(jnp.stack(info).astype(jnp.int32), *arrays)


def fast_grads(core, feed_stage, head_q, head_kv, gains, states, da, to_home):
    dp = lax.axis_index("dp")
    rank = lax.axis_index("seq")
    line = rank // 2
    spot = dp * 4 + line
    gains = jnp.concatenate(gains).reshape(1, -1, LANES)
    gains = jnp.broadcast_to(gains, (32,) + gains.shape[1:])
    gains = lax.all_to_all(gains, ("dp", "seq"), 0, 0, tiled=True)
    feed_part = added(feed_stage).reshape(3, 960, LANES)
    feed_part = after(feed_part, kept(head_q, head_kv))

    feed_got = jnp.concatenate([feed_part[:1], feed_part])
    feed_got = lax.all_to_all(feed_got, "dp", 0, 0, tiled=True)
    head_q, head_kv = added(head_q), added(head_kv)
    head_stage = line_start(
        jnp.stack(
            [
                jnp.concatenate(stack_rows(head_q, 0, 512)),
                jnp.concatenate(stack_rows(head_q, 512, 1024)),
                head_kv[:1024],
                head_kv[1024:],
            ]
        )
    )
    feed_flat = local(
        feed_flat_kernel,
        jax.ShapeDtypeStruct((7680, LANES), F32),
        [],
        (core, spot),
        feed_got,
        xor_seq(feed_got, 1),
    )
    chain = [(8 * d + s, 8 * d + s + 2) for d in range(4) for s in range(8) if 8 * d + s < 30]
    before = lax.ppermute(feed_flat[-16:], ("dp", "seq"), chain)
    head_stage, gains, before = after((head_stage, gains, before))
    head_part = added(line_next(head_stage))
    tail = jnp.where(
        line < 2,
        jnp.concatenate([head_part[512 - TAIL // 2 : 512], head_part[1024 - TAIL // 2 :]]),
        head_part[1024 - TAIL :],
    )
    ring = [(8 * d + s, 8 * d + (s + 2) % 8) for d in range(4) for s in range(8)]
    tail = lax.ppermute(tail, ("dp", "seq"), ring)
    tail, da = after((tail, da))
    dx_rows = to_home(da)
    head_all = after(jnp.concatenate([head_part, tail]), dx_rows[0])
    head_got = [head_all]
    for distance in (1, 2, 3):
        pairs = plane_pairs(distance, lambda d, s: d == 0 or (d == 1 and s < 2))
        head_got.append(lax.ppermute(head_all, ("dp", "seq"), pairs))
    gains = jnp.sum(gains, axis=0)
    head_got = jnp.stack(head_got)
    head_far = xor_seq(head_got, 1)

    index = spot * 2 + core
    start = jnp.asarray(STARTS, jnp.int32)[index]
    info = (core, spot, start, index * (SHARD % LANES) % LANES, rank * 72 // LANES, rank * 72 % LANES)
    rows = jax.ShapeDtypeStruct((ROWS, LANES), F32)
    results = local(
        finish_kernel,
        [rows, rows, rows, jax.ShapeDtypeStruct((ROWS, LANES), BF)],
        [pltpu.VMEM((WIDE, LANES), F32), pltpu.VMEM((ROWS + 16, LANES), F32)],
        info, head_got, head_far, feed_flat, before, gains, *states,
    )
    results, dx_rows = after((results, dx_rows))
    return *results, dx_rows


def gather_weights(block):
    blocks = lax.all_gather(block, "seq", axis=0)
    body, ends = blocks[:, :3840], blocks[:, 3840:3848]
    heads = body[1:, :8] + ends[:-1]
    heads = jnp.concatenate([body[:1, :8], heads])
    rows = jnp.concatenate([heads, body[:, 8:]], axis=1).reshape(-1, LANES)
    rows = jnp.concatenate([rows, ends[-1]])
    return rows.reshape(-1)[: 8 * SHARD]


def norm_back(x, gain, grad):
    r = lax.rsqrt(jnp.mean(x * x, axis=-1, keepdims=True) + EPS_NORM)
    xh = x * r
    dg = grad * gain
    return r * (dg - xh * jnp.mean(dg * xh, axis=-1, keepdims=True))


def into_kernel(count, *refs):
    grads, weights = refs[:count], refs[count : 2 * count]
    x, out, gain_out = refs[2 * count :]
    total = None
    for grad, weight in zip(grads, weights):
        part = dot_t(grad[...], weight[...])
        total = part if total is None else total + part
    out[...] = total.astype(BF)
    xv = x[...].astype(F32)
    xh = xv * lax.rsqrt(jnp.mean(xv * xv, axis=-1, keepdims=True) + EPS_NORM)

    @pl.when(pl.program_id(0) == 0)
    def _():
        gain_out[...] = jnp.zeros_like(gain_out)

    gain_out[...] += jnp.sum((total * xh).reshape(xv.shape[0] // 8, 8, D), axis=0)


def into_input(grads, weights, x):
    rows = x.shape[0]
    bm = 256
    row = lambda width: pl.BlockSpec((bm, width), lambda i: (i, 0))
    return pl.pallas_call(
        functools.partial(into_kernel, len(grads)),
        out_shape=[jax.ShapeDtypeStruct((rows, D), BF), jax.ShapeDtypeStruct((8, D), F32)],
        grid=(rows // bm,),
        in_specs=[row(grad.shape[1]) for grad in grads]
        + [whole(weight.shape) for weight in weights]
        + [row(D)],
        out_specs=[row(D), whole((8, D))],
        compiler_params=params(),
        cost_estimate=SMALL,
    )(*grads, *weights, x)


def tables(positions):
    half_dim = HEAD_DIM // 2
    frequency = ROPE_BASE ** (-jnp.arange(half_dim, dtype=F32) * 2.0 / HEAD_DIM)
    angles = positions.astype(F32)[:, None] * frequency[None, :]
    cosine, sine = jnp.cos(angles), jnp.sin(angles)
    return jnp.concatenate([cosine, cosine], 1), jnp.concatenate([-sine, sine], 1)


def shards(x_prompt, x_cont, dy_prompt, dy_cont, prompt_pos, weights, master, moment1, moment2):
    count = lax.axis_size("seq")
    rank = lax.axis_index("seq")
    half = count // 2
    side = rank // half
    core = rank % CORES
    chips = half // CORES
    p = x_prompt.shape[1]
    c = x_cont.shape[1]
    prompt_len = p * count
    own_p = 4 * p
    first = core == 0

    def pick(lo, hi):
        return jnp.where(first, lo, hi)

    def share(mine, got):
        return pick(mine, got), pick(got, mine)

    def far_rows(block):
        rows = block[None]
        mask = 2
        while mask < half:
            rows = jnp.concatenate([rows, xor_seq(rows, mask)])
            mask *= 2
        return rows[1:]

    def sides(prompt, cont):
        rows = jnp.concatenate([prompt, cont], axis=1)
        own = lax.dynamic_index_in_dim(rows, side, 0, keepdims=False)
        other = lax.dynamic_index_in_dim(rows, 1 - side, 0, keepdims=False)
        return own, other

    def join(own, recv, own_got, recv_got):
        lo, hi = share(own, own_got)
        lo2, hi2 = share(recv, recv_got)
        rows_p = [lo[:p], lo2[:p], hi[:p], hi2[:p]]
        rows_c = [lo[p:], lo2[p:], hi[p:], hi2[p:]]
        return jnp.concatenate(rows_p + rows_c, axis=0)

    x_own, x_other = sides(x_prompt, x_cont)
    x_recv = xor_seq(x_other, half)
    far_one = far_rows(x_own[:p])
    x_own_got = xor_seq(x_own, 1)

    lanes = weights.reshape(-1, LANES)
    g1, g2, gq, gk = gain_vectors(weights)
    w_q = matrix(lanes, "wq", True, D, 128, core)
    w_k = matrix(lanes, "wk", True, D, 256, core)
    w_v = matrix(lanes, "wv", True, D, 256, core)
    x_recv = after(x_recv, w_q, w_k, w_v)
    far_two = far_rows(x_recv[:p])
    x_recv_got = xor_seq(x_recv, 1)
    far_one = after(far_one, x_recv)
    far_one_got = xor_seq(far_one, 1)
    lanes = after(lanes, x_recv)
    w_g = matrix(lanes, "wg", True, D, 128, core)
    w_u = matrix(lanes, "wu", True, D, 128, core)
    x_recv_got = after(x_recv_got, w_g, w_u)
    x = join(x_own, x_recv, x_own_got, x_recv_got)

    chip_ids = (rank - core) ^ (CORES * jnp.arange(chips)[:, None, None])
    ids = (chip_ids + jnp.arange(CORES)[None, :, None]) ^ (half * jnp.arange(2)[None, None, :])
    own_group = lax.dynamic_index_in_dim(prompt_pos, side, 0, keepdims=False)
    key_pos = jnp.take(own_group.reshape(count, p), ids.reshape(-1), axis=0).reshape(-1)
    quarter = c // 2
    steps = jnp.arange(quarter, dtype=jnp.int32)
    own_half = [
        prompt_len + jnp.concatenate([k * quarter + steps, (3 - k) * quarter + steps])
        for k in range(CORES)
    ]
    cont_pos = jnp.concatenate([own_half[0], own_half[0], own_half[1], own_half[1]])
    seg = jnp.tile(jnp.repeat(jnp.arange(2, dtype=jnp.int32), c), CORES)
    big = 2 * prompt_len + 4 * c
    cont_code = seg * big + cont_pos
    query_pos = jnp.concatenate([key_pos[:own_p], cont_pos])
    cont_q = jnp.stack([cont_code, seg * big])
    pos = {
        "q_col": query_pos[:, None], "q_row": query_pos[None, :],
        "k_col": key_pos[:, None], "k_row": key_pos[None, :],
        "cq_col": cont_q.T, "cq_row": cont_q,
        "ck_col": cont_code[:, None], "ck_row": cont_code[None, :],
    }
    cos_own, sin_own = tables(query_pos)
    cos_far, sin_far = tables(key_pos[own_p:])

    a, q, qraw, k_own, kraw_own, v_own = project(x, g1, cos_own, sin_own, w_q, w_k, w_v, gq, gk, True)
    far_two = after(far_two, a)
    far_two_got = xor_seq(far_two, 1)
    lanes = after(lanes, a)
    w_d = matrix(lanes, "wd", False, FF, 384, core)
    w_o = matrix(lanes, "wo", False, HEADS * HEAD_DIM, 256, core)
    far_two_got = after(far_two_got, w_d, w_o)
    dy_own, dy_other = after(sides(dy_prompt, dy_cont), far_two)
    dy_recv = xor_seq(dy_other, half)
    dy_own_got = xor_seq(dy_own, 1)
    lo, hi = share(far_one, far_one_got)
    lo2, hi2 = share(far_two, far_two_got)
    x_far = jnp.stack([lo, lo2, hi, hi2], axis=1).reshape(-1, D)
    a_far, k_far, kraw_far, v_far = project(x_far, g1, cos_far, sin_far, w_q, w_k, w_v, gq, gk, False)
    rows = x.shape[0]
    o_p, level_p = attend(q, k_own, v_own, k_far, v_far, pos, own_p, False)
    part_p = dot(o_p, w_o).astype(BF)
    part_p_got = xor_seq(part_p, 1)
    q, part_p, dy_recv = after((q, part_p, dy_recv))
    dy_recv_got = xor_seq(dy_recv, 1)
    o_c, level_c = attend(q, k_own, v_own, k_far, v_far, pos, own_p, True)
    o_c, dy_recv_got = after((o_c, dy_recv_got))
    part_c = dot(o_c, w_o).astype(BF)
    part_c_got = xor_seq(part_c, 1)
    part_p_got = after(part_p_got, part_c)
    dy = join(dy_own, dy_recv, dy_own_got, dy_recv_got)
    *filled, y_p, db_p = feed((), 0, rows, x, part_p, part_p_got, dy, g2, w_g, w_u, w_d)
    db_p_got = xor_seq(db_p, 1)
    o = jnp.concatenate([o_p, o_c])
    o_got = xor_seq(o, 1)
    part_c_got, o_got = after((part_c_got, o_got), db_p)
    *filled, y_c, db_c = feed(filled, own_p, rows, x, part_c, part_c_got, dy, g2, w_g, w_u, w_d)
    h1, b, hid, dgate, dup = filled
    db_c_got = xor_seq(db_c, 1)
    hid_got = xor_seq(hid, 1)
    level = jnp.concatenate([level_p, level_c], axis=2)
    y_part = jnp.concatenate([y_p, y_c])
    fast = count == 8 and lax.axis_size("dp") == 4
    def core_rows(rows, which):
        return jnp.concatenate(
            [
                lax.dynamic_slice_in_dim(rows, which * 2 * p, 2 * p),
                lax.dynamic_slice_in_dim(rows, own_p + which * 2 * c, 2 * c),
            ]
        )

    y_got = xor_seq(core_rows(y_part, 1 - core), 1)
    if fast:
        grad_g, grad_u = t_dot(b, dgate).astype(BF), t_dot(b, dup).astype(BF)
        grad_g, db_p_got, db_c_got = after((grad_g, db_p_got, db_c_got))
        flow = {"wg": plane_step(grad_g, "wg", 0)}
        flow["wu"] = plane_step(after(grad_u, kept(flow["wg"])), "wu", 0)
        dy_cols = cut(dy, core)
        grad_d = t_dot(hid, dy_cols).astype(BF)
        hid_got, y_got = after((hid_got, y_got), kept(flow["wg"], flow["wu"]))
        grad_d = share(grad_d, t_dot(hid_got, dy_cols).astype(BF))
        flow["wd"] = plane_step(jnp.concatenate(grad_d), "wd", 0)
        db_p_got, db_c_got = after((db_p_got, db_c_got), kept(flow["wd"]))
    y_core = core_rows(h1, core) + core_rows(y_part, core).astype(F32) + y_got.astype(F32)
    *filled, dg2_p = back_norm((), 0, h1, dy, db_p, db_p_got, g2, w_o)
    *filled, dg2_c = back_norm(filled, own_p, h1, dy, db_c, db_c_got, g2, w_o)
    dh1, da_out, d_o = filled
    dg2 = jnp.sum(dg2_p + dg2_c, axis=0)

    filled, waits = (), [y_core]
    back = []
    if fast:
        states = [
            jnp.concatenate([state, jnp.zeros((ROWS * LANES - SHARD,), F32)]).reshape(ROWS, LANES)
            for state in (master, moment1, moment2)
        ]
        waits += states
        cols = cut(da_out, core)
        grad_o = share(t_dot(o, cols).astype(BF), t_dot(o_got, cols).astype(BF))
        flow["wo"] = plane_step(jnp.concatenate(grad_o), "wo", 0)
        flow["wg"], flow["wu"] = after((flow["wg"], flow["wu"]), flow["wo"][0])
        for name in ("wg", "wu"):
            flow[name] = plane_step(added(flow[name]), name, 1)
        waits += kept(*flow.values())
    for head in range(KV_HEADS_C):
        *filled, dgq, dgk = attend_back(
            head, filled, waits, q, qraw, d_o, o, level,
            (k_own, v_own, kraw_own), (k_far, v_far, kraw_far),
            (cos_own, sin_own, cos_far, sin_far), gq, gk, pos, own_p,
        )
        waits = []
        back.append((dgq, dgk))
        if head == 2:
            y_rows = after(y_rows, dgq)
            waits = [y_rows[1]]
        if fast and head == 1:
            flow = after(flow, dgq)
            flow["wg"], flow["wu"] = added(flow["wg"]), added(flow["wu"])
            for name in ("wd", "wo"):
                flow[name] = plane_step(added(flow[name]), name, 1)
            waits += [flow["wg"], flow["wu"]] + kept(flow["wd"], flow["wo"])
        if head == 1:
            y_rows = home_start(after(y_core, dgq, waits), half, p, c)
            waits.append(y_rows[0])
        if fast and head == 2:
            flow = after(flow, dgq)
            flow["wd"], flow["wo"] = added(flow["wd"]), added(flow["wo"])
            feed_stage = feed_line(flow)
            waits += kept(feed_stage)
    dq, dk_own, dv_own, dk_far, dv_far = filled
    dgq, dgk = [sum(parts) for parts in zip(*back)]
    y_prompt, y_cont = home_end(y_rows, side, p)

    if fast:
        grad_q = t_dot(a, dq).astype(BF)
        grad_q, feed_stage = after((grad_q, feed_stage))
        head_q = plane_step(grad_q, "wq", 0)
        a_all = after(jnp.concatenate([a, a_far]), kept(head_q))
        pair = [(dk_own, dk_far), (dv_own, dv_far)]
        pair = [t_dot(a_all, jnp.concatenate(part)).astype(BF) for part in pair]
        head_kv = plane_step(jnp.concatenate(pair), "wk", 0)
        feed_stage = line_next(feed_stage)
        dk_own, dk_far = after((dk_own, dk_far), kept(feed_stage, head_q, head_kv))

    da_far, gain_far = into_input((dk_far, dv_far), (w_k, w_v), x_far)
    da_far = da_far.reshape(chips - 1, CORES, 2 * p, D)
    da_own, gain_own = into_input((dq, dk_own, dv_own), (w_q, w_k, w_v), x)
    dg1 = jnp.sum(gain_far + gain_own, axis=0)
    far_keep = lax.dynamic_index_in_dim(da_far, core, 1, keepdims=False)
    far_send = lax.dynamic_index_in_dim(da_far, 1 - core, 1, keepdims=False)
    sent = jnp.concatenate([core_rows(da_own, 1 - core), far_send.reshape(-1, D)])
    got = xor_seq(sent, 1)
    if fast:
        head_q, head_kv, feed_stage = after((head_q, head_kv, feed_stage))
        head_q = plane_step(added(head_q), "wq", 1)
        head_kv = plane_step(added(head_kv), "wk", 1)
        got = after(got, kept(head_q, head_kv))
    mine = core_rows(da_own, core).astype(F32) + got[: rows // 2].astype(F32)
    far_sum = far_keep.astype(F32) + got[rows // 2 :].reshape(far_keep.shape).astype(F32)
    blocks = jnp.concatenate([mine[None, : 2 * p], far_sum])
    mask = half // 2
    while mask > 1:
        near, away = blocks[: mask // 2], blocks[mask // 2 :].astype(BF)
        if fast:
            head_q, head_kv = after((head_q, head_kv), away)
        blocks = near + xor_seq(away, mask).astype(F32)
        mask //= 2
    da = jnp.concatenate([blocks[0], mine[2 * p :]])

    def to_dx(da):
        return core_rows(dh1, core) + norm_back(core_rows(x, core).astype(F32), g1, da)

    if fast:
        gains = [dg1, jnp.sum(dgq, 0), jnp.sum(dgk, 0), 0.5 * dg2]
        *results, block, dx_rows = fast_grads(
            core, feed_stage, head_q, head_kv, gains, states, da, lambda da: home_start(to_dx(da), half, p, c)
        )
        weights_new = gather_weights(block)
        grad_shard, moment1_new, master_new = [one.reshape(-1)[:SHARD] for one in results]
    else:
        grad_shard = plain_grads(
            pick, a, a_far, b, o, hid, dgate, dup, dy, da_out, dq,
            (dk_own, dk_far), (dv_own, dv_far), dg1, dgq, dgk, dg2,
        )
        dx_rows = home_start(to_dx(da), half, p, c)
        moment1_new, master_new = adam(grad_shard, master, moment1, moment2)
        weights_new = lax.all_gather(master_new.astype(BF), "seq", axis=0, tiled=True)
    dx_prompt, dx_cont = home_end(dx_rows, side, p)
    return (y_prompt, y_cont, dx_prompt, dx_cont, grad_shard, master_new, moment1_new, weights_new)


def solution(mesh):
    placed = (
        P("dp", "seq", None),
        P("dp", "seq", None),
        P("dp", "seq", None),
        P("dp", "seq", None),
        P("dp", None),
        P(),
        P(("dp", "seq")),
        P(("dp", "seq")),
        P(("dp", "seq")),
    )
    return jax.shard_map(
        shards,
        mesh=mesh,
        in_specs=placed,
        out_specs=(
            P("dp", "seq", None),
            P("dp", "seq", None),
            P("dp", "seq", None),
            P("dp", "seq", None),
            P(("dp", "seq")),
            P(("dp", "seq")),
            P(("dp", "seq")),
            P("dp"),
        ),
        check_vma=False,
    )
```
